256 devices in a mesh: pos: 32 (over y, z_hi, core), tile: 8 (over x, z_lo).
Axes of the slice: x: 4, y: 4, z: 8 (z_hi: 4, z_lo: 2; z = z_hi * 2 + z_lo), core: 2. Of those that a mesh axis runs over, the one named last changes fastest.
Arguments:
- object_field: float32 [2, 2, 8192, 2048], P(None, None, 'pos', 'tile'), may hold values from -4 to 4
- probe_modes: float32 [4, 2, 256, 256], replicated, may hold values from -5 to 5
- amplitudes: float32 [256, 256, 256], P(('pos', 'tile')), may hold values from 0 to 3
- corners: int32 [256, 2], P(('pos', 'tile')), may hold values from 0 to 255
Outputs:
- object_grad: float32 [2, 2, 8192, 2048], P(None, None, 'pos', 'tile')
- probe_grad: float32 [4, 2, 256, 256], replicated
The draws below stay inside these ranges and needn't reach their ends.
Inputs may be any that keep to these rules, and one draw needn't show every extreme that they name: `corners`: each position's window starts inside the block of the device that holds the position.
All inputs are finite; a program needn't handle non-finite values.
Results may differ from the reference program's by a relative error of at most 0.0003.
Values sent between devices are 32-bit elements; how exact they have to be, the bound alone decides.
No kernel may reach another device: no remote copies, remote signals or barrier semaphores. Data moves between devices by JAX's collectives and lax.ppermute only.
A program may use at most 128 MiB of HBM per device.

```python
import math
import jax
import jax.numpy as jnp
from jax import lax

PS = 256
MODES = 4
SLICES = 2
BLOCK = 256
POS_DEV = 1
HEIGHT = 8192
WIDTH = 2048
POSITIONS = 256


def set_ends(result, stream_key, low, high):
    index_at = [jax.random.randint(jax.random.fold_in(stream_key, axis), (), 0, length) for axis, length in enumerate(result.shape)]
    main_axis = result.shape.index(max(result.shape))
    neighbour = index_at[:main_axis] + [(index_at[main_axis] + 1) % result.shape[main_axis]] + index_at[main_axis + 1:]
    return result.at[tuple(index_at)].set(low).at[tuple(neighbour)].set(high)


def shard_levels(rng, shape, shards, low, largest):
    def one(dim, blocks):
        heights = jax.random.uniform(jax.random.fold_in(jax.random.fold_in(rng, 6), dim), (blocks,), jnp.float32, low / len(shards), largest / len(shards))
        return jnp.repeat(jnp.exp(heights), shape[dim] // blocks).reshape((-1,) + (1,) * (len(shape) - dim - 1))

    gain = one(*shards[0])
    for cut in shards[1:]:
        gain = gain * one(*cut)
    return gain


def scatter_about(own_key, extent, deviation, most, cuts=(), kind=jnp.bfloat16):
    array = deviation * jax.random.normal(own_key, extent, jnp.float32)
    if cuts:
        array = array * shard_levels(own_key, extent, cuts, -0.22, 0.18)
    return jnp.clip(array, -most, most).astype(kind)


def setup_inputs(seed: int = 0) -> dict:
    arg_keys = jax.random.split(jax.random.key(seed), 5)
    object_field = scatter_about(arg_keys[0], (SLICES, 2, HEIGHT, WIDTH), 0.7, 4.0, ((2, 32), (3, 8)), jnp.float32)
    probe_modes = scatter_about(arg_keys[1], (MODES, 2, PS, PS), 1.0, 5.0, (), jnp.float32)
    amplitudes = jnp.clip(3.0 * jax.random.uniform(arg_keys[2], (POSITIONS, PS, PS), jnp.float32) ** shard_levels(arg_keys[2], (POSITIONS, PS, PS), ((0, 256),), -0.2, 0.2), 0.0, 3.0)
    corners = set_ends(jax.random.randint(arg_keys[3], (POSITIONS, 2), 0, BLOCK), jax.random.fold_in(arg_keys[3], 1), 0, BLOCK - 1).astype(jnp.int32)
    return dict(object_field=object_field, probe_modes=probe_modes, amplitudes=amplitudes, corners=corners)


def tables(length):
    counter = jnp.arange(length, dtype=jnp.int32)
    product = counter[:, None] * counter[None, :] % length
    angles = product.astype(jnp.float32) * (-2.0 * math.pi / length)
    normal = 1.0 / math.sqrt(length)
    frequency = jnp.where(counter < length // 2, counter, counter - length)
    squared = frequency * frequency
    phases = (squared[:, None] + squared[None, :]).astype(jnp.float32) * (-math.pi / (2.0 * length))
    fourier = (jnp.cos(angles) * normal, jnp.sin(angles) * normal)
    fresnel = (jnp.cos(phases), jnp.sin(phases))
    return (fourier, fresnel)

def matmul_high(left_operand, right_operand):
    return jnp.matmul(left_operand, right_operand, precision=lax.Precision.HIGHEST)

def product_left(matrix, operand):
    return (matmul_high(matrix[0], operand[0]) - matmul_high(matrix[1], operand[1]), matmul_high(matrix[0], operand[1]) + matmul_high(matrix[1], operand[0]))

def product_right(operand, matrix):
    return (matmul_high(operand[0], matrix[0]) - matmul_high(operand[1], matrix[1]), matmul_high(operand[0], matrix[1]) + matmul_high(operand[1], matrix[0]))

def multiply(first, second):
    return (first[0] * second[0] - first[1] * second[1], first[0] * second[1] + first[1] * second[0])

def conjugate(value):
    return (value[0], -value[1])

def transform(operand, matrix):
    return product_right(product_left(matrix, operand), matrix)

def position_terms(window, probe_modes, amplitude, fourier, fresnel):
    layers = [(window[layer_index, 0], window[layer_index, 1]) for layer_index in range(window.shape[0])]
    inverse = conjugate(fourier)
    incoming = [(probe_modes[:, 0], probe_modes[:, 1])]
    current = multiply(incoming[0], layers[0])
    for layer_index in range(1, len(layers)):
        propagated = transform(multiply(fresnel, transform(current, fourier)), inverse)
        incoming.append(propagated)
        current = multiply(propagated, layers[layer_index])
    farfield = transform(current, fourier)
    intensity = lax.optimization_barrier(jnp.sum(farfield[0] * farfield[0] + farfield[1] * farfield[1], axis=0))
    factor = 1.0 - amplitude / jnp.sqrt(intensity + 1.0)
    backward = transform((factor * farfield[0], factor * farfield[1]), inverse)
    gradients = []
    for layer_index in reversed(range(len(layers))):
        partial_term = multiply(conjugate(incoming[layer_index]), backward)
        gradients.append(jnp.stack([lax.optimization_barrier(jnp.sum(partial_term[0], axis=0)), lax.optimization_barrier(jnp.sum(partial_term[1], axis=0))]))
        backward = multiply(conjugate(layers[layer_index]), backward)
        if layer_index > 0:
            backward = transform(multiply(conjugate(fresnel), transform(backward, fourier)), inverse)
    window_grad = jnp.stack(gradients[::-1])
    probe_term = jnp.stack([backward[0], backward[1]], axis=1)
    return (window_grad, probe_term)

def reference(object_field, probe_modes, amplitudes, corners):
    length = probe_modes.shape[-1]
    fourier, fresnel = tables(length)
    padded = jnp.pad(object_field, ((0, 0), (0, 0), (0, length), (0, length)))
    across = WIDTH // BLOCK
    owners = jnp.arange(POSITIONS, dtype=jnp.int32) // POS_DEV
    row_start = (owners // across * BLOCK + corners[:, 0]).astype(jnp.int32)
    col_start = (owners % across * BLOCK + corners[:, 1]).astype(jnp.int32)
    zero_index = jnp.zeros((), jnp.int32)

    def visit(carried, element):
        grad_field, probe_sum = carried
        amplitude, row_at, col_at = element
        starts = (zero_index, zero_index, row_at.astype(jnp.int32), col_at.astype(jnp.int32))
        window = lax.dynamic_slice(padded, starts, (SLICES, 2, length, length))
        window_grad, probe_term = position_terms(window, probe_modes, amplitude, fourier, fresnel)
        placed = lax.dynamic_slice(grad_field, starts, (SLICES, 2, length, length)) + window_grad
        return ((lax.dynamic_update_slice(grad_field, placed, starts), probe_sum + probe_term), None)
    initial = (jnp.zeros(padded.shape, jnp.float32), jnp.zeros(probe_modes.shape, jnp.float32))
    (grad_field, probe_grad), unused = lax.scan(visit, initial, (amplitudes, row_start, col_start))
    return (grad_field[:, :, :HEIGHT, :WIDTH], probe_grad)
```

```python
import math

import jax
import jax.numpy as jnp
import numpy as np
from jax import lax
from jax.experimental import pallas as pl
from jax.experimental.pallas import tpu as pltpu
from jax.sharding import PartitionSpec as P

N = 256
H = 128
F32 = jnp.float32
BF16 = jnp.bfloat16


def split_np(matrix):
    high = matrix.astype(np.float32).astype(jnp.bfloat16)
    low = (matrix - high.astype(np.float64)).astype(np.float32).astype(jnp.bfloat16)
    return high, low


def constants():
    count = np.arange(N)
    fourier = np.exp(-2j * np.pi * (np.outer(count, count) % N) / N) / math.sqrt(N)
    freq = np.where(count < H, count, count - N).astype(np.float64)
    fresnel = np.exp(-1j * np.pi * freq * freq / (2.0 * N))
    prop = (np.conj(fourier) * fresnel[None, :]) @ fourier
    straight, turned = prop[:H, :H], prop[:H, ::-1][:, :H]
    mats = []
    for part in ((straight + turned) / 2, (straight - turned) / 2):
        for side in (part, np.conj(part)):
            real, imag = side.real, side.imag
            right = np.block([[real, imag], [-imag, real]])
            high, low = split_np(right)
            mats.append(np.concatenate([high, high, low], axis=0))
            left = np.block([[real, -imag], [imag, real]])
            high, low = split_np(left)
            mats.append(np.concatenate([high, high, low], axis=1))
    half = np.arange(H) - 127.5
    angle = 2 * np.pi * np.outer(half, half) / N
    zero = np.zeros((H, H))
    both = np.block([[np.cos(angle) / 16, zero], [zero, np.sin(angle) / 16]])
    high, low = split_np(both)
    right_b = np.concatenate([high, high, low], axis=0)
    left_b = np.concatenate([high, high, low], axis=1)
    rights = np.stack([mats[0], mats[4], mats[2], mats[6], right_b])
    lefts = np.stack([mats[1], mats[5], mats[3], mats[7], left_b])
    order = np.concatenate([np.arange(H), N - 1 - np.arange(H)])
    tilt = np.exp(-2j * np.pi * 127.5 * order / N)
    phase = np.outer(tilt, tilt)
    phases = np.stack([phase.real, phase.imag]).astype(np.float32)
    return rights, lefts, phases


def mirror(value):
    lanes = H - 1 - lax.broadcasted_iota(jnp.int32, (N, H), 1)
    right = jnp.take_along_axis(value[:, H:], lanes, axis=1)
    value = jnp.concatenate([value[:, :H], right], axis=1)
    rows = 7 - lax.broadcasted_iota(jnp.int32, (8, N), 0)
    tiles = [
        jnp.take_along_axis(value[N - 8 - 8 * i : N - 8 * i], rows, axis=0) for i in range(H // 8)
    ]
    return jnp.concatenate([value[:H]] + tiles, axis=0)


def parts(value):
    high = value.astype(BF16)
    return high, (value - high.astype(F32)).astype(BF16)


def dot(left, right):
    return jnp.dot(left, right, preferred_element_type=F32)


CH = 16
CHUNKS = H // CH


def fold4(tl, tr, bl, br):
    a, b = tl + bl, tr + br
    c, d = tl - bl, tr - br
    return a + b, a - b, c + d, c - d


def mul(a, b):
    return a[0] * b[0] - a[1] * b[1], a[0] * b[1] + a[1] * b[0]


def mulc(a, b):
    return a[0] * b[0] + a[1] * b[1], a[0] * b[1] - a[1] * b[0]


QUADS = ((0, 0), (0, 1), (1, 0), (1, 1))


def quad(ref, lead, row, q):
    r, c = q
    return ref[lead + (slice(r * H + row, r * H + row + CH), slice(c * H, c * H + H))]


def put(ref, lead, row, q, value):
    r, c = q
    ref[lead + (slice(r * H + row, r * H + row + CH), slice(c * H, c * H + H))] = value


def store_right_prop(op, mode, row, real, imag):
    for index, (r, c) in enumerate(QUADS):
        for part, value in ((0, real[index]), (1, imag[index])):
            high, low = parts(value)
            rows = slice(mode * N + r * H + row, mode * N + r * H + row + CH)
            op[c, rows, part * H : part * H + H] = high
            op[c, rows, N + part * H : N + part * H + H] = low


def store_right_four(op, mode, row, real, imag):
    for index, (r, c) in enumerate(QUADS):
        for part, value in ((0, real[index]), (1, imag[index])):
            high, low = parts(value)
            rows = slice(mode * N + r * H + row, mode * N + r * H + row + CH)
            op[part, rows, c * H : c * H + H] = high
            op[part, rows, N + c * H : N + c * H + H] = low


def three(ref_value):
    return jnp.concatenate([ref_value, ref_value[:, :N]], axis=1)


def prop_products(op, mid, out, rights, lefts, even, odd, modes):
    for c, which in ((0, even), (1, odd)):
        for m in range(modes):
            rows = slice(m * N, m * N + N)
            res = dot(three(op[c, rows, :]), rights[which])
            high, low = parts(res)
            for level, value in ((0, high), (1, low)):
                for r in (0, 1):
                    for p in (0, 1):
                        mid[
                            r,
                            level * N + p * H : level * N + p * H + H,
                            m * N + c * H : m * N + c * H + H,
                        ] = value[r * H : r * H + H, p * H : p * H + H]
    for r, which in ((0, even), (1, odd)):
        for m in range(modes):
            cols = slice(m * N, m * N + N)
            x = mid[r, :, cols]
            x = jnp.concatenate([x, x[:N]], axis=0)
            out[r, :, cols] = dot(lefts[which], x)


def four_products(op, mid, out, rights, lefts, modes):
    for p in (0, 1):
        for m in range(modes):
            rows = slice(m * N, m * N + N)
            res = dot(three(op[p, rows, :]), rights[4])
            high, low = parts(res)
            mid[p, :N, m * N : m * N + N] = high
            mid[p, N:, m * N : m * N + N] = low
    for p in (0, 1):
        for m in range(modes):
            cols = slice(m * N, m * N + N)
            x = mid[p, :, cols]
            x = jnp.concatenate([x, x[:N]], axis=0)
            out[p, :, cols] = dot(lefts[4], x)


def load_prop(out, mode, row):
    result = []
    for p in (0, 1):
        result.append(
            [
                out[r, p * H + row : p * H + row + CH, mode * N + c * H : mode * N + c * H + H]
                for r, c in QUADS
            ]
        )
    return result


def load_four(out, mode, row, sign):
    real, imag = [
        [
            out[p, r * H + row : r * H + row + CH, mode * N + c * H : mode * N + c * H + H]
            for r, c in QUADS
        ]
        for p in (0, 1)
    ]
    if sign > 0:
        return (
            [real[0], imag[1], imag[2], -real[3]],
            [imag[0], -real[1], -real[2], -imag[3]],
        )
    return (
        [real[0], -imag[1], -imag[2], -real[3]],
        [imag[0], real[1], real[2], -imag[3]],
    )


def unfold4(ee, eo, oe, oo):
    a, b = ee + eo, ee - eo
    c, d = oe + oo, oe - oo
    return a + c, b + d, a - c, b - d


def main_kernel(
    corner, own, right, lower, probes, amp, rights, lefts, phases,
    terms, grads,
    obj, q1, op, mid, out, acc,
):
    modes = probes.shape[0]
    y0, x0 = corner[0, 0], corner[0, 1]
    up = lax.rem(N - y0, N)
    back = lax.rem(N - x0, N)
    below = lax.broadcasted_iota(jnp.int32, (N, N), 0) < y0
    beside = lax.broadcasted_iota(jnp.int32, (N, N), 1) < x0
    for s in range(2):
        window = []
        for p in range(2):
            upper = jnp.where(beside, right[s, p], own[s, p])
            value = jnp.where(below, lower[s, p], upper)
            value = pltpu.roll(pltpu.roll(value, up, 0), back, 1)
            window.append(mirror(value))
        if s == 1:
            window = mul(window, (phases[0], phases[1]))
        obj[s, 0], obj[s, 1] = window

    def field(ref, lead, row, q):
        return quad(ref, lead + (0,), row, q), quad(ref, lead + (1,), row, q)

    def fold_pairs(pairs):
        return fold4(*[v[0] for v in pairs]), fold4(*[v[1] for v in pairs])

    for m in range(modes):
        for k in range(CHUNKS):
            row = k * CH
            pairs = [mul(field(probes, (m,), row, q), field(obj, (0,), row, q)) for q in QUADS]
            store_right_prop(op, m, row, *fold_pairs(pairs))
    prop_products(op, mid, out, rights, lefts, 0, 1, modes)
    for m in range(modes):
        for k in range(CHUNKS):
            row = k * CH
            real, imag = load_prop(out, m, row)
            pixels = list(zip(unfold4(*real), unfold4(*imag)))
            for q, v in zip(QUADS, pixels):
                put(q1, (m, 0), row, q, v[0])
                put(q1, (m, 1), row, q, v[1])
            pairs = [mul(v, field(obj, (1,), row, q)) for q, v in zip(QUADS, pixels)]
            store_right_four(op, m, row, *fold_pairs(pairs))
    four_products(op, mid, out, rights, lefts, modes)
    for k in range(CHUNKS):
        row = k * CH
        total = [jnp.zeros((CH, H), F32)] * 4
        for m in range(modes):
            real, imag = load_four(out, m, row, 1)
            for i, v in enumerate(zip(unfold4(*real), unfold4(*imag))):
                total[i] = total[i] + (v[0] * v[0] + v[1] * v[1])
        factor = [
            1.0 - quad(amp, (0,), row, q) * lax.rsqrt(total[i] + 1.0) for i, q in enumerate(QUADS)
        ]
        for m in range(modes):
            real, imag = load_four(out, m, row, 1)
            pairs = [
                (factor[i] * v[0], factor[i] * v[1])
                for i, v in enumerate(zip(unfold4(*real), unfold4(*imag)))
            ]
            store_right_four(op, m, row, *fold_pairs(pairs))
    four_products(op, mid, out, rights, lefts, modes)
    for k in range(CHUNKS):
        row = k * CH
        total = [(jnp.zeros((CH, H), F32), jnp.zeros((CH, H), F32))] * 4
        for m in range(modes):
            real, imag = load_four(out, m, row, -1)
            pairs = []
            for i, v in enumerate(zip(unfold4(*real), unfold4(*imag))):
                q = QUADS[i]
                g = mulc(field(q1, (m,), row, q), v)
                total[i] = (total[i][0] + g[0], total[i][1] + g[1])
                pairs.append(mulc(field(obj, (1,), row, q), v))
            store_right_prop(op, m, row, *fold_pairs(pairs))
        for i, q in enumerate(QUADS):
            phase = (quad(phases, (0,), row, q), quad(phases, (1,), row, q))
            g = mulc(phase, total[i])
            put(acc, (1, 0), row, q, g[0])
            put(acc, (1, 1), row, q, g[1])
    prop_products(op, mid, out, rights, lefts, 2, 3, modes)
    for k in range(CHUNKS):
        row = k * CH
        total = [(jnp.zeros((CH, H), F32), jnp.zeros((CH, H), F32))] * 4
        for m in range(modes):
            real, imag = load_prop(out, m, row)
            for i, v in enumerate(zip(unfold4(*real), unfold4(*imag))):
                q = QUADS[i]
                g = mulc(field(probes, (m,), row, q), v)
                total[i] = (total[i][0] + g[0], total[i][1] + g[1])
                t = mulc(field(obj, (0,), row, q), v)
                put(terms, (m, 0), row, q, t[0])
                put(terms, (m, 1), row, q, t[1])
        for i, q in enumerate(QUADS):
            put(acc, (0, 0), row, q, total[i][0])
            put(acc, (0, 1), row, q, total[i][1])
    for m in range(modes):
        for p in range(2):
            terms[m, p] = mirror(terms[m, p])
    for s in range(2):
        for p in range(2):
            grads[s, p] = pltpu.roll(pltpu.roll(mirror(acc[s, p]), y0, 0), x0, 1)


def mirror_kernel(source, target):
    target[0] = mirror(source[0])


def mirrored(images):
    return pl.pallas_call(
        mirror_kernel,
        grid=(images.shape[0],),
        in_specs=[pl.BlockSpec((1, N, N), lambda i: (i, 0, 0))],
        out_specs=pl.BlockSpec((1, N, N), lambda i: (i, 0, 0)),
        out_shape=jax.ShapeDtypeStruct(images.shape, F32),
    )(images)


def compute(corner, own, right, lower, probes, amp):
    rights, lefts, phases = (jnp.asarray(v) for v in constants())
    modes = probes.shape[0]
    flip = mirrored(probes.reshape(-1, N, N)).reshape(probes.shape)
    flip_amp = mirrored(amp)
    vmem = pl.BlockSpec(memory_space=pltpu.VMEM)
    return pl.pallas_call(
        main_kernel,
        in_specs=[pl.BlockSpec(memory_space=pltpu.SMEM)] + [vmem] * 8,
        out_specs=[vmem, vmem],
        out_shape=[
            jax.ShapeDtypeStruct(probes.shape, F32),
            jax.ShapeDtypeStruct(own.shape, F32),
        ],
        scratch_shapes=[
            pltpu.VMEM((2, 2, N, N), F32),
            pltpu.VMEM((modes, 2, N, N), F32),
            pltpu.VMEM((2, modes * N, 2 * N), BF16),
            pltpu.VMEM((2, 2 * N, modes * N), BF16),
            pltpu.VMEM((2, N, modes * N), F32),
            pltpu.VMEM((2, 2, N, N), F32),
        ],
        compiler_params=pltpu.CompilerParams(vmem_limit_bytes=56 * 1024 * 1024),
        cost_estimate=pl.CostEstimate(
            flops=12_000_000_000, bytes_accessed=12 << 20, transcendentals=0
        ),
    )(corner, own, right, lower, flip, flip_amp, rights, lefts, phases)


POS = ("y", "zh", "core")
TILE = ("x", "zl")


def shifted(value, axes, steps):
    count = math.prod(lax.axis_size(axis) for axis in axes)
    first, last = (max(0, -steps), min(count, count - steps))
    return lax.ppermute(value, axes, [(source, source + steps) for source in range(first, last)])


def piece(value, index):
    return lax.dynamic_index_in_dim(value, index, 0, keepdims=False)


def ring(value, axis, step):
    count = lax.axis_size(axis)
    return lax.ppermute(value, axis, [(i, (i + step) % count) for i in range(count)])


def scatter_sum(value, axis):
    count, me = lax.axis_size(axis), lax.axis_index(axis)
    arrived = [
        ring(piece(value, (me + step) % count), axis, step) for step in range(1, count)
    ]
    total = piece(value, me)
    for part in arrived:
        total = total + part
    return total


def gather(value, axis):
    count, me = lax.axis_size(axis), lax.axis_index(axis)
    whole = jnp.zeros((count,) + value.shape, value.dtype)
    whole = lax.dynamic_update_index_in_dim(whole, value, me, 0)
    for step in range(1, count):
        part = ring(value, axis, step)
        whole = lax.dynamic_update_index_in_dim(whole, part, (me + count - step) % count, 0)
    return whole


def exchange_sum(value, axis, bit):
    count = lax.axis_size(axis)
    return value + lax.ppermute(value, axis, [(i, i ^ bit) for i in range(count)])


def total_over_devices(value, order):
    shape = value.shape
    axes = ("core",) + order
    for axis in axes:
        value = scatter_sum(value.reshape(lax.axis_size(axis), -1, N), axis)
    value = exchange_sum(value, "zl", 1)
    value = exchange_sum(value, "zh", 1)
    value = exchange_sum(value, "zh", 2)
    for axis in axes[::-1]:
        value = gather(value, axis)
        value = value.reshape(-1, N)
    return value.reshape(shape)


def per_device(object_field, probe_modes, amplitudes, corners):
    row = lax.broadcasted_iota(jnp.int32, (N, N), 0)
    col = lax.broadcasted_iota(jnp.int32, (N, N), 1)
    y0, x0 = corners[0, 0], corners[0, 1]
    above = shifted(corners, POS, 1)
    y1, x1 = above[0, 0], above[0, 1]
    right = shifted(object_field, TILE, -1)
    mixed = jnp.where(col < x1, right, object_field)
    lower = shifted(mixed, POS, -1)
    terms, grads = compute(corners, object_field, right, lower, probe_modes, amplitudes)
    arrived = shifted(grads, POS, 1)
    probe_grad = total_over_devices(terms, ("x", "y"))
    kept = jnp.where(row >= y0, grads, 0.0)
    taken = jnp.where(row < y1, arrived, 0.0)
    leaving = jnp.where(col < x0, kept, 0.0) + jnp.where(col < x1, taken, 0.0)
    staying = jnp.where(col >= x0, kept, 0.0) + jnp.where(col >= x1, taken, 0.0)
    object_grad = staying + shifted(leaving, TILE, 1)
    return (object_grad, probe_grad)


def solution(mesh):
    split = jax.sharding.Mesh(mesh.devices.reshape(4, 4, 2, 4, 2), POS + TILE)
    in_specs = (
        P(None, None, POS, TILE),
        P(),
        P(POS + TILE, None, None),
        P(POS + TILE, None),
    )
    out_specs = (P(None, None, POS, TILE), P())
    return jax.shard_map(
        per_device, mesh=split, in_specs=in_specs, out_specs=out_specs, check_vma=False
    )
```

```python
import math

import jax
import jax.numpy as jnp
import numpy as np
from jax import lax
from jax.experimental import pallas as pl
from jax.experimental.pallas import tpu as pltpu
from jax.sharding import PartitionSpec as P

N = 256
H = 128
F32 = jnp.float32
BF16 = jnp.bfloat16


def split_np(matrix):
    high = matrix.astype(np.float32).astype(jnp.bfloat16)
    low = (matrix - high.astype(np.float64)).astype(np.float32).astype(jnp.bfloat16)
    return high, low


def constants():
    count = np.arange(N)
    fourier = np.exp(-2j * np.pi * (np.outer(count, count) % N) / N) / math.sqrt(N)
    freq = np.where(count < H, count, count - N).astype(np.float64)
    fresnel = np.exp(-1j * np.pi * freq * freq / (2.0 * N))
    prop = (np.conj(fourier) * fresnel[None, :]) @ fourier
    straight, turned = prop[:H, :H], prop[:H, ::-1][:, :H]
    mats = []
    for part in ((straight + turned) / 2, (straight - turned) / 2):
        for side in (part, np.conj(part)):
            real, imag = side.real, side.imag
            mats.append(np.stack(split_np(np.block([[real, imag], [-imag, real]]))))
    half = np.arange(H) - 127.5
    angle = 2 * np.pi * np.outer(half, half) / N
    zero = np.zeros((H, H))
    both = np.block([[np.cos(angle) / 16, zero], [zero, np.sin(angle) / 16]])
    mats.append(np.stack(split_np(both)))
    table = np.stack(mats)
    order = np.concatenate([np.arange(H), N - 1 - np.arange(H)])
    tilt = np.exp(-2j * np.pi * 127.5 * order / N)
    phase = np.outer(tilt, tilt)
    phases = np.stack([phase.real, phase.imag]).astype(np.float32)
    return table, phases


def mirror(value):
    lanes = H - 1 - lax.broadcasted_iota(jnp.int32, (N, H), 1)
    right = jnp.take_along_axis(value[:, H:], lanes, axis=1)
    value = jnp.concatenate([value[:, :H], right], axis=1)
    rows = 7 - lax.broadcasted_iota(jnp.int32, (8, N), 0)
    tiles = [
        jnp.take_along_axis(value[N - 8 - 8 * i : N - 8 * i], rows, axis=0) for i in range(H // 8)
    ]
    return jnp.concatenate([value[:H]] + tiles, axis=0)


def parts(value):
    high = value.astype(BF16)
    return high, (value - high.astype(F32)).astype(BF16)


def dot(left, right):
    return jnp.dot(left, right, preferred_element_type=F32)


CH = 16
CHUNKS = H // CH


def fold4(tl, tr, bl, br):
    a, b = tl + bl, tr + br
    c, d = tl - bl, tr - br
    return a + b, a - b, c + d, c - d


def mul(a, b):
    return a[0] * b[0] - a[1] * b[1], a[0] * b[1] + a[1] * b[0]


def mulc(a, b):
    return a[0] * b[0] + a[1] * b[1], a[0] * b[1] - a[1] * b[0]


QUADS = ((0, 0), (0, 1), (1, 0), (1, 1))


def quad(ref, lead, row, q):
    r, c = q
    return ref[lead + (slice(r * H + row, r * H + row + CH), slice(c * H, c * H + H))]


def put(ref, lead, row, q, value):
    r, c = q
    ref[lead + (slice(r * H + row, r * H + row + CH), slice(c * H, c * H + H))] = value


def store_right_prop(op, mode, row, real, imag):
    for index, (r, c) in enumerate(QUADS):
        for part, value in ((0, real[index]), (1, imag[index])):
            high, low = parts(value)
            rows = slice(mode * N + r * H + row, mode * N + r * H + row + CH)
            op[c, rows, part * H : part * H + H] = high
            op[c, rows, N + part * H : N + part * H + H] = low


def store_right_four(op, mode, row, real, imag):
    for index, (r, c) in enumerate(QUADS):
        for part, value in ((0, real[index]), (1, imag[index])):
            high, low = parts(value)
            rows = slice(mode * N + r * H + row, mode * N + r * H + row + CH)
            op[part, rows, c * H : c * H + H] = high
            op[part, rows, N + c * H : N + c * H + H] = low


def stack_rows(table, which):
    return jnp.concatenate([table[which, 0], table[which, 0], table[which, 1]], axis=0)


def stack_cols(table, which):
    return jnp.concatenate([table[which, 0], table[which, 0], table[which, 1]], axis=1)


def three(ref_value):
    return jnp.concatenate([ref_value, ref_value[:, :N]], axis=1)


def prop_products(op, mid, out, table, conjugate, modes):
    for c in (0, 1):
        matrix = stack_rows(table, 2 * c + conjugate)
        for m in range(modes):
            rows = slice(m * N, m * N + N)
            res = dot(three(op[c, rows, :]), matrix)
            high, low = parts(res)
            for level, value in ((0, high), (1, low)):
                for r in (0, 1):
                    for p in (0, 1):
                        mid[
                            r,
                            level * N + p * H : level * N + p * H + H,
                            m * N + c * H : m * N + c * H + H,
                        ] = value[r * H : r * H + H, p * H : p * H + H]
    for r in (0, 1):
        matrix = stack_cols(table, 2 * r + 1 - conjugate)
        for m in range(modes):
            cols = slice(m * N, m * N + N)
            x = mid[r, :, cols]
            x = jnp.concatenate([x, x[:N]], axis=0)
            out[r, :, cols] = dot(matrix, x)


def four_products(op, mid, out, table, modes):
    matrix = stack_rows(table, 4)
    for p in (0, 1):
        for m in range(modes):
            rows = slice(m * N, m * N + N)
            res = dot(three(op[p, rows, :]), matrix)
            high, low = parts(res)
            mid[p, :N, m * N : m * N + N] = high
            mid[p, N:, m * N : m * N + N] = low
    matrix = stack_cols(table, 4)
    for p in (0, 1):
        for m in range(modes):
            cols = slice(m * N, m * N + N)
            x = mid[p, :, cols]
            x = jnp.concatenate([x, x[:N]], axis=0)
            out[p, :, cols] = dot(matrix, x)


def load_prop(out, mode, row):
    result = []
    for p in (0, 1):
        result.append(
            [
                out[r, p * H + row : p * H + row + CH, mode * N + c * H : mode * N + c * H + H]
                for r, c in QUADS
            ]
        )
    return result


def load_four(out, mode, row, sign):
    real, imag = [
        [
            out[p, r * H + row : r * H + row + CH, mode * N + c * H : mode * N + c * H + H]
            for r, c in QUADS
        ]
        for p in (0, 1)
    ]
    if sign > 0:
        return (
            [real[0], imag[1], imag[2], -real[3]],
            [imag[0], -real[1], -real[2], -imag[3]],
        )
    return (
        [real[0], -imag[1], -imag[2], -real[3]],
        [imag[0], real[1], real[2], -imag[3]],
    )


def unfold4(ee, eo, oe, oo):
    a, b = ee + eo, ee - eo
    c, d = oe + oo, oe - oo
    return a + c, b + d, a - c, b - d


def main_kernel(
    place, own, right, other, probes, amp, table, phases,
    terms, grads,
    obj, q1, op, mid, out, acc,
):
    modes = probes.shape[0]
    y0, x0, odd, live = place[0], place[1], place[2], place[3]
    up = lax.rem(N - y0, N)
    back = lax.rem(N - x0, N)
    rows = lax.broadcasted_iota(jnp.int32, (N, N), 0)
    mine = jnp.where(rows >= y0, 1 - odd, odd) > 0
    beside = lax.broadcasted_iota(jnp.int32, (N, N), 1) < x0
    scale = live.astype(F32)
    for s in range(2):
        window = []
        for p in range(2):
            value = jnp.where(beside, right[s, p], own[s, p]) * scale
            value = jnp.where(mine, value, other[s, p])
            value = pltpu.roll(pltpu.roll(value, up, 0), back, 1)
            window.append(mirror(value))
        if s == 1:
            window = mul(window, (phases[0], phases[1]))
        obj[s, 0], obj[s, 1] = window

    def field(ref, lead, row, q):
        return quad(ref, lead + (0,), row, q), quad(ref, lead + (1,), row, q)

    def fold_pairs(pairs):
        return fold4(*[v[0] for v in pairs]), fold4(*[v[1] for v in pairs])

    for m in range(modes):
        for k in range(CHUNKS):
            row = k * CH
            pairs = [mul(field(probes, (m,), row, q), field(obj, (0,), row, q)) for q in QUADS]
            store_right_prop(op, m, row, *fold_pairs(pairs))
    prop_products(op, mid, out, table, 0, modes)
    for m in range(modes):
        for k in range(CHUNKS):
            row = k * CH
            real, imag = load_prop(out, m, row)
            pixels = list(zip(unfold4(*real), unfold4(*imag)))
            for q, v in zip(QUADS, pixels):
                put(q1, (m, 0), row, q, v[0])
                put(q1, (m, 1), row, q, v[1])
            pairs = [mul(v, field(obj, (1,), row, q)) for q, v in zip(QUADS, pixels)]
            store_right_four(op, m, row, *fold_pairs(pairs))
    four_products(op, mid, out, table, modes)
    for k in range(CHUNKS):
        row = k * CH
        total = [jnp.zeros((CH, H), F32)] * 4
        for m in range(modes):
            real, imag = load_four(out, m, row, 1)
            for i, v in enumerate(zip(unfold4(*real), unfold4(*imag))):
                total[i] = total[i] + (v[0] * v[0] + v[1] * v[1])
        factor = [
            1.0 - quad(amp, (0,), row, q) * lax.rsqrt(total[i] + 1.0) for i, q in enumerate(QUADS)
        ]
        for m in range(modes):
            real, imag = load_four(out, m, row, 1)
            pairs = [
                (factor[i] * v[0], factor[i] * v[1])
                for i, v in enumerate(zip(unfold4(*real), unfold4(*imag)))
            ]
            store_right_four(op, m, row, *fold_pairs(pairs))
    four_products(op, mid, out, table, modes)
    for k in range(CHUNKS):
        row = k * CH
        total = [(jnp.zeros((CH, H), F32), jnp.zeros((CH, H), F32))] * 4
        for m in range(modes):
            real, imag = load_four(out, m, row, -1)
            pairs = []
            for i, v in enumerate(zip(unfold4(*real), unfold4(*imag))):
                q = QUADS[i]
                g = mulc(field(q1, (m,), row, q), v)
                total[i] = (total[i][0] + g[0], total[i][1] + g[1])
                pairs.append(mulc(field(obj, (1,), row, q), v))
            store_right_prop(op, m, row, *fold_pairs(pairs))
        for i, q in enumerate(QUADS):
            phase = (quad(phases, (0,), row, q), quad(phases, (1,), row, q))
            g = mulc(phase, total[i])
            put(acc, (1, 0), row, q, g[0])
            put(acc, (1, 1), row, q, g[1])
    prop_products(op, mid, out, table, 1, modes)
    for k in range(CHUNKS):
        row = k * CH
        total = [(jnp.zeros((CH, H), F32), jnp.zeros((CH, H), F32))] * 4
        for m in range(modes):
            real, imag = load_prop(out, m, row)
            for i, v in enumerate(zip(unfold4(*real), unfold4(*imag))):
                q = QUADS[i]
                g = mulc(field(probes, (m,), row, q), v)
                total[i] = (total[i][0] + g[0], total[i][1] + g[1])
                t = mulc(field(obj, (0,), row, q), v)
                put(terms, (m, 0), row, q, t[0])
                put(terms, (m, 1), row, q, t[1])
        for i, q in enumerate(QUADS):
            put(acc, (0, 0), row, q, total[i][0])
            put(acc, (0, 1), row, q, total[i][1])
    for m in range(modes):
        for p in range(2):
            terms[m, p] = mirror(terms[m, p])
    for s in range(2):
        for p in range(2):
            grads[s, p] = pltpu.roll(pltpu.roll(mirror(acc[s, p]), y0, 0), x0, 1)


def mirror_kernel(source, target):
    target[0] = mirror(source[0])


def mirrored(images):
    return pl.pallas_call(
        mirror_kernel,
        grid=(images.shape[0],),
        in_specs=[pl.BlockSpec((1, N, N), lambda i: (i, 0, 0))],
        out_specs=pl.BlockSpec((1, N, N), lambda i: (i, 0, 0)),
        out_shape=jax.ShapeDtypeStruct(images.shape, F32),
    )(images)


def compute(place, own, right, other, probes, amp):
    table, phases = (jnp.asarray(v) for v in constants())
    modes = probes.shape[0]
    flip = mirrored(probes.reshape(-1, N, N)).reshape(probes.shape)
    flip_amp = mirrored(amp)
    vmem = pl.BlockSpec(memory_space=pltpu.VMEM)
    return pl.pallas_call(
        main_kernel,
        in_specs=[pl.BlockSpec(memory_space=pltpu.SMEM)] + [vmem] * 7,
        out_specs=[vmem, vmem],
        out_shape=[
            jax.ShapeDtypeStruct(probes.shape, F32),
            jax.ShapeDtypeStruct(own.shape, F32),
        ],
        scratch_shapes=[
            pltpu.VMEM((2, 2, N, N), F32),
            pltpu.VMEM((modes, 2, N, N), F32),
            pltpu.VMEM((2, modes * N, 2 * N), BF16),
            pltpu.VMEM((2, 2 * N, modes * N), BF16),
            pltpu.VMEM((2, N, modes * N), F32),
            pltpu.VMEM((2, 2, N, N), F32),
        ],
        compiler_params=pltpu.CompilerParams(vmem_limit_bytes=48 * 1024 * 1024),
        cost_estimate=pl.CostEstimate(
            flops=12_000_000_000, bytes_accessed=12 << 20, transcendentals=0
        ),
    )(place, own, right, other, flip, flip_amp, table, phases)


POS = ("y", "zh", "core")
TILE = ("x", "zl")
ROWS = 32
COLUMNS = 8


def shifted(value, axes, steps):
    count = math.prod(lax.axis_size(axis) for axis in axes)
    first, last = (max(0, -steps), min(count, count - steps))
    return lax.ppermute(value, axes, [(source, source + steps) for source in range(first, last)])


def piece(value, index):
    return lax.dynamic_index_in_dim(value, index, 0, keepdims=False)


def ring(value, axis, step):
    count = lax.axis_size(axis)
    return lax.ppermute(value, axis, [(i, (i + step) % count) for i in range(count)])


def pieces(value, axis):
    count, me = lax.axis_size(axis), lax.axis_index(axis)
    value = value.reshape(count, -1, N)
    return [piece(value, (me + step) % count) for step in range(1, count)] + [piece(value, me)]


def scatter_sum(parts, axis):
    arrived = [ring(part, axis, step + 1) for step, part in enumerate(parts[:-1])]
    total = parts[-1]
    for part in arrived:
        total = total + part
    return total


def after(value, *others):
    return lax.optimization_barrier((value,) + others)[0]


def gather(value, axis):
    count, me = lax.axis_size(axis), lax.axis_index(axis)
    whole = jnp.zeros((count,) + value.shape, value.dtype)
    whole = lax.dynamic_update_index_in_dim(whole, value, me, 0)
    for step in range(1, count):
        part = ring(value, axis, step)
        whole = lax.dynamic_update_index_in_dim(whole, part, (me + count - step) % count, 0)
    return whole


def exchange_sum(value, axis, bit):
    count = lax.axis_size(axis)
    return value + lax.ppermute(value, axis, [(i, i ^ bit) for i in range(count)])


def spread(value, order):
    value = exchange_sum(value, "zl", 1)
    value = exchange_sum(value, "zh", 1)
    value = exchange_sum(value, "zh", 2)
    for axis in order[::-1] + ("core",):
        value = gather(value, axis).reshape(-1, N)
    return value


def moved(value, even, odd):
    pairs = []
    for row in range(ROWS):
        for column in range(COLUMNS):
            target = row + (odd if column % 2 else even)
            if column % 2:
                target %= ROWS
            if 0 <= target < ROWS:
                pairs.append((row * COLUMNS + column, target * COLUMNS + column))
    return lax.ppermute(value, POS + TILE, pairs)


def per_device(object_field, probe_modes, amplitudes, corners):
    row = lax.broadcasted_iota(jnp.int32, (N, N), 0)
    col = lax.broadcasted_iota(jnp.int32, (N, N), 1)
    odd = lax.axis_index("zl")
    is_odd = odd == 1
    first = (lax.axis_index(POS) == 0) & is_odd
    above = lax.ppermute(corners, POS, [(i, (i + 1) % ROWS) for i in range(ROWS)])
    yp, xp = [jnp.where(is_odd, above[0, i], corners[0, i]) for i in (0, 1)]
    yq, xq = [jnp.where(is_odd, corners[0, i], above[0, i]) for i in (0, 1)]
    amplitude = moved(amplitudes, 0, 1)
    right = shifted(object_field, TILE, -1)
    mixed = jnp.where(col < xq, right, object_field)
    other = moved(mixed, -1, 1)
    live = jnp.where(first, 0, 1)
    place = jnp.stack([yp, xp, odd, live]).astype(jnp.int32)
    terms, grads = compute(place, object_field, right, other, probe_modes, amplitude)
    arrived = moved(grads, 1, -1)
    partial = scatter_sum(pieces(terms, "core"), "core")
    across = pieces(partial, "x")
    partial = scatter_sum(across, "x")
    partial = scatter_sum(pieces(partial, "y"), "y")
    arrived = after(arrived, *across)
    kept = jnp.where(((row >= yp) != is_odd) & ~first, grads, 0.0)
    taken = jnp.where((row < yq) != is_odd, arrived, 0.0)
    leaving = jnp.where(col < xp, kept, 0.0) + jnp.where(col < xq, taken, 0.0)
    staying = jnp.where(col >= xp, kept, 0.0) + jnp.where(col >= xq, taken, 0.0)
    received = shifted(leaving, TILE, 1)
    partial = after(partial, received)
    object_grad = staying + received
    probe_grad = spread(partial, ("x", "y")).reshape(terms.shape)
    return (object_grad, probe_grad)


def solution(mesh):
    split = jax.sharding.Mesh(mesh.devices.reshape(4, 4, 2, 4, 2), POS + TILE)
    in_specs = (
        P(None, None, POS, TILE),
        P(),
        P(POS + TILE, None, None),
        P(POS + TILE, None),
    )
    out_specs = (P(None, None, POS, TILE), P())
    return jax.shard_map(
        per_device, mesh=split, in_specs=in_specs, out_specs=out_specs, check_vma=False
    )
```

```python
import functools
import math

import jax
import jax.numpy as jnp
import numpy as np
from jax import lax
from jax.experimental import pallas as pl
from jax.experimental.pallas import tpu as pltpu
from jax.sharding import PartitionSpec as P

N = 256
H = 128
F32 = jnp.float32
BF16 = jnp.bfloat16


def split_np(matrix):
    high = matrix.astype(np.float32).astype(jnp.bfloat16)
    low = (matrix - high.astype(np.float64)).astype(np.float32).astype(jnp.bfloat16)
    return high, low


def constants():
    count = np.arange(N)
    fourier = np.exp(-2j * np.pi * (np.outer(count, count) % N) / N) / math.sqrt(N)
    freq = np.where(count < H, count, count - N).astype(np.float64)
    fresnel = np.exp(-1j * np.pi * freq * freq / (2.0 * N))
    prop = (np.conj(fourier) * fresnel[None, :]) @ fourier
    straight, turned = prop[:H, :H], prop[:H, ::-1][:, :H]
    mats = []
    for part in ((straight + turned) / 2, (straight - turned) / 2):
        for side in (part, np.conj(part)):
            real, imag = side.real, side.imag
            mats.append(np.stack(split_np(np.block([[real, imag], [-imag, real]]))))
    half = np.arange(H) - 127.5
    angle = 2 * np.pi * np.outer(half, half) / N
    zero = np.zeros((H, H))
    both = np.block([[np.cos(angle) / 16, zero], [zero, np.sin(angle) / 16]])
    mats.append(np.stack(split_np(both)))
    table = np.stack(mats)
    order = np.concatenate([np.arange(H), N - 1 - np.arange(H)])
    tilt = np.exp(-2j * np.pi * 127.5 * order / N)
    phase = np.outer(tilt, tilt)
    phases = np.stack([phase.real, phase.imag]).astype(np.float32)
    return table, phases


def mirror(value):
    lanes = H - 1 - lax.broadcasted_iota(jnp.int32, (N, H), 1)
    right = jnp.take_along_axis(value[:, H:], lanes, axis=1)
    value = jnp.concatenate([value[:, :H], right], axis=1)
    rows = 7 - lax.broadcasted_iota(jnp.int32, (8, N), 0)
    tiles = [
        jnp.take_along_axis(value[N - 8 - 8 * i : N - 8 * i], rows, axis=0) for i in range(H // 8)
    ]
    return jnp.concatenate([value[:H]] + tiles, axis=0)


def parts(value):
    high = value.astype(BF16)
    return high, (value - high.astype(F32)).astype(BF16)


def dot(left, right):
    return jnp.dot(left, right, preferred_element_type=F32)


CH = 16
CHUNKS = H // CH


def fold4(tl, tr, bl, br):
    a, b = tl + bl, tr + br
    c, d = tl - bl, tr - br
    return a + b, a - b, c + d, c - d


def mul(a, b):
    return a[0] * b[0] - a[1] * b[1], a[0] * b[1] + a[1] * b[0]


def mulc(a, b):
    return a[0] * b[0] + a[1] * b[1], a[0] * b[1] - a[1] * b[0]


QUADS = ((0, 0), (0, 1), (1, 0), (1, 1))


def quad(ref, lead, row, q):
    r, c = q
    return ref[lead + (slice(r * H + row, r * H + row + CH), slice(c * H, c * H + H))]


def put(ref, lead, row, q, value):
    r, c = q
    ref[lead + (slice(r * H + row, r * H + row + CH), slice(c * H, c * H + H))] = value


def store_right_prop(op, mode, row, real, imag):
    for index, (r, c) in enumerate(QUADS):
        for part, value in ((0, real[index]), (1, imag[index])):
            high, low = parts(value)
            rows = slice(mode * N + r * H + row, mode * N + r * H + row + CH)
            op[c, rows, part * H : part * H + H] = high
            op[c, rows, N + part * H : N + part * H + H] = low


def store_right_four(op, mode, row, real, imag):
    for index, (r, c) in enumerate(QUADS):
        for part, value in ((0, real[index]), (1, imag[index])):
            high, low = parts(value)
            rows = slice(mode * N + r * H + row, mode * N + r * H + row + CH)
            op[part, rows, c * H : c * H + H] = high
            op[part, rows, N + c * H : N + c * H + H] = low


def stack_rows(table, which):
    return jnp.concatenate([table[which, 0], table[which, 0], table[which, 1]], axis=0)


def stack_cols(table, which):
    return jnp.concatenate([table[which, 0], table[which, 0], table[which, 1]], axis=1)


def three(ref_value):
    return jnp.concatenate([ref_value, ref_value[:, :N]], axis=1)


def prop_products(op, mid, out, table, conjugate, modes):
    for c in (0, 1):
        matrix = stack_rows(table, 2 * c + conjugate)
        for m in range(modes):
            rows = slice(m * N, m * N + N)
            res = dot(three(op[c, rows, :]), matrix)
            high, low = parts(res)
            for level, value in ((0, high), (1, low)):
                for r in (0, 1):
                    for p in (0, 1):
                        mid[
                            r,
                            level * N + p * H : level * N + p * H + H,
                            m * N + c * H : m * N + c * H + H,
                        ] = value[r * H : r * H + H, p * H : p * H + H]
    for r in (0, 1):
        matrix = stack_cols(table, 2 * r + 1 - conjugate)
        for m in range(modes):
            cols = slice(m * N, m * N + N)
            x = mid[r, :, cols]
            x = jnp.concatenate([x, x[:N]], axis=0)
            out[r, :, cols] = dot(matrix, x)


def four_products(op, mid, out, table, modes):
    matrix = stack_rows(table, 4)
    for p in (0, 1):
        for m in range(modes):
            rows = slice(m * N, m * N + N)
            res = dot(three(op[p, rows, :]), matrix)
            high, low = parts(res)
            mid[p, :N, m * N : m * N + N] = high
            mid[p, N:, m * N : m * N + N] = low
    matrix = stack_cols(table, 4)
    for p in (0, 1):
        for m in range(modes):
            cols = slice(m * N, m * N + N)
            x = mid[p, :, cols]
            x = jnp.concatenate([x, x[:N]], axis=0)
            out[p, :, cols] = dot(matrix, x)


def load_prop(out, mode, row):
    result = []
    for p in (0, 1):
        result.append(
            [
                out[r, p * H + row : p * H + row + CH, mode * N + c * H : mode * N + c * H + H]
                for r, c in QUADS
            ]
        )
    return result


def load_four(out, mode, row, sign):
    real, imag = [
        [
            out[p, r * H + row : r * H + row + CH, mode * N + c * H : mode * N + c * H + H]
            for r, c in QUADS
        ]
        for p in (0, 1)
    ]
    if sign > 0:
        return (
            [real[0], imag[1], imag[2], -real[3]],
            [imag[0], -real[1], -real[2], -imag[3]],
        )
    return (
        [real[0], -imag[1], -imag[2], -real[3]],
        [imag[0], real[1], real[2], -imag[3]],
    )


def unfold4(ee, eo, oe, oo):
    a, b = ee + eo, ee - eo
    c, d = oe + oo, oe - oo
    return a + c, b + d, a - c, b - d


def field(ref, lead, row, q):
    return quad(ref, lead + (0,), row, q), quad(ref, lead + (1,), row, q)


def fold_pairs(pairs):
    return fold4(*[v[0] for v in pairs]), fold4(*[v[1] for v in pairs])


def window_of(place, mine, other):
    y0, x0, odd = place[0], place[1], place[2]
    scale = place[3].astype(F32)
    rows = lax.broadcasted_iota(jnp.int32, (N, N), 0)
    upper = jnp.where(rows >= y0, 1 - odd, odd) > 0
    result = []
    for p in range(2):
        value = jnp.where(upper, mine[p] * scale, other[p])
        value = pltpu.roll(pltpu.roll(value, lax.rem(N - y0, N), 0), lax.rem(N - x0, N), 1)
        result.append(mirror(value))
    return result


def wrapped(place, value):
    return pltpu.roll(pltpu.roll(mirror(value), place[0], 0), place[1], 1)


def add_pair(total, value):
    return total[0] + value[0], total[1] + value[1]


def zeros():
    return [(jnp.zeros((CH, H), F32), jnp.zeros((CH, H), F32))] * 4


def first_kernel(place, mine, other, probes, table, q1, obj, op, mid, out):
    modes = probes.shape[0]
    obj[0], obj[1] = window_of(place, mine, other)
    for m in range(modes):
        for k in range(CHUNKS):
            row = k * CH
            pairs = [mul(field(probes, (m,), row, q), field(obj, (), row, q)) for q in QUADS]
            store_right_prop(op, m, row, *fold_pairs(pairs))
    prop_products(op, mid, out, table, 0, modes)
    for m in range(modes):
        for k in range(CHUNKS):
            row = k * CH
            real, imag = load_prop(out, m, row)
            for q, v in zip(QUADS, zip(unfold4(*real), unfold4(*imag))):
                put(q1, (m, 0), row, q, v[0])
                put(q1, (m, 1), row, q, v[1])


def second_kernel(
    place, mine, other, q1, amplitude, table, phases, grads, back_send, back_keep,
    obj, amp, op, mid, out,
):
    modes = q1.shape[0]
    obj[0], obj[1] = mul(window_of(place, mine, other), (phases[0], phases[1]))
    amp[...] = mirror(amplitude[0])
    for m in range(modes):
        for k in range(CHUNKS):
            row = k * CH
            pairs = [mul(field(q1, (m,), row, q), field(obj, (), row, q)) for q in QUADS]
            store_right_four(op, m, row, *fold_pairs(pairs))
    four_products(op, mid, out, table, modes)
    for k in range(CHUNKS):
        row = k * CH
        total = [jnp.zeros((CH, H), F32)] * 4
        for m in range(modes):
            real, imag = load_four(out, m, row, 1)
            for i, v in enumerate(zip(unfold4(*real), unfold4(*imag))):
                total[i] = total[i] + (v[0] * v[0] + v[1] * v[1])
        factor = [
            1.0 - quad(amp, (), row, q) * lax.rsqrt(total[i] + 1.0) for i, q in enumerate(QUADS)
        ]
        for m in range(modes):
            real, imag = load_four(out, m, row, 1)
            pairs = [
                (factor[i] * v[0], factor[i] * v[1])
                for i, v in enumerate(zip(unfold4(*real), unfold4(*imag)))
            ]
            store_right_four(op, m, row, *fold_pairs(pairs))
    four_products(op, mid, out, table, modes)
    for k in range(CHUNKS):
        row = k * CH
        total = zeros()
        for m in range(modes):
            real, imag = load_four(out, m, row, -1)
            pairs = []
            for i, v in enumerate(zip(unfold4(*real), unfold4(*imag))):
                q = QUADS[i]
                total[i] = add_pair(total[i], mulc(field(q1, (m,), row, q), v))
                pairs.append(mulc(field(obj, (), row, q), v))
            back = back_send if m < modes // 2 else back_keep
            store_right_prop(back, m % (modes // 2), row, *fold_pairs(pairs))
        for i, q in enumerate(QUADS):
            total[i] = mulc(field(phases, (), row, q), total[i])
        for i, q in enumerate(QUADS):
            put(grads, (0,), row, q, total[i][0])
            put(grads, (1,), row, q, total[i][1])
    for p in range(2):
        grads[p] = wrapped(place, grads[p])


def third_kernel(start, last, place, back, obj, probes, table, before, terms, grads, mid, out):
    modes = terms.shape[0]
    prop_products(back, mid, out, table, 1, modes)
    for k in range(CHUNKS):
        row = k * CH
        total = [field(before, (), row, q) for q in QUADS] if last else zeros()
        for m in range(modes):
            real, imag = load_prop(out, m, row)
            for i, v in enumerate(zip(unfold4(*real), unfold4(*imag))):
                q = QUADS[i]
                total[i] = add_pair(total[i], mulc(field(probes, (start + m,), row, q), v))
                term = mulc(field(obj, (), row, q), v)
                put(terms, (m, 0), row, q, term[0])
                put(terms, (m, 1), row, q, term[1])
        for i, q in enumerate(QUADS):
            put(grads, (0,), row, q, total[i][0])
            put(grads, (1,), row, q, total[i][1])
    for m in range(modes):
        for p in range(2):
            terms[m, p] = mirror(terms[m, p])
    if last:
        for p in range(2):
            grads[p] = wrapped(place, grads[p])


def call(kernel, args, shapes, scratch, flops):
    spec = pl.BlockSpec(memory_space=pltpu.VMEM)
    return pl.pallas_call(
        kernel,
        in_specs=[pl.BlockSpec(memory_space=pltpu.SMEM)] + [spec] * (len(args) - 1),
        out_specs=[spec] * len(shapes),
        out_shape=[jax.ShapeDtypeStruct(shape, dtype) for shape, dtype in shapes],
        scratch_shapes=[pltpu.VMEM(shape, dtype) for shape, dtype in scratch],
        compiler_params=pltpu.CompilerParams(vmem_limit_bytes=32 * 1024 * 1024),
        cost_estimate=pl.CostEstimate(flops=flops, bytes_accessed=4 << 20, transcendentals=0),
    )(*args)


def products_scratch(modes):
    return [((2, 2 * N, modes * N), BF16), ((2, N, modes * N), F32)]


def operand(modes):
    return ((2, modes * N, 2 * N), BF16)


def first(place, mine, other, probes, table):
    modes = probes.shape[0]
    return call(
        first_kernel,
        (place, mine, other, probes, table),
        [(probes.shape, F32), ((2, N, N), F32)],
        [operand(modes)] + products_scratch(modes),
        3 << 30,
    )


def second(place, mine, other, q1, amplitude, table, phases):
    modes = q1.shape[0]
    return call(
        second_kernel,
        (place, mine, other, q1, amplitude, table, phases),
        [((2, N, N), F32), operand(modes // 2), operand(modes // 2)],
        [((2, N, N), F32), ((N, N), F32), operand(modes)] + products_scratch(modes),
        6 << 30,
    )


def third(start, place, back, obj, probes, table, before):
    modes = probes.shape[0] // 2
    last = before is not None
    return call(
        functools.partial(third_kernel, start, last),
        (place, back, obj, probes, table, before if last else place[None]),
        [((modes, 2, N, N), F32), ((2, N, N), F32)],
        products_scratch(modes),
        2 << 30,
    )


def stage_kernel(core, source, table, phases, target, table_out, phases_out):
    target[0] = mirror(source[0])

    @pl.when(pl.program_id(0) == 0)
    def _():
        table_out[...] = table[...]
        phases_out[...] = phases[...]


def staged(core, probes):
    table, phases = (jnp.asarray(v) for v in constants())
    images = probes.reshape(-1, N, N)
    count = images.shape[0]
    half = count // 2
    whole = lambda value: pl.BlockSpec(value.shape, lambda i, core: (0,) * value.ndim)
    flip, table, phases = pl.pallas_call(
        stage_kernel,
        grid_spec=pltpu.PrefetchScalarGridSpec(
            num_scalar_prefetch=1,
            grid=(count,),
            in_specs=[
                pl.BlockSpec((1, N, N), lambda i, core: ((i + half * (1 - core[0])) % count, 0, 0)),
                whole(table),
                whole(phases),
            ],
            out_specs=[
                pl.BlockSpec((1, N, N), lambda i, core: (i, 0, 0)),
                whole(table),
                whole(phases),
            ],
        ),
        out_shape=[
            jax.ShapeDtypeStruct(images.shape, F32),
            jax.ShapeDtypeStruct(table.shape, table.dtype),
            jax.ShapeDtypeStruct(phases.shape, phases.dtype),
        ],
    )(core, images, table, phases)
    return flip.reshape(probes.shape), table, phases


POS = ("y", "zh", "core")
TILE = ("x", "zl")
ROWS = 32
COLUMNS = 8
MODES = 4


def shifted(value, axes, steps):
    count = math.prod(lax.axis_size(axis) for axis in axes)
    first, last = (max(0, -steps), min(count, count - steps))
    return lax.ppermute(value, axes, [(source, source + steps) for source in range(first, last)])


def piece(value, index):
    return lax.dynamic_index_in_dim(value, index, 0, keepdims=False)


def ring(value, axis, step):
    count = lax.axis_size(axis)
    return lax.ppermute(value, axis, [(i, (i + step) % count) for i in range(count)])


def pieces(value, axis):
    count, me = lax.axis_size(axis), lax.axis_index(axis)
    value = value.reshape(count, -1, N)
    return [piece(value, (me + step) % count) for step in range(1, count)] + [piece(value, me)]


def scatter_sum(parts, axis):
    arrived = [ring(part, axis, step + 1) for step, part in enumerate(parts[:-1])]
    total = parts[-1]
    for part in arrived:
        total = total + part
    return total


def after(value, *others):
    return lax.optimization_barrier((value,) + others)[0]


def gather(value, axis):
    count, me = lax.axis_size(axis), lax.axis_index(axis)
    whole = jnp.zeros((count,) + value.shape, value.dtype)
    whole = lax.dynamic_update_index_in_dim(whole, value, me, 0)
    for step in range(1, count):
        part = ring(value, axis, step)
        whole = lax.dynamic_update_index_in_dim(whole, part, (me + count - step) % count, 0)
    return whole


def exchange(value, bits):
    axes = ("zh", "zl")
    count = math.prod(lax.axis_size(axis) for axis in axes)
    return lax.ppermute(value, axes, [(i, i ^ bits) for i in range(count)])


def spread(value, order):
    value = (value + exchange(value, 1)) + (exchange(value, 2) + exchange(value, 3))
    value = value + exchange(value, 4)
    for axis in order[::-1] + ("core",):
        value = gather(value, axis).reshape(-1, N)
    return value


def moved(value, even, odd):
    pairs = []
    for row in range(ROWS):
        for column in range(COLUMNS):
            target = row + (odd if column % 2 else even)
            if column % 2:
                target %= ROWS
            if 0 <= target < ROWS:
                pairs.append((row * COLUMNS + column, target * COLUMNS + column))
    return lax.ppermute(value, POS + TILE, pairs)


def per_device(object_field, probe_modes, amplitudes, corners):
    row = lax.broadcasted_iota(jnp.int32, (N, N), 0)
    col = lax.broadcasted_iota(jnp.int32, (N, N), 1)
    odd = lax.axis_index("zl")
    is_odd = odd == 1
    first_row = (lax.axis_index(POS) == 0) & is_odd
    above = lax.ppermute(corners, POS, [(i, (i + 1) % ROWS) for i in range(ROWS)])
    yp, xp = [jnp.where(is_odd, above[0, i], corners[0, i]) for i in (0, 1)]
    yq, xq = [jnp.where(is_odd, corners[0, i], above[0, i]) for i in (0, 1)]
    amplitude = moved(amplitudes, 0, 1)
    live = jnp.where(first_row, 0, 1)
    place = jnp.stack([yp, xp, odd, live]).astype(jnp.int32)
    flip, table, phases = staged(lax.axis_index("core").astype(jnp.int32).reshape(1), probe_modes)
    mine, other = [], []
    rights = [shifted(object_field[s], TILE, -1) for s in range(2)]
    rights[0] = after(rights[0], flip)
    for s in range(2):
        mixed = jnp.where(col < xq, rights[s], object_field[s])
        mine.append(jnp.where(col < xp, rights[s], object_field[s]))
        other.append(moved(mixed, -1, 1))
        if s == 0:
            rights[1] = after(rights[1], mixed)

    def split(grads, arrived):
        kept = jnp.where(((row >= yp) != is_odd) & ~first_row, grads, 0.0)
        taken = jnp.where((row < yq) != is_odd, arrived, 0.0)
        leaving = jnp.where(col < xp, kept, 0.0) + jnp.where(col < xq, taken, 0.0)
        staying = jnp.where(col >= xp, kept, 0.0) + jnp.where(col >= xq, taken, 0.0)
        return staying, leaving

    q1, obj = first(place, mine[0], other[0], flip, table)
    grads1, back_send, back_keep = second(place, mine[1], other[1], q1, amplitude, table, phases)
    arrived1 = moved(grads1, 1, -1)
    send, part = third(0, place, back_send, obj, flip, table, None)
    got = lax.ppermute(send, "core", [(0, 1), (1, 0)])
    keep, grads0 = third(MODES // 2, place, back_keep, obj, flip, table, part)
    arrived0 = moved(grads0, 1, -1)
    across = pieces(keep + got, "x")
    staying1, leaving1 = split(grads1, after(arrived1, *across))
    received1 = shifted(leaving1, TILE, 1)
    across[-1] = after(across[-1], leaving1)
    partial = scatter_sum(across, "x")
    across = pieces(partial, "y")
    staying0, leaving0 = split(grads0, after(arrived0, *across))
    received0 = shifted(leaving0, TILE, 1)
    across[-1] = after(across[-1], leaving0)
    partial = scatter_sum(across, "y")
    partial = after(partial, received0, received1)
    object_grad = jnp.stack([staying0 + received0, staying1 + received1])
    probe_grad = spread(partial, ("x", "y")).reshape(probe_modes.shape)
    return (object_grad, probe_grad)


def solution(mesh):
    split = jax.sharding.Mesh(mesh.devices.reshape(4, 4, 2, 4, 2), POS + TILE)
    in_specs = (
        P(None, None, POS, TILE),
        P(),
        P(POS + TILE, None, None),
        P(POS + TILE, None),
    )
    out_specs = (P(None, None, POS, TILE), P())
    return jax.shard_map(
        per_device, mesh=split, in_specs=in_specs, out_specs=out_specs, check_vma=False
    )
```

```python
import functools
import math

import jax
import jax.numpy as jnp
import numpy as np
from jax import lax
from jax.experimental import pallas as pl
from jax.experimental.pallas import tpu as pltpu
from jax.sharding import PartitionSpec as P

N = 256
H = 128
F32 = jnp.float32
BF16 = jnp.bfloat16


def split_np(matrix):
    high = matrix.astype(np.float32).astype(jnp.bfloat16)
    low = (matrix - high.astype(np.float64)).astype(np.float32).astype(jnp.bfloat16)
    return high, low


def constants():
    count = np.arange(N)
    fourier = np.exp(-2j * np.pi * (np.outer(count, count) % N) / N) / math.sqrt(N)
    freq = np.where(count < H, count, count - N).astype(np.float64)
    fresnel = np.exp(-1j * np.pi * freq * freq / (2.0 * N))
    prop = (np.conj(fourier) * fresnel[None, :]) @ fourier
    straight, turned = prop[:H, :H], prop[:H, ::-1][:, :H]
    mats = []
    for part in ((straight + turned) / 2, (straight - turned) / 2):
        for side in (part, np.conj(part)):
            real, imag = side.real, side.imag
            mats.append(np.stack(split_np(np.block([[real, imag], [-imag, real]]))))
    half = np.arange(H) - 127.5
    angle = 2 * np.pi * np.outer(half, half) / N
    zero = np.zeros((H, H))
    both = np.block([[np.cos(angle) / 16, zero], [zero, np.sin(angle) / 16]])
    mats.append(np.stack(split_np(both)))
    table = np.stack(mats)
    order = np.concatenate([np.arange(H), N - 1 - np.arange(H)])
    tilt = np.exp(-2j * np.pi * 127.5 * order / N)
    phase = np.outer(tilt, tilt)
    phases = np.stack([phase.real, phase.imag]).astype(np.float32)
    return table, phases


def mirror(value):
    lanes = H - 1 - lax.broadcasted_iota(jnp.int32, (N, H), 1)
    right = jnp.take_along_axis(value[:, H:], lanes, axis=1)
    value = jnp.concatenate([value[:, :H], right], axis=1)
    rows = 7 - lax.broadcasted_iota(jnp.int32, (8, N), 0)
    tiles = [
        jnp.take_along_axis(value[N - 8 - 8 * i : N - 8 * i], rows, axis=0) for i in range(H // 8)
    ]
    return jnp.concatenate([value[:H]] + tiles, axis=0)


def parts(value):
    high = value.astype(BF16)
    return high, (value - high.astype(F32)).astype(BF16)


def dot(left, right):
    return jnp.dot(left, right, preferred_element_type=F32)


CH = 16
CHUNKS = H // CH


def fold4(tl, tr, bl, br):
    a, b = tl + bl, tr + br
    c, d = tl - bl, tr - br
    return a + b, a - b, c + d, c - d


def mul(a, b):
    return a[0] * b[0] - a[1] * b[1], a[0] * b[1] + a[1] * b[0]


def mulc(a, b):
    return a[0] * b[0] + a[1] * b[1], a[0] * b[1] - a[1] * b[0]


QUADS = ((0, 0), (0, 1), (1, 0), (1, 1))


def quad(ref, lead, row, q):
    r, c = q
    return ref[lead + (slice(r * H + row, r * H + row + CH), slice(c * H, c * H + H))]


def put(ref, lead, row, q, value):
    r, c = q
    ref[lead + (slice(r * H + row, r * H + row + CH), slice(c * H, c * H + H))] = value


def store_right_prop(op, mode, row, real, imag):
    for index, (r, c) in enumerate(QUADS):
        for part, value in ((0, real[index]), (1, imag[index])):
            high, low = parts(value)
            rows = slice(mode * N + r * H + row, mode * N + r * H + row + CH)
            op[c, rows, part * H : part * H + H] = high
            op[c, rows, N + part * H : N + part * H + H] = low


def store_right_four(op, mode, row, real, imag):
    for index, (r, c) in enumerate(QUADS):
        for part, value in ((0, real[index]), (1, imag[index])):
            high, low = parts(value)
            rows = slice(mode * N + r * H + row, mode * N + r * H + row + CH)
            op[part, rows, c * H : c * H + H] = high
            op[part, rows, N + c * H : N + c * H + H] = low


def stack_rows(table, which):
    return jnp.concatenate([table[which, 0], table[which, 0], table[which, 1]], axis=0)


def stack_cols(table, which):
    return jnp.concatenate([table[which, 0], table[which, 0], table[which, 1]], axis=1)


def three(ref_value):
    return jnp.concatenate([ref_value, ref_value[:, :N]], axis=1)


def prop_products(op, mid, out, table, conjugate, modes):
    for c in (0, 1):
        matrix = stack_rows(table, 2 * c + conjugate)
        for m in range(modes):
            rows = slice(m * N, m * N + N)
            res = dot(three(op[c, rows, :]), matrix)
            high, low = parts(res)
            for level, value in ((0, high), (1, low)):
                for r in (0, 1):
                    for p in (0, 1):
                        mid[
                            r,
                            level * N + p * H : level * N + p * H + H,
                            m * N + c * H : m * N + c * H + H,
                        ] = value[r * H : r * H + H, p * H : p * H + H]
    for r in (0, 1):
        matrix = stack_cols(table, 2 * r + 1 - conjugate)
        for m in range(modes):
            cols = slice(m * N, m * N + N)
            x = mid[r, :, cols]
            x = jnp.concatenate([x, x[:N]], axis=0)
            out[r, :, cols] = dot(matrix, x)


def four_products(op, mid, out, table, modes):
    matrix = stack_rows(table, 4)
    for p in (0, 1):
        for m in range(modes):
            rows = slice(m * N, m * N + N)
            res = dot(three(op[p, rows, :]), matrix)
            high, low = parts(res)
            mid[p, :N, m * N : m * N + N] = high
            mid[p, N:, m * N : m * N + N] = low
    matrix = stack_cols(table, 4)
    for p in (0, 1):
        for m in range(modes):
            cols = slice(m * N, m * N + N)
            x = mid[p, :, cols]
            x = jnp.concatenate([x, x[:N]], axis=0)
            out[p, :, cols] = dot(matrix, x)


def load_prop(out, mode, row):
    result = []
    for p in (0, 1):
        result.append(
            [
                out[r, p * H + row : p * H + row + CH, mode * N + c * H : mode * N + c * H + H]
                for r, c in QUADS
            ]
        )
    return result


def load_four(out, mode, row, sign):
    real, imag = [
        [
            out[p, r * H + row : r * H + row + CH, mode * N + c * H : mode * N + c * H + H]
            for r, c in QUADS
        ]
        for p in (0, 1)
    ]
    if sign > 0:
        return (
            [real[0], imag[1], imag[2], -real[3]],
            [imag[0], -real[1], -real[2], -imag[3]],
        )
    return (
        [real[0], -imag[1], -imag[2], -real[3]],
        [imag[0], real[1], real[2], -imag[3]],
    )


def unfold4(ee, eo, oe, oo):
    a, b = ee + eo, ee - eo
    c, d = oe + oo, oe - oo
    return a + c, b + d, a - c, b - d


def field(ref, lead, row, q):
    return quad(ref, lead + (0,), row, q), quad(ref, lead + (1,), row, q)


def fold_pairs(pairs):
    return fold4(*[v[0] for v in pairs]), fold4(*[v[1] for v in pairs])


def window_of(place, mine, other):
    y0, x0, odd = place[0], place[1], place[2]
    scale = place[3].astype(F32)
    rows = lax.broadcasted_iota(jnp.int32, (N, N), 0)
    upper = jnp.where(rows >= y0, 1 - odd, odd) > 0
    result = []
    for p in range(2):
        value = jnp.where(upper, mine[p] * scale, other[p])
        value = pltpu.roll(pltpu.roll(value, lax.rem(N - y0, N), 0), lax.rem(N - x0, N), 1)
        result.append(mirror(value))
    return result


def wrapped(place, value):
    return pltpu.roll(pltpu.roll(mirror(value), place[0], 0), place[1], 1)


def add_pair(total, value):
    return total[0] + value[0], total[1] + value[1]


def zeros():
    return [(jnp.zeros((CH, H), F32), jnp.zeros((CH, H), F32))] * 4


def first_kernel(place, mine, other, probes, table, q1, obj, op, mid, out):
    modes = probes.shape[0]
    obj[0], obj[1] = window_of(place, mine, other)
    for m in range(modes):
        for k in range(CHUNKS):
            row = k * CH
            pairs = [mul(field(probes, (m,), row, q), field(obj, (), row, q)) for q in QUADS]
            store_right_prop(op, m, row, *fold_pairs(pairs))
    prop_products(op, mid, out, table, 0, modes)
    for m in range(modes):
        for k in range(CHUNKS):
            row = k * CH
            real, imag = load_prop(out, m, row)
            for q, v in zip(QUADS, zip(unfold4(*real), unfold4(*imag))):
                put(q1, (m, 0), row, q, v[0])
                put(q1, (m, 1), row, q, v[1])


def second_kernel(
    place, mine, other, q1, amplitude, table, phases, grads, back_send, back_keep,
    obj, amp, op, mid, out,
):
    modes = q1.shape[0]
    obj[0], obj[1] = mul(window_of(place, mine, other), (phases[0], phases[1]))
    amp[...] = mirror(amplitude[0])
    for m in range(modes):
        for k in range(CHUNKS):
            row = k * CH
            pairs = [mul(field(q1, (m,), row, q), field(obj, (), row, q)) for q in QUADS]
            store_right_four(op, m, row, *fold_pairs(pairs))
    four_products(op, mid, out, table, modes)
    for k in range(CHUNKS):
        row = k * CH
        total = [jnp.zeros((CH, H), F32)] * 4
        for m in range(modes):
            real, imag = load_four(out, m, row, 1)
            for i, v in enumerate(zip(unfold4(*real), unfold4(*imag))):
                total[i] = total[i] + (v[0] * v[0] + v[1] * v[1])
        factor = [
            1.0 - quad(amp, (), row, q) * lax.rsqrt(total[i] + 1.0) for i, q in enumerate(QUADS)
        ]
        for m in range(modes):
            real, imag = load_four(out, m, row, 1)
            pairs = [
                (factor[i] * v[0], factor[i] * v[1])
                for i, v in enumerate(zip(unfold4(*real), unfold4(*imag)))
            ]
            store_right_four(op, m, row, *fold_pairs(pairs))
    four_products(op, mid, out, table, modes)
    for k in range(CHUNKS):
        row = k * CH
        total = zeros()
        for m in range(modes):
            real, imag = load_four(out, m, row, -1)
            pairs = []
            for i, v in enumerate(zip(unfold4(*real), unfold4(*imag))):
                q = QUADS[i]
                total[i] = add_pair(total[i], mulc(field(q1, (m,), row, q), v))
                pairs.append(mulc(field(obj, (), row, q), v))
            back = back_send if m < modes // 2 else back_keep
            store_right_prop(back, m % (modes // 2), row, *fold_pairs(pairs))
        for i, q in enumerate(QUADS):
            total[i] = mulc(field(phases, (), row, q), total[i])
        for i, q in enumerate(QUADS):
            put(grads, (0,), row, q, total[i][0])
            put(grads, (1,), row, q, total[i][1])
    for p in range(2):
        grads[p] = wrapped(place, grads[p])


def third_kernel(start, last, place, back, obj, probes, table, before, terms, grads, mid, out):
    modes = terms.shape[0]
    prop_products(back, mid, out, table, 1, modes)
    for k in range(CHUNKS):
        row = k * CH
        total = [field(before, (), row, q) for q in QUADS] if last else zeros()
        for m in range(modes):
            real, imag = load_prop(out, m, row)
            for i, v in enumerate(zip(unfold4(*real), unfold4(*imag))):
                q = QUADS[i]
                total[i] = add_pair(total[i], mulc(field(probes, (start + m,), row, q), v))
                term = mulc(field(obj, (), row, q), v)
                put(terms, (m, 0), row, q, term[0])
                put(terms, (m, 1), row, q, term[1])
        for i, q in enumerate(QUADS):
            put(grads, (0,), row, q, total[i][0])
            put(grads, (1,), row, q, total[i][1])
    for m in range(modes):
        for p in range(2):
            terms[m, p] = mirror(terms[m, p])
    if last:
        for p in range(2):
            grads[p] = wrapped(place, grads[p])


def call(kernel, args, shapes, scratch, flops, mib):
    spec = pl.BlockSpec(memory_space=pltpu.VMEM)
    return pl.pallas_call(
        kernel,
        in_specs=[pl.BlockSpec(memory_space=pltpu.SMEM)] + [spec] * (len(args) - 1),
        out_specs=[spec] * len(shapes),
        out_shape=[jax.ShapeDtypeStruct(shape, dtype) for shape, dtype in shapes],
        scratch_shapes=[pltpu.VMEM(shape, dtype) for shape, dtype in scratch],
        compiler_params=pltpu.CompilerParams(vmem_limit_bytes=mib << 20),
        cost_estimate=pl.CostEstimate(flops=flops, bytes_accessed=4 << 20, transcendentals=0),
    )(*args)


def products_scratch(modes):
    return [((2, 2 * N, modes * N), BF16), ((2, N, modes * N), F32)]


def operand(modes):
    return ((2, modes * N, 2 * N), BF16)


def first(place, mine, other, probes, table):
    modes = probes.shape[0]
    return call(
        first_kernel,
        (place, mine, other, probes, table),
        [(probes.shape, F32), ((2, N, N), F32)],
        [operand(modes)] + products_scratch(modes),
        3 << 30,
        20,
    )


def second(place, mine, other, q1, amplitude, table, phases):
    modes = q1.shape[0]
    return call(
        second_kernel,
        (place, mine, other, q1, amplitude, table, phases),
        [((2, N, N), F32), operand(modes // 2), operand(modes // 2)],
        [((2, N, N), F32), ((N, N), F32), operand(modes)] + products_scratch(modes),
        6 << 30,
        24,
    )


def third(start, place, back, obj, probes, table, before):
    modes = probes.shape[0] // 2
    last = before is not None
    return call(
        functools.partial(third_kernel, start, last),
        (place, back, obj, probes, table, before if last else place[None]),
        [((modes, 2, N, N), F32), ((2, N, N), F32)],
        products_scratch(modes),
        2 << 30,
        14,
    )


def stage_kernel(core, source, table, phases, target, table_out, phases_out):
    target[0] = mirror(source[0])

    @pl.when(pl.program_id(0) == 0)
    def _():
        table_out[...] = table[...]
        phases_out[...] = phases[...]


def staged(core, probes):
    table, phases = (jnp.asarray(v) for v in constants())
    images = probes.reshape(-1, N, N)
    count = images.shape[0]
    half = count // 2
    whole = lambda value: pl.BlockSpec(value.shape, lambda i, core: (0,) * value.ndim)
    flip, table, phases = pl.pallas_call(
        stage_kernel,
        grid_spec=pltpu.PrefetchScalarGridSpec(
            num_scalar_prefetch=1,
            grid=(count,),
            in_specs=[
                pl.BlockSpec((1, N, N), lambda i, core: ((i + half * (1 - core[0])) % count, 0, 0)),
                whole(table),
                whole(phases),
            ],
            out_specs=[
                pl.BlockSpec((1, N, N), lambda i, core: (i, 0, 0)),
                whole(table),
                whole(phases),
            ],
        ),
        out_shape=[
            jax.ShapeDtypeStruct(images.shape, F32),
            jax.ShapeDtypeStruct(table.shape, table.dtype),
            jax.ShapeDtypeStruct(phases.shape, phases.dtype),
        ],
    )(core, images, table, phases)
    return flip.reshape(probes.shape), table, phases


POS = ("y", "zh", "core")
TILE = ("x", "zl")
ROWS = 32
COLUMNS = 8
MODES = 4


def shifted(value, axes, steps):
    count = math.prod(lax.axis_size(axis) for axis in axes)
    first, last = (max(0, -steps), min(count, count - steps))
    return lax.ppermute(value, axes, [(source, source + steps) for source in range(first, last)])


def piece(value, index):
    return lax.dynamic_index_in_dim(value, index, 0, keepdims=False)


def ring(value, axis, step):
    count = lax.axis_size(axis)
    return lax.ppermute(value, axis, [(i, (i + step) % count) for i in range(count)])


def pieces(value, axis):
    count, me = lax.axis_size(axis), lax.axis_index(axis)
    value = value.reshape(count, -1, N)
    return [piece(value, (me + step) % count) for step in range(1, count)] + [piece(value, me)]


def scatter_sum(parts, axis):
    arrived = [ring(part, axis, step + 1) for step, part in enumerate(parts[:-1])]
    total = parts[-1]
    for part in arrived:
        total = total + part
    return total


def after(value, *others):
    return lax.optimization_barrier((value,) + others)[0]


def gather(value, axis, *beside):
    count, me = lax.axis_size(axis), lax.axis_index(axis)
    whole = jnp.zeros((count,) + value.shape, value.dtype)
    whole = after(lax.dynamic_update_index_in_dim(whole, value, me, 0), *beside)
    for step in range(1, count):
        part = ring(value, axis, step)
        whole = lax.dynamic_update_index_in_dim(whole, part, (me + count - step) % count, 0)
    return whole


def exchange(value, bits):
    axes = ("zh", "zl")
    count = math.prod(lax.axis_size(axis) for axis in axes)
    return lax.ppermute(value, axes, [(i, i ^ bits) for i in range(count)])


def summed_over_z(value):
    value = (value + exchange(value, 1)) + (exchange(value, 2) + exchange(value, 3))
    return value + exchange(value, 4)


def place_kernel(index, source, *refs):
    target, semaphore = refs[-2:]
    copy = pltpu.make_async_copy(source, target.at[index[0]], semaphore)
    copy.start()
    copy.wait()


def placed(index, value, whole):
    anywhere = pl.BlockSpec(memory_space=pl.ANY)
    return pl.pallas_call(
        place_kernel,
        in_specs=[pl.BlockSpec(memory_space=pltpu.SMEM)] + [anywhere] * (1 if whole is None else 2),
        out_specs=anywhere,
        out_shape=jax.ShapeDtypeStruct((2,) + value.shape, value.dtype),
        scratch_shapes=[pltpu.SemaphoreType.DMA],
        input_output_aliases={} if whole is None else {2: 0},
    )(index, value, *([] if whole is None else [whole]))


def moved(value, even, odd):
    pairs = []
    for row in range(ROWS):
        for column in range(COLUMNS):
            target = row + (odd if column % 2 else even)
            if column % 2:
                target %= ROWS
            if 0 <= target < ROWS:
                pairs.append((row * COLUMNS + column, target * COLUMNS + column))
    return lax.ppermute(value, POS + TILE, pairs)


def per_device(object_field, probe_modes, amplitudes, corners):
    row = lax.broadcasted_iota(jnp.int32, (N, N), 0)
    col = lax.broadcasted_iota(jnp.int32, (N, N), 1)
    odd = lax.axis_index("zl")
    is_odd = odd == 1
    first_row = (lax.axis_index(POS) == 0) & is_odd
    above = lax.ppermute(corners, POS, [(i, (i + 1) % ROWS) for i in range(ROWS)])
    yp, xp = [jnp.where(is_odd, above[0, i], corners[0, i]) for i in (0, 1)]
    yq, xq = [jnp.where(is_odd, corners[0, i], above[0, i]) for i in (0, 1)]
    amplitude = moved(amplitudes, 0, 1)
    live = jnp.where(first_row, 0, 1)
    place = jnp.stack([yp, xp, odd, live]).astype(jnp.int32)
    flip, table, phases = staged(lax.axis_index("core").astype(jnp.int32).reshape(1), probe_modes)
    mine, other = [], []
    right = after(shifted(object_field, TILE, -1), flip)
    for s in range(2):
        mixed = jnp.where(col < xq, right[s], object_field[s])
        mine.append(jnp.where(col < xp, right[s], object_field[s]))
        other.append(moved(mixed, -1, 1))
        right = after(right, mixed)

    def split(grads, arrived):
        kept = jnp.where(((row >= yp) != is_odd) & ~first_row, grads, 0.0)
        taken = jnp.where((row < yq) != is_odd, arrived, 0.0)
        leaving = jnp.where(col < xp, kept, 0.0) + jnp.where(col < xq, taken, 0.0)
        staying = jnp.where(col >= xp, kept, 0.0) + jnp.where(col >= xq, taken, 0.0)
        return staying, leaving

    q1, obj = first(place, mine[0], other[0], flip, table)
    grads1, back_send, back_keep = second(place, mine[1], other[1], q1, amplitude, table, phases)
    arrived1 = moved(grads1, 1, -1)
    send, part = third(0, place, back_send, obj, flip, table, None)
    got = lax.ppermute(send, "core", [(0, 1), (1, 0)])
    keep, grads0 = third(MODES // 2, place, back_keep, obj, flip, table, part)
    arrived0 = moved(grads0, 1, -1)
    across = pieces(keep + got, "x")
    staying1, leaving1 = split(grads1, after(arrived1, *across))
    received1 = shifted(leaving1, TILE, 1)
    across[-1] = after(across[-1], leaving1)
    partial = scatter_sum(across, "x")
    across = pieces(partial, "y")
    staying0, leaving0 = split(grads0, after(arrived0, *across))
    received0 = shifted(leaving0, TILE, 1)
    across[-1] = after(across[-1], leaving0)
    partial = scatter_sum(across, "y")
    partial = after(partial, received0, received1)
    object_grad = jnp.stack([staying0 + received0, staying1 + received1])
    total = gather(summed_over_z(partial), "y").reshape(-1, N)
    total = gather(total, "x", object_grad).reshape(-1, N)
    core = lax.axis_index("core").astype(jnp.int32).reshape(1)
    whole = placed(core, total, None)
    opposite = lax.ppermute(total, "core", [(0, 1), (1, 0)])
    probe_grad = placed(1 - core, opposite, whole).reshape(probe_modes.shape)
    return (object_grad, probe_grad)


def solution(mesh):
    split = jax.sharding.Mesh(mesh.devices.reshape(4, 4, 2, 4, 2), POS + TILE)
    in_specs = (
        P(None, None, POS, TILE),
        P(),
        P(POS + TILE, None, None),
        P(POS + TILE, None),
    )
    out_specs = (P(None, None, POS, TILE), P())
    return jax.shard_map(
        per_device, mesh=split, in_specs=in_specs, out_specs=out_specs, check_vma=False
    )
```

```python
import functools
import math

import jax
import jax.numpy as jnp
import numpy as np
from jax import lax
from jax.experimental import pallas as pl
from jax.experimental.pallas import tpu as pltpu
from jax.sharding import PartitionSpec as P

N = 256
H = 128
F32 = jnp.float32
BF16 = jnp.bfloat16


def split_np(matrix):
    high = matrix.astype(np.float32).astype(jnp.bfloat16)
    low = (matrix - high.astype(np.float64)).astype(np.float32).astype(jnp.bfloat16)
    return high, low


def constants():
    count = np.arange(N)
    fourier = np.exp(-2j * np.pi * (np.outer(count, count) % N) / N) / math.sqrt(N)
    freq = np.where(count < H, count, count - N).astype(np.float64)
    fresnel = np.exp(-1j * np.pi * freq * freq / (2.0 * N))
    prop = (np.conj(fourier) * fresnel[None, :]) @ fourier
    straight, turned = prop[:H, :H], prop[:H, ::-1][:, :H]
    mats = []
    for part in ((straight + turned) / 2, (straight - turned) / 2):
        for side in (part, np.conj(part)):
            real, imag = side.real, side.imag
            mats.append(np.stack(split_np(np.block([[real, imag], [-imag, real]]))))
    half = np.arange(H) - 127.5
    angle = 2 * np.pi * np.outer(half, half) / N
    zero = np.zeros((H, H))
    both = np.block([[np.cos(angle) / 16, zero], [zero, np.sin(angle) / 16]])
    mats.append(np.stack(split_np(both)))
    table = np.stack(mats)
    order = np.concatenate([np.arange(H), N - 1 - np.arange(H)])
    tilt = np.exp(-2j * np.pi * 127.5 * order / N)
    phase = np.outer(tilt, tilt)
    phases = np.stack([phase.real, phase.imag]).astype(np.float32)
    return table, phases


def mirror(value):
    lanes = H - 1 - lax.broadcasted_iota(jnp.int32, (N, H), 1)
    right = jnp.take_along_axis(value[:, H:], lanes, axis=1)
    value = jnp.concatenate([value[:, :H], right], axis=1)
    rows = 7 - lax.broadcasted_iota(jnp.int32, (8, N), 0)
    tiles = [
        jnp.take_along_axis(value[N - 8 - 8 * i : N - 8 * i], rows, axis=0) for i in range(H // 8)
    ]
    return jnp.concatenate([value[:H]] + tiles, axis=0)


def parts(value):
    high = value.astype(BF16)
    return high, (value - high.astype(F32)).astype(BF16)


def dot(left, right):
    return jnp.dot(left, right, preferred_element_type=F32)


CH = 16
CHUNKS = H // CH


def fold4(tl, tr, bl, br):
    a, b = tl + bl, tr + br
    c, d = tl - bl, tr - br
    return a + b, a - b, c + d, c - d


def mul(a, b):
    return a[0] * b[0] - a[1] * b[1], a[0] * b[1] + a[1] * b[0]


def mulc(a, b):
    return a[0] * b[0] + a[1] * b[1], a[0] * b[1] - a[1] * b[0]


QUADS = ((0, 0), (0, 1), (1, 0), (1, 1))


def quad(ref, lead, row, q):
    r, c = q
    return ref[lead + (slice(r * H + row, r * H + row + CH), slice(c * H, c * H + H))]


def put(ref, lead, row, q, value):
    r, c = q
    ref[lead + (slice(r * H + row, r * H + row + CH), slice(c * H, c * H + H))] = value


def store_right_prop(op, mode, row, real, imag):
    for index, (r, c) in enumerate(QUADS):
        for part, value in ((0, real[index]), (1, imag[index])):
            high, low = parts(value)
            rows = slice(mode * N + r * H + row, mode * N + r * H + row + CH)
            op[c, rows, part * H : part * H + H] = high
            op[c, rows, N + part * H : N + part * H + H] = low


def store_right_four(op, mode, row, real, imag):
    for index, (r, c) in enumerate(QUADS):
        for part, value in ((0, real[index]), (1, imag[index])):
            high, low = parts(value)
            rows = slice(mode * N + r * H + row, mode * N + r * H + row + CH)
            op[part, rows, c * H : c * H + H] = high
            op[part, rows, N + c * H : N + c * H + H] = low


def stack_rows(table, which):
    return jnp.concatenate([table[which, 0], table[which, 0], table[which, 1]], axis=0)


def stack_cols(table, which):
    return jnp.concatenate([table[which, 0], table[which, 0], table[which, 1]], axis=1)


def three(ref_value):
    return jnp.concatenate([ref_value, ref_value[:, :N]], axis=1)


def prop_products(op, mid, out, table, conjugate, modes):
    for c in (0, 1):
        matrix = stack_rows(table, 2 * c + conjugate)
        for m in range(modes):
            rows = slice(m * N, m * N + N)
            res = dot(three(op[c, rows, :]), matrix)
            high, low = parts(res)
            for level, value in ((0, high), (1, low)):
                for r in (0, 1):
                    for p in (0, 1):
                        mid[
                            r,
                            level * N + p * H : level * N + p * H + H,
                            m * N + c * H : m * N + c * H + H,
                        ] = value[r * H : r * H + H, p * H : p * H + H]
    for r in (0, 1):
        matrix = stack_cols(table, 2 * r + 1 - conjugate)
        for m in range(modes):
            cols = slice(m * N, m * N + N)
            x = mid[r, :, cols]
            x = jnp.concatenate([x, x[:N]], axis=0)
            out[r, :, cols] = dot(matrix, x)


def four_products(op, mid, out, table, modes):
    matrix = stack_rows(table, 4)
    for p in (0, 1):
        for m in range(modes):
            rows = slice(m * N, m * N + N)
            res = dot(three(op[p, rows, :]), matrix)
            high, low = parts(res)
            mid[p, :N, m * N : m * N + N] = high
            mid[p, N:, m * N : m * N + N] = low
    matrix = stack_cols(table, 4)
    for p in (0, 1):
        for m in range(modes):
            cols = slice(m * N, m * N + N)
            x = mid[p, :, cols]
            x = jnp.concatenate([x, x[:N]], axis=0)
            out[p, :, cols] = dot(matrix, x)


def load_prop(out, mode, row):
    result = []
    for p in (0, 1):
        result.append(
            [
                out[r, p * H + row : p * H + row + CH, mode * N + c * H : mode * N + c * H + H]
                for r, c in QUADS
            ]
        )
    return result


def load_four(out, mode, row, sign):
    real, imag = [
        [
            out[p, r * H + row : r * H + row + CH, mode * N + c * H : mode * N + c * H + H]
            for r, c in QUADS
        ]
        for p in (0, 1)
    ]
    if sign > 0:
        return (
            [real[0], imag[1], imag[2], -real[3]],
            [imag[0], -real[1], -real[2], -imag[3]],
        )
    return (
        [real[0], -imag[1], -imag[2], -real[3]],
        [imag[0], real[1], real[2], -imag[3]],
    )


def unfold4(ee, eo, oe, oo):
    a, b = ee + eo, ee - eo
    c, d = oe + oo, oe - oo
    return a + c, b + d, a - c, b - d


def field(ref, lead, row, q):
    return quad(ref, lead + (0,), row, q), quad(ref, lead + (1,), row, q)


def fold_pairs(pairs):
    return fold4(*[v[0] for v in pairs]), fold4(*[v[1] for v in pairs])


def window_of(place, mine, other):
    y0, x0, odd = place[0], place[1], place[2]
    scale = place[3].astype(F32)
    rows = lax.broadcasted_iota(jnp.int32, (N, N), 0)
    upper = jnp.where(rows >= y0, 1 - odd, odd) > 0
    result = []
    for p in range(2):
        value = jnp.where(upper, mine[p] * scale, other[p])
        value = pltpu.roll(pltpu.roll(value, lax.rem(N - y0, N), 0), lax.rem(N - x0, N), 1)
        result.append(mirror(value))
    return result


def wrapped(place, value):
    return pltpu.roll(pltpu.roll(mirror(value), place[0], 0), place[1], 1)


def add_pair(total, value):
    return total[0] + value[0], total[1] + value[1]


def zeros():
    return [(jnp.zeros((CH, H), F32), jnp.zeros((CH, H), F32))] * 4


def first_kernel(place, mine, other, probes, table, q1, obj, op, mid, out):
    modes = probes.shape[0]
    obj[0], obj[1] = window_of(place, mine, other)
    for m in range(modes):
        for k in range(CHUNKS):
            row = k * CH
            pairs = [mul(field(probes, (m,), row, q), field(obj, (), row, q)) for q in QUADS]
            store_right_prop(op, m, row, *fold_pairs(pairs))
    prop_products(op, mid, out, table, 0, modes)
    for m in range(modes):
        for k in range(CHUNKS):
            row = k * CH
            real, imag = load_prop(out, m, row)
            for q, v in zip(QUADS, zip(unfold4(*real), unfold4(*imag))):
                put(q1, (m, 0), row, q, v[0])
                put(q1, (m, 1), row, q, v[1])


def second_kernel(
    place, mine, other, q1, amplitude, table, phases, probes, first_obj,
    grads1, grads0, send, keep,
    obj, amp, op, mid, out,
):
    modes = q1.shape[0]
    obj[0], obj[1] = mul(window_of(place, mine, other), (phases[0], phases[1]))
    amp[...] = mirror(amplitude[0])
    for m in range(modes):
        for k in range(CHUNKS):
            row = k * CH
            pairs = [mul(field(q1, (m,), row, q), field(obj, (), row, q)) for q in QUADS]
            store_right_four(op, m, row, *fold_pairs(pairs))
    four_products(op, mid, out, table, modes)
    for k in range(CHUNKS):
        row = k * CH
        total = [jnp.zeros((CH, H), F32)] * 4
        for m in range(modes):
            real, imag = load_four(out, m, row, 1)
            for i, v in enumerate(zip(unfold4(*real), unfold4(*imag))):
                total[i] = total[i] + (v[0] * v[0] + v[1] * v[1])
        factor = [
            1.0 - quad(amp, (), row, q) * lax.rsqrt(total[i] + 1.0) for i, q in enumerate(QUADS)
        ]
        for m in range(modes):
            real, imag = load_four(out, m, row, 1)
            pairs = [
                (factor[i] * v[0], factor[i] * v[1])
                for i, v in enumerate(zip(unfold4(*real), unfold4(*imag)))
            ]
            store_right_four(op, m, row, *fold_pairs(pairs))
    four_products(op, mid, out, table, modes)
    for k in range(CHUNKS):
        row = k * CH
        total = zeros()
        for m in range(modes):
            real, imag = load_four(out, m, row, -1)
            pairs = []
            for i, v in enumerate(zip(unfold4(*real), unfold4(*imag))):
                q = QUADS[i]
                total[i] = add_pair(total[i], mulc(field(q1, (m,), row, q), v))
                pairs.append(mulc(field(obj, (), row, q), v))
            store_right_prop(op, m, row, *fold_pairs(pairs))
        for i, q in enumerate(QUADS):
            total[i] = mulc(field(phases, (), row, q), total[i])
        for i, q in enumerate(QUADS):
            put(grads1, (0,), row, q, total[i][0])
            put(grads1, (1,), row, q, total[i][1])
    prop_products(op, mid, out, table, 1, modes)
    half = modes // 2
    for k in range(CHUNKS):
        row = k * CH
        total = zeros()
        for m in range(modes):
            real, imag = load_prop(out, m, row)
            terms = send if m < half else keep
            for i, v in enumerate(zip(unfold4(*real), unfold4(*imag))):
                q = QUADS[i]
                total[i] = add_pair(total[i], mulc(field(probes, (m,), row, q), v))
                term = mulc(field(first_obj, (), row, q), v)
                put(terms, (m % half, 0), row, q, term[0])
                put(terms, (m % half, 1), row, q, term[1])
        for i, q in enumerate(QUADS):
            put(grads0, (0,), row, q, total[i][0])
            put(grads0, (1,), row, q, total[i][1])
    for terms in (send, keep):
        for m in range(half):
            for p in range(2):
                terms[m, p] = mirror(terms[m, p])
    for p in range(2):
        grads1[p] = wrapped(place, grads1[p])
        grads0[p] = wrapped(place, grads0[p])


def call(kernel, args, shapes, scratch, flops, mib):
    spec = pl.BlockSpec(memory_space=pltpu.VMEM)
    return pl.pallas_call(
        kernel,
        in_specs=[pl.BlockSpec(memory_space=pltpu.SMEM)] + [spec] * (len(args) - 1),
        out_specs=[spec] * len(shapes),
        out_shape=[jax.ShapeDtypeStruct(shape, dtype) for shape, dtype in shapes],
        scratch_shapes=[pltpu.VMEM(shape, dtype) for shape, dtype in scratch],
        compiler_params=pltpu.CompilerParams(vmem_limit_bytes=mib << 20),
        cost_estimate=pl.CostEstimate(flops=flops, bytes_accessed=4 << 20, transcendentals=0),
    )(*args)


def products_scratch(modes):
    return [((2, 2 * N, modes * N), BF16), ((2, N, modes * N), F32)]


def operand(modes):
    return ((2, modes * N, 2 * N), BF16)


def first(place, mine, other, probes, table):
    modes = probes.shape[0]
    return call(
        first_kernel,
        (place, mine, other, probes, table),
        [(probes.shape, F32), ((2, N, N), F32)],
        [operand(modes)] + products_scratch(modes),
        3 << 30,
        20,
    )


def second(place, mine, other, q1, amplitude, table, phases, probes, first_obj):
    modes = q1.shape[0]
    field_shape, terms_shape = ((2, N, N), F32), ((modes // 2, 2, N, N), F32)
    return call(
        second_kernel,
        (place, mine, other, q1, amplitude, table, phases, probes, first_obj),
        [field_shape, field_shape, terms_shape, terms_shape],
        [field_shape, ((N, N), F32), operand(modes)] + products_scratch(modes),
        9 << 30,
        26,
    )


def stage_kernel(core, source, table, phases, target, table_out, phases_out):
    target[0] = mirror(source[0])

    @pl.when(pl.program_id(0) == 0)
    def _():
        table_out[...] = table[...]
        phases_out[...] = phases[...]


def staged(core, probes):
    table, phases = (jnp.asarray(v) for v in constants())
    images = probes.reshape(-1, N, N)
    count = images.shape[0]
    half = count // 2
    whole = lambda value: pl.BlockSpec(value.shape, lambda i, core: (0,) * value.ndim)
    flip, table, phases = pl.pallas_call(
        stage_kernel,
        grid_spec=pltpu.PrefetchScalarGridSpec(
            num_scalar_prefetch=1,
            grid=(count,),
            in_specs=[
                pl.BlockSpec((1, N, N), lambda i, core: ((i + half * (1 - core[0])) % count, 0, 0)),
                whole(table),
                whole(phases),
            ],
            out_specs=[
                pl.BlockSpec((1, N, N), lambda i, core: (i, 0, 0)),
                whole(table),
                whole(phases),
            ],
        ),
        out_shape=[
            jax.ShapeDtypeStruct(images.shape, F32),
            jax.ShapeDtypeStruct(table.shape, table.dtype),
            jax.ShapeDtypeStruct(phases.shape, phases.dtype),
        ],
    )(core, images, table, phases)
    return flip.reshape(probes.shape), table, phases


POS = ("y", "zh", "core")
TILE = ("x", "zl")
ROWS = 32
COLUMNS = 8
MODES = 4


def shifted(value, axes, steps):
    count = math.prod(lax.axis_size(axis) for axis in axes)
    first, last = (max(0, -steps), min(count, count - steps))
    return lax.ppermute(value, axes, [(source, source + steps) for source in range(first, last)])


def piece(value, index):
    return lax.dynamic_index_in_dim(value, index, 0, keepdims=False)


def ring(value, axis, step):
    count = lax.axis_size(axis)
    return lax.ppermute(value, axis, [(i, (i + step) % count) for i in range(count)])


def pieces(value, axis):
    count, me = lax.axis_size(axis), lax.axis_index(axis)
    value = value.reshape(count, -1, N)
    return [piece(value, (me + step) % count) for step in range(1, count)] + [piece(value, me)]


def scatter_sum(parts, axis):
    arrived = [ring(part, axis, step + 1) for step, part in enumerate(parts[:-1])]
    total = parts[-1]
    for part in arrived:
        total = total + part
    return total


def after(value, *others):
    return lax.optimization_barrier((value,) + others)[0]


def gather(value, axis, *beside):
    count, me = lax.axis_size(axis), lax.axis_index(axis)
    whole = jnp.zeros((count,) + value.shape, value.dtype)
    whole = after(lax.dynamic_update_index_in_dim(whole, value, me, 0), *beside)
    for step in range(1, count):
        part = ring(value, axis, step)
        whole = lax.dynamic_update_index_in_dim(whole, part, (me + count - step) % count, 0)
    return whole


def exchange(value, bits):
    axes = ("zh", "zl")
    count = math.prod(lax.axis_size(axis) for axis in axes)
    return lax.ppermute(value, axes, [(i, i ^ bits) for i in range(count)])


def summed_over_z(value):
    value = (value + exchange(value, 1)) + (exchange(value, 2) + exchange(value, 3))
    return value + exchange(value, 4)


def place_kernel(index, source, *refs):
    target, semaphore = refs[-2:]
    copy = pltpu.make_async_copy(source, target.at[index[0]], semaphore)
    copy.start()
    copy.wait()


def placed(index, value, whole):
    anywhere = pl.BlockSpec(memory_space=pl.ANY)
    return pl.pallas_call(
        place_kernel,
        in_specs=[pl.BlockSpec(memory_space=pltpu.SMEM), pl.BlockSpec(memory_space=pltpu.VMEM)]
        + [anywhere] * (0 if whole is None else 1),
        out_specs=anywhere,
        out_shape=jax.ShapeDtypeStruct((2,) + value.shape, value.dtype),
        scratch_shapes=[pltpu.SemaphoreType.DMA],
        input_output_aliases={} if whole is None else {2: 0},
    )(index, value, *([] if whole is None else [whole]))


def moved(value, even, odd):
    pairs = []
    for row in range(ROWS):
        for column in range(COLUMNS):
            target = row + (odd if column % 2 else even)
            if column % 2:
                target %= ROWS
            if 0 <= target < ROWS:
                pairs.append((row * COLUMNS + column, target * COLUMNS + column))
    return lax.ppermute(value, POS + TILE, pairs)


def per_device(object_field, probe_modes, amplitudes, corners):
    row = lax.broadcasted_iota(jnp.int32, (N, N), 0)
    col = lax.broadcasted_iota(jnp.int32, (N, N), 1)
    odd = lax.axis_index("zl")
    is_odd = odd == 1
    first_row = (lax.axis_index(POS) == 0) & is_odd
    above = lax.ppermute(corners, POS, [(i, (i + 1) % ROWS) for i in range(ROWS)])
    yp, xp = [jnp.where(is_odd, above[0, i], corners[0, i]) for i in (0, 1)]
    yq, xq = [jnp.where(is_odd, corners[0, i], above[0, i]) for i in (0, 1)]
    live = jnp.where(first_row, 0, 1)
    place = jnp.stack([yp, xp, odd, live]).astype(jnp.int32)
    flip, table, phases = staged(lax.axis_index("core").astype(jnp.int32).reshape(1), probe_modes)
    right = after(shifted(after(object_field, above), TILE, -1), flip)
    mixed = jnp.where(col < xq, right, object_field)
    mine = jnp.where(col < xp, right, object_field)
    other = [moved(mixed[s], -1, 1) for s in range(2)]

    def split(grads, arrived):
        kept = jnp.where(((row >= yp) != is_odd) & ~first_row, grads, 0.0)
        taken = jnp.where((row < yq) != is_odd, arrived, 0.0)
        leaving = jnp.where(col < xp, kept, 0.0) + jnp.where(col < xq, taken, 0.0)
        staying = jnp.where(col >= xp, kept, 0.0) + jnp.where(col >= xq, taken, 0.0)
        return staying, leaving

    amplitude = moved(after(amplitudes, mixed), 0, 1)
    q1, obj = first(place, mine[0], other[0], flip, table)
    grads1, grads0, send, keep = second(
        place, mine[1], other[1], q1, amplitude, table, phases, flip, obj
    )
    swap = [(0, 1), (1, 0)]
    arrived1 = moved(grads1, 1, -1)
    across = pieces(keep + lax.ppermute(send, "core", swap), "y")
    staying1, leaving1 = split(grads1, after(arrived1, *across))
    received1 = shifted(leaving1, TILE, 1)
    across[-1] = after(across[-1], leaving1)
    partial = after(scatter_sum(across, "y"), received1)
    total = summed_over_z(scatter_sum(pieces(partial, "x"), "x"))
    grads0 = after(grads0, total)
    arrived0 = moved(grads0, 1, -1)
    total = gather(total, "x").reshape(-1, N)
    staying0, leaving0 = split(grads0, arrived0)
    received0 = shifted(after(leaving0, total), TILE, 1)
    total = after(gather(total, "y", leaving0).reshape(-1, N), received0)
    core = lax.axis_index("core").astype(jnp.int32).reshape(1)
    whole = placed(core, total, None)
    probe_grad = placed(1 - core, lax.ppermute(total, "core", swap), whole)
    probe_grad = probe_grad.reshape(probe_modes.shape)
    object_grad = jnp.stack([staying0 + received0, staying1 + received1])
    return (object_grad, probe_grad)


def solution(mesh):
    split = jax.sharding.Mesh(mesh.devices.reshape(4, 4, 2, 4, 2), POS + TILE)
    in_specs = (
        P(None, None, POS, TILE),
        P(),
        P(POS + TILE, None, None),
        P(POS + TILE, None),
    )
    out_specs = (P(None, None, POS, TILE), P())
    return jax.shard_map(
        per_device, mesh=split, in_specs=in_specs, out_specs=out_specs, check_vma=False
    )
```

```python
import functools
import math

import jax
import jax.numpy as jnp
import numpy as np
from jax import lax
from jax.experimental import pallas as pl
from jax.experimental.pallas import tpu as pltpu
from jax.sharding import PartitionSpec as P

N = 256
H = 128
F32 = jnp.float32
BF16 = jnp.bfloat16


def split_np(matrix):
    high = matrix.astype(np.float32).astype(jnp.bfloat16)
    low = (matrix - high.astype(np.float64)).astype(np.float32).astype(jnp.bfloat16)
    return high, low


def constants():
    count = np.arange(N)
    fourier = np.exp(-2j * np.pi * (np.outer(count, count) % N) / N) / math.sqrt(N)
    freq = np.where(count < H, count, count - N).astype(np.float64)
    fresnel = np.exp(-1j * np.pi * freq * freq / (2.0 * N))
    prop = (np.conj(fourier) * fresnel[None, :]) @ fourier
    straight, turned = prop[:H, :H], prop[:H, ::-1][:, :H]
    mats = []
    for part in ((straight + turned) / 2, (straight - turned) / 2):
        for side in (part, np.conj(part)):
            real, imag = side.real, side.imag
            mats.append(np.stack(split_np(np.block([[real, imag], [-imag, real]]))))
    half = np.arange(H) - 127.5
    angle = 2 * np.pi * np.outer(half, half) / N
    zero = np.zeros((H, H))
    both = np.block([[np.cos(angle) / 16, zero], [zero, np.sin(angle) / 16]])
    mats.append(np.stack(split_np(both)))
    table = np.stack(mats)
    order = np.concatenate([np.arange(H), N - 1 - np.arange(H)])
    tilt = np.exp(-2j * np.pi * 127.5 * order / N)
    phase = np.outer(tilt, tilt)
    phases = np.stack([phase.real, phase.imag]).astype(np.float32)
    return table, phases


def mirror(value):
    lanes = H - 1 - lax.broadcasted_iota(jnp.int32, (N, H), 1)
    right = jnp.take_along_axis(value[:, H:], lanes, axis=1)
    value = jnp.concatenate([value[:, :H], right], axis=1)
    rows = 7 - lax.broadcasted_iota(jnp.int32, (8, N), 0)
    tiles = [
        jnp.take_along_axis(value[N - 8 - 8 * i : N - 8 * i], rows, axis=0) for i in range(H // 8)
    ]
    return jnp.concatenate([value[:H]] + tiles, axis=0)


def parts(value):
    high = value.astype(BF16)
    return high, (value - high.astype(F32)).astype(BF16)


def dot(left, right):
    return jnp.dot(left, right, preferred_element_type=F32)


CH = 16
CHUNKS = H // CH


def fold4(tl, tr, bl, br):
    a, b = tl + bl, tr + br
    c, d = tl - bl, tr - br
    return a + b, a - b, c + d, c - d


def mul(a, b):
    return a[0] * b[0] - a[1] * b[1], a[0] * b[1] + a[1] * b[0]


def mulc(a, b):
    return a[0] * b[0] + a[1] * b[1], a[0] * b[1] - a[1] * b[0]


QUADS = ((0, 0), (0, 1), (1, 0), (1, 1))


def quad(ref, lead, row, q):
    r, c = q
    return ref[lead + (slice(r * H + row, r * H + row + CH), slice(c * H, c * H + H))]


def put(ref, lead, row, q, value):
    r, c = q
    ref[lead + (slice(r * H + row, r * H + row + CH), slice(c * H, c * H + H))] = value


def store_right_prop(op, mode, row, real, imag):
    for index, (r, c) in enumerate(QUADS):
        for part, value in ((0, real[index]), (1, imag[index])):
            high, low = parts(value)
            rows = slice(mode * N + r * H + row, mode * N + r * H + row + CH)
            op[c, rows, part * H : part * H + H] = high
            op[c, rows, N + part * H : N + part * H + H] = low


def store_right_four(op, mode, row, real, imag):
    for index, (r, c) in enumerate(QUADS):
        for part, value in ((0, real[index]), (1, imag[index])):
            high, low = parts(value)
            rows = slice(mode * N + r * H + row, mode * N + r * H + row + CH)
            op[part, rows, c * H : c * H + H] = high
            op[part, rows, N + c * H : N + c * H + H] = low


def stack_rows(table, which):
    return jnp.concatenate([table[which, 0], table[which, 0], table[which, 1]], axis=0)


def stack_cols(table, which):
    return jnp.concatenate([table[which, 0], table[which, 0], table[which, 1]], axis=1)


def three(ref_value):
    return jnp.concatenate([ref_value, ref_value[:, :N]], axis=1)


def prop_products(op, mid, out, table, conjugate, modes):
    for c in (0, 1):
        matrix = stack_rows(table, 2 * c + conjugate)
        for m in range(modes):
            rows = slice(m * N, m * N + N)
            res = dot(three(op[c, rows, :]), matrix)
            high, low = parts(res)
            for level, value in ((0, high), (1, low)):
                for r in (0, 1):
                    for p in (0, 1):
                        mid[
                            r,
                            level * N + p * H : level * N + p * H + H,
                            m * N + c * H : m * N + c * H + H,
                        ] = value[r * H : r * H + H, p * H : p * H + H]
    for r in (0, 1):
        matrix = stack_cols(table, 2 * r + 1 - conjugate)
        for m in range(modes):
            cols = slice(m * N, m * N + N)
            x = mid[r, :, cols]
            x = jnp.concatenate([x, x[:N]], axis=0)
            out[r, :, cols] = dot(matrix, x)


def four_products(op, mid, out, table, modes):
    matrix = stack_rows(table, 4)
    for p in (0, 1):
        for m in range(modes):
            rows = slice(m * N, m * N + N)
            res = dot(three(op[p, rows, :]), matrix)
            high, low = parts(res)
            mid[p, :N, m * N : m * N + N] = high
            mid[p, N:, m * N : m * N + N] = low
    matrix = stack_cols(table, 4)
    for p in (0, 1):
        for m in range(modes):
            cols = slice(m * N, m * N + N)
            x = mid[p, :, cols]
            x = jnp.concatenate([x, x[:N]], axis=0)
            out[p, :, cols] = dot(matrix, x)


def load_prop(out, mode, row):
    result = []
    for p in (0, 1):
        result.append(
            [
                out[r, p * H + row : p * H + row + CH, mode * N + c * H : mode * N + c * H + H]
                for r, c in QUADS
            ]
        )
    return result


def load_four(out, mode, row, sign):
    real, imag = [
        [
            out[p, r * H + row : r * H + row + CH, mode * N + c * H : mode * N + c * H + H]
            for r, c in QUADS
        ]
        for p in (0, 1)
    ]
    if sign > 0:
        return (
            [real[0], imag[1], imag[2], -real[3]],
            [imag[0], -real[1], -real[2], -imag[3]],
        )
    return (
        [real[0], -imag[1], -imag[2], -real[3]],
        [imag[0], real[1], real[2], -imag[3]],
    )


def unfold4(ee, eo, oe, oo):
    a, b = ee + eo, ee - eo
    c, d = oe + oo, oe - oo
    return a + c, b + d, a - c, b - d


def field(ref, lead, row, q):
    return quad(ref, lead + (0,), row, q), quad(ref, lead + (1,), row, q)


def fold_pairs(pairs):
    return fold4(*[v[0] for v in pairs]), fold4(*[v[1] for v in pairs])


def window_of(place, mine, other):
    y0, x0, odd = place[0], place[1], place[2]
    scale = place[3].astype(F32)
    rows = lax.broadcasted_iota(jnp.int32, (N, N), 0)
    upper = jnp.where(rows >= y0, 1 - odd, odd) > 0
    result = []
    for p in range(2):
        value = jnp.where(upper, mine[p] * scale, other[p])
        value = pltpu.roll(pltpu.roll(value, lax.rem(N - y0, N), 0), lax.rem(N - x0, N), 1)
        result.append(mirror(value))
    return result


def wrapped(place, value):
    return pltpu.roll(pltpu.roll(mirror(value), place[0], 0), place[1], 1)


def add_pair(total, value):
    return total[0] + value[0], total[1] + value[1]


def zeros():
    return [(jnp.zeros((CH, H), F32), jnp.zeros((CH, H), F32))] * 4


def first_kernel(place, mine, other, probes, table, q1, obj, op, mid, out):
    modes = probes.shape[0]
    obj[0], obj[1] = window_of(place, mine, other)
    for m in range(modes):
        for k in range(CHUNKS):
            row = k * CH
            pairs = [mul(field(probes, (m,), row, q), field(obj, (), row, q)) for q in QUADS]
            store_right_prop(op, m, row, *fold_pairs(pairs))
    prop_products(op, mid, out, table, 0, modes)
    for m in range(modes):
        for k in range(CHUNKS):
            row = k * CH
            real, imag = load_prop(out, m, row)
            for q, v in zip(QUADS, zip(unfold4(*real), unfold4(*imag))):
                put(q1, (m, 0), row, q, v[0])
                put(q1, (m, 1), row, q, v[1])


def second_kernel(
    place, mine, other, q1, amplitude, table, phases, probes, first_obj,
    grads, send, keep,
    obj, amp, op, mid, out,
):
    modes = q1.shape[0]
    obj[0], obj[1] = mul(window_of(place, mine, other), (phases[0], phases[1]))
    amp[...] = mirror(amplitude[0])
    for m in range(modes):
        for k in range(CHUNKS):
            row = k * CH
            pairs = [mul(field(q1, (m,), row, q), field(obj, (), row, q)) for q in QUADS]
            store_right_four(op, m, row, *fold_pairs(pairs))
    four_products(op, mid, out, table, modes)
    for k in range(CHUNKS):
        row = k * CH
        total = [jnp.zeros((CH, H), F32)] * 4
        for m in range(modes):
            real, imag = load_four(out, m, row, 1)
            for i, v in enumerate(zip(unfold4(*real), unfold4(*imag))):
                total[i] = total[i] + (v[0] * v[0] + v[1] * v[1])
        factor = [
            1.0 - quad(amp, (), row, q) * lax.rsqrt(total[i] + 1.0) for i, q in enumerate(QUADS)
        ]
        for m in range(modes):
            real, imag = load_four(out, m, row, 1)
            pairs = [
                (factor[i] * v[0], factor[i] * v[1])
                for i, v in enumerate(zip(unfold4(*real), unfold4(*imag)))
            ]
            store_right_four(op, m, row, *fold_pairs(pairs))
    four_products(op, mid, out, table, modes)
    for k in range(CHUNKS):
        row = k * CH
        total = zeros()
        for m in range(modes):
            real, imag = load_four(out, m, row, -1)
            pairs = []
            for i, v in enumerate(zip(unfold4(*real), unfold4(*imag))):
                q = QUADS[i]
                total[i] = add_pair(total[i], mulc(field(q1, (m,), row, q), v))
                pairs.append(mulc(field(obj, (), row, q), v))
            store_right_prop(op, m, row, *fold_pairs(pairs))
        for i, q in enumerate(QUADS):
            total[i] = mulc(field(phases, (), row, q), total[i])
        for i, q in enumerate(QUADS):
            put(grads, (1, 0), row, q, total[i][0])
            put(grads, (1, 1), row, q, total[i][1])
    prop_products(op, mid, out, table, 1, modes)
    half = modes // 2
    for k in range(CHUNKS):
        row = k * CH
        total = zeros()
        for m in range(modes):
            real, imag = load_prop(out, m, row)
            terms = send if m < half else keep
            for i, v in enumerate(zip(unfold4(*real), unfold4(*imag))):
                q = QUADS[i]
                total[i] = add_pair(total[i], mulc(field(probes, (m,), row, q), v))
                term = mulc(field(first_obj, (), row, q), v)
                put(terms, (m % half, 0), row, q, term[0])
                put(terms, (m % half, 1), row, q, term[1])
        for i, q in enumerate(QUADS):
            put(grads, (0, 0), row, q, total[i][0])
            put(grads, (0, 1), row, q, total[i][1])
    for terms in (send, keep):
        for m in range(half):
            for p in range(2):
                terms[m, p] = mirror(terms[m, p])
    for s in range(2):
        for p in range(2):
            grads[s, p] = wrapped(place, grads[s, p])


def call(kernel, args, shapes, scratch, flops, mib):
    spec = pl.BlockSpec(memory_space=pltpu.VMEM)
    return pl.pallas_call(
        kernel,
        in_specs=[pl.BlockSpec(memory_space=pltpu.SMEM)] + [spec] * (len(args) - 1),
        out_specs=[spec] * len(shapes),
        out_shape=[jax.ShapeDtypeStruct(shape, dtype) for shape, dtype in shapes],
        scratch_shapes=[pltpu.VMEM(shape, dtype) for shape, dtype in scratch],
        compiler_params=pltpu.CompilerParams(vmem_limit_bytes=mib << 20),
        cost_estimate=pl.CostEstimate(flops=flops, bytes_accessed=4 << 20, transcendentals=0),
    )(*args)


def products_scratch(modes):
    return [((2, 2 * N, modes * N), BF16), ((2, N, modes * N), F32)]


def operand(modes):
    return ((2, modes * N, 2 * N), BF16)


def first(place, mine, other, probes, table):
    modes = probes.shape[0]
    return call(
        first_kernel,
        (place, mine, other, probes, table),
        [(probes.shape, F32), ((2, N, N), F32)],
        [operand(modes)] + products_scratch(modes),
        3 << 30,
        20,
    )


def second(place, mine, other, q1, amplitude, table, phases, probes, first_obj):
    modes = q1.shape[0]
    field_shape, terms_shape = ((2, N, N), F32), ((modes // 2, 2, N, N), F32)
    return call(
        second_kernel,
        (place, mine, other, q1, amplitude, table, phases, probes, first_obj),
        [((2, 2, N, N), F32), terms_shape, terms_shape],
        [field_shape, ((N, N), F32), operand(modes)] + products_scratch(modes),
        9 << 30,
        26,
    )


def stage_kernel(core, source, table, phases, target, table_out, phases_out):
    target[0] = mirror(source[0])

    @pl.when(pl.program_id(0) == 0)
    def _():
        table_out[...] = table[...]
        phases_out[...] = phases[...]


def staged(core, probes):
    table, phases = (jnp.asarray(v) for v in constants())
    images = probes.reshape(-1, N, N)
    count = images.shape[0]
    half = count // 2
    whole = lambda value: pl.BlockSpec(value.shape, lambda i, core: (0,) * value.ndim)
    flip, table, phases = pl.pallas_call(
        stage_kernel,
        grid_spec=pltpu.PrefetchScalarGridSpec(
            num_scalar_prefetch=1,
            grid=(count,),
            in_specs=[
                pl.BlockSpec((1, N, N), lambda i, core: ((i + half * (1 - core[0])) % count, 0, 0)),
                whole(table),
                whole(phases),
            ],
            out_specs=[
                pl.BlockSpec((1, N, N), lambda i, core: (i, 0, 0)),
                whole(table),
                whole(phases),
            ],
        ),
        out_shape=[
            jax.ShapeDtypeStruct(images.shape, F32),
            jax.ShapeDtypeStruct(table.shape, table.dtype),
            jax.ShapeDtypeStruct(phases.shape, phases.dtype),
        ],
    )(core, images, table, phases)
    return flip.reshape(probes.shape), table, phases


POS = ("y", "zh", "core")
TILE = ("x", "zl")
ROWS = 32
COLUMNS = 8
MODES = 4


def shifted(value, axes, steps):
    count = math.prod(lax.axis_size(axis) for axis in axes)
    first, last = (max(0, -steps), min(count, count - steps))
    return lax.ppermute(value, axes, [(source, source + steps) for source in range(first, last)])


def piece(value, index):
    return lax.dynamic_index_in_dim(value, index, 0, keepdims=False)


def ring(value, axis, step):
    count = lax.axis_size(axis)
    return lax.ppermute(value, axis, [(i, (i + step) % count) for i in range(count)])


def pieces(value, axis):
    count, me = lax.axis_size(axis), lax.axis_index(axis)
    value = value.reshape(count, -1, N)
    return [piece(value, (me + step) % count) for step in range(1, count)] + [piece(value, me)]


def scatter_sum(parts, axis):
    arrived = [ring(part, axis, step + 1) for step, part in enumerate(parts[:-1])]
    total = parts[-1]
    for part in arrived:
        total = total + part
    return total


def after(value, *others):
    return lax.optimization_barrier((value,) + others)[0]


def gather(value, axis, *beside):
    count, me = lax.axis_size(axis), lax.axis_index(axis)
    whole = jnp.zeros((count,) + value.shape, value.dtype)
    whole = after(lax.dynamic_update_index_in_dim(whole, value, me, 0), *beside)
    for step in range(1, count):
        part = ring(value, axis, step)
        whole = lax.dynamic_update_index_in_dim(whole, part, (me + count - step) % count, 0)
    return whole.reshape(-1, N)


def exchange(value, bits):
    axes = ("zh", "zl")
    count = math.prod(lax.axis_size(axis) for axis in axes)
    return lax.ppermute(value, axes, [(i, i ^ bits) for i in range(count)])


def summed_over_z(value):
    value = (value + exchange(value, 1)) + (exchange(value, 2) + exchange(value, 3))
    return value + exchange(value, 4)


COPIES = 8


def place_kernel(index, source, *refs):
    target, semaphores = refs[-2:]
    rows = source.shape[0] // COPIES
    copies = [
        pltpu.make_async_copy(
            source.at[pl.ds(i * rows, rows)],
            target.at[index[0], pl.ds(i * rows, rows)],
            semaphores.at[i],
        )
        for i in range(COPIES)
    ]
    for copy in copies:
        copy.start()
    for copy in copies:
        copy.wait()


def placed(index, value, whole):
    anywhere = pl.BlockSpec(memory_space=pl.ANY)
    return pl.pallas_call(
        place_kernel,
        in_specs=[pl.BlockSpec(memory_space=pltpu.SMEM), pl.BlockSpec(memory_space=pltpu.VMEM)]
        + [anywhere] * (0 if whole is None else 1),
        out_specs=anywhere,
        out_shape=jax.ShapeDtypeStruct((2,) + value.shape, value.dtype),
        scratch_shapes=[pltpu.SemaphoreType.DMA((COPIES,))],
        input_output_aliases={} if whole is None else {2: 0},
    )(index, value, *([] if whole is None else [whole]))


def moved(value, even, odd):
    pairs = []
    for row in range(ROWS):
        for column in range(COLUMNS):
            target = row + (odd if column % 2 else even)
            if column % 2:
                target %= ROWS
            if 0 <= target < ROWS:
                pairs.append((row * COLUMNS + column, target * COLUMNS + column))
    return lax.ppermute(value, POS + TILE, pairs)


def per_device(object_field, probe_modes, amplitudes, corners):
    row = lax.broadcasted_iota(jnp.int32, (N, N), 0)
    col = lax.broadcasted_iota(jnp.int32, (N, N), 1)
    odd = lax.axis_index("zl")
    is_odd = odd == 1
    first_row = (lax.axis_index(POS) == 0) & is_odd
    above = lax.ppermute(corners, POS, [(i, (i + 1) % ROWS) for i in range(ROWS)])
    yp, xp = [jnp.where(is_odd, above[0, i], corners[0, i]) for i in (0, 1)]
    yq, xq = [jnp.where(is_odd, corners[0, i], above[0, i]) for i in (0, 1)]
    live = jnp.where(first_row, 0, 1)
    place = jnp.stack([yp, xp, odd, live]).astype(jnp.int32)
    flip, table, phases = staged(lax.axis_index("core").astype(jnp.int32).reshape(1), probe_modes)
    right = after(shifted(after(object_field, above), TILE, -1), flip)
    mine, mixed = [
        [jnp.where(col < x, right[s], object_field[s]) for s in range(2)] for x in (xp, xq)
    ]
    other = [moved(mixed[s], -1, 1) for s in range(2)]

    def split(grads, arrived):
        kept = jnp.where(((row >= yp) != is_odd) & ~first_row, grads, 0.0)
        taken = jnp.where((row < yq) != is_odd, arrived, 0.0)
        leaving = jnp.where(col < xp, kept, 0.0) + jnp.where(col < xq, taken, 0.0)
        staying = jnp.where(col >= xp, kept, 0.0) + jnp.where(col >= xq, taken, 0.0)
        return staying, leaving

    amplitude = moved(after(amplitudes, *mixed), 0, 1)
    q1, obj = first(place, mine[0], other[0], flip, table)
    grads, send, keep = second(
        place, mine[1], other[1], q1, amplitude, table, phases, flip, obj
    )
    swap = [(0, 1), (1, 0)]
    arrived = moved(grads, 1, -1)
    across = pieces(keep + lax.ppermute(send, "core", swap), "y")
    across = pieces(after(scatter_sum(across, "y"), arrived), "x")
    staying, leaving = split(grads, arrived)
    across[-1] = after(across[-1], leaving)
    total = summed_over_z(scatter_sum(across, "x"))
    total = gather(total, "x")
    received = shifted(after(leaving, total), TILE, 1)
    total = gather(total, "y", received)
    object_grad = staying + received
    total = after(total, object_grad)
    core = lax.axis_index("core").astype(jnp.int32).reshape(1)
    whole = placed(core, total, None)
    probe_grad = placed(1 - core, lax.ppermute(total, "core", swap), whole)
    probe_grad = probe_grad.reshape(probe_modes.shape)
    return (object_grad, probe_grad)


def solution(mesh):
    split = jax.sharding.Mesh(mesh.devices.reshape(4, 4, 2, 4, 2), POS + TILE)
    in_specs = (
        P(None, None, POS, TILE),
        P(),
        P(POS + TILE, None, None),
        P(POS + TILE, None),
    )
    out_specs = (P(None, None, POS, TILE), P())
    return jax.shard_map(
        per_device, mesh=split, in_specs=in_specs, out_specs=out_specs, check_vma=False
    )
```

```python
import functools
import math

import jax
import jax.numpy as jnp
import numpy as np
from jax import lax
from jax.experimental import pallas as pl
from jax.experimental.pallas import tpu as pltpu
from jax.sharding import PartitionSpec as P

N = 256
H = 128
F32 = jnp.float32
BF16 = jnp.bfloat16


def split_np(matrix):
    high = matrix.astype(np.float32).astype(jnp.bfloat16)
    low = (matrix - high.astype(np.float64)).astype(np.float32).astype(jnp.bfloat16)
    return high, low


def constants():
    count = np.arange(N)
    fourier = np.exp(-2j * np.pi * (np.outer(count, count) % N) / N) / math.sqrt(N)
    freq = np.where(count < H, count, count - N).astype(np.float64)
    fresnel = np.exp(-1j * np.pi * freq * freq / (2.0 * N))
    prop = (np.conj(fourier) * fresnel[None, :]) @ fourier
    straight, turned = prop[:H, :H], prop[:H, ::-1][:, :H]
    mats = []
    for part in ((straight + turned) / 2, (straight - turned) / 2):
        for side in (part, np.conj(part)):
            real, imag = side.real, side.imag
            mats.append(np.stack(split_np(np.block([[real, imag], [-imag, real]]))))
    half = np.arange(H) - 127.5
    angle = 2 * np.pi * np.outer(half, half) / N
    zero = np.zeros((H, H))
    both = np.block([[np.cos(angle) / 16, zero], [zero, np.sin(angle) / 16]])
    mats.append(np.stack(split_np(both)))
    table = np.stack(mats)
    order = np.concatenate([np.arange(H), N - 1 - np.arange(H)])
    tilt = np.exp(-2j * np.pi * 127.5 * order / N)
    phase = np.outer(tilt, tilt)
    phases = np.stack([phase.real, phase.imag]).astype(np.float32)
    return table, phases


def mirror(value):
    lanes = H - 1 - lax.broadcasted_iota(jnp.int32, (N, H), 1)
    right = jnp.take_along_axis(value[:, H:], lanes, axis=1)
    value = jnp.concatenate([value[:, :H], right], axis=1)
    rows = 7 - lax.broadcasted_iota(jnp.int32, (8, N), 0)
    tiles = [
        jnp.take_along_axis(value[N - 8 - 8 * i : N - 8 * i], rows, axis=0) for i in range(H // 8)
    ]
    return jnp.concatenate([value[:H]] + tiles, axis=0)


def parts(value):
    high = value.astype(BF16)
    return high, (value - high.astype(F32)).astype(BF16)


def dot(left, right):
    return jnp.dot(left, right, preferred_element_type=F32)


CH = 16
CHUNKS = H // CH


def fold4(tl, tr, bl, br):
    a, b = tl + bl, tr + br
    c, d = tl - bl, tr - br
    return a + b, a - b, c + d, c - d


def mul(a, b):
    return a[0] * b[0] - a[1] * b[1], a[0] * b[1] + a[1] * b[0]


def mulc(a, b):
    return a[0] * b[0] + a[1] * b[1], a[0] * b[1] - a[1] * b[0]


QUADS = ((0, 0), (0, 1), (1, 0), (1, 1))


def quad(ref, lead, row, q):
    r, c = q
    return ref[lead + (slice(r * H + row, r * H + row + CH), slice(c * H, c * H + H))]


def put(ref, lead, row, q, value):
    r, c = q
    ref[lead + (slice(r * H + row, r * H + row + CH), slice(c * H, c * H + H))] = value


def store_right_prop(op, mode, row, real, imag):
    for index, (r, c) in enumerate(QUADS):
        for part, value in ((0, real[index]), (1, imag[index])):
            high, low = parts(value)
            rows = slice(mode * N + r * H + row, mode * N + r * H + row + CH)
            op[c, rows, part * H : part * H + H] = high
            op[c, rows, N + part * H : N + part * H + H] = low


def store_right_four(op, mode, row, real, imag):
    for index, (r, c) in enumerate(QUADS):
        for part, value in ((0, real[index]), (1, imag[index])):
            high, low = parts(value)
            rows = slice(mode * N + r * H + row, mode * N + r * H + row + CH)
            op[part, rows, c * H : c * H + H] = high
            op[part, rows, N + c * H : N + c * H + H] = low


def stack_rows(table, which):
    return jnp.concatenate([table[which, 0], table[which, 0], table[which, 1]], axis=0)


def stack_cols(table, which):
    return jnp.concatenate([table[which, 0], table[which, 0], table[which, 1]], axis=1)


def three(ref_value):
    return jnp.concatenate([ref_value, ref_value[:, :N]], axis=1)


def prop_products(op, mid, out, table, conjugate, modes):
    for c in (0, 1):
        matrix = stack_rows(table, 2 * c + conjugate)
        for m in range(modes):
            rows = slice(m * N, m * N + N)
            res = dot(three(op[c, rows, :]), matrix)
            high, low = parts(res)
            for level, value in ((0, high), (1, low)):
                for r in (0, 1):
                    for p in (0, 1):
                        mid[
                            r,
                            level * N + p * H : level * N + p * H + H,
                            m * N + c * H : m * N + c * H + H,
                        ] = value[r * H : r * H + H, p * H : p * H + H]
    for r in (0, 1):
        matrix = stack_cols(table, 2 * r + 1 - conjugate)
        for m in range(modes):
            cols = slice(m * N, m * N + N)
            x = mid[r, :, cols]
            x = jnp.concatenate([x, x[:N]], axis=0)
            out[r, :, cols] = dot(matrix, x)


def four_products(op, mid, out, table, modes):
    matrix = stack_rows(table, 4)
    for p in (0, 1):
        for m in range(modes):
            rows = slice(m * N, m * N + N)
            res = dot(three(op[p, rows, :]), matrix)
            high, low = parts(res)
            mid[p, :N, m * N : m * N + N] = high
            mid[p, N:, m * N : m * N + N] = low
    matrix = stack_cols(table, 4)
    for p in (0, 1):
        for m in range(modes):
            cols = slice(m * N, m * N + N)
            x = mid[p, :, cols]
            x = jnp.concatenate([x, x[:N]], axis=0)
            out[p, :, cols] = dot(matrix, x)


def load_prop(out, mode, row):
    result = []
    for p in (0, 1):
        result.append(
            [
                out[r, p * H + row : p * H + row + CH, mode * N + c * H : mode * N + c * H + H]
                for r, c in QUADS
            ]
        )
    return result


def load_four(out, mode, row, sign):
    real, imag = [
        [
            out[p, r * H + row : r * H + row + CH, mode * N + c * H : mode * N + c * H + H]
            for r, c in QUADS
        ]
        for p in (0, 1)
    ]
    if sign > 0:
        return (
            [real[0], imag[1], imag[2], -real[3]],
            [imag[0], -real[1], -real[2], -imag[3]],
        )
    return (
        [real[0], -imag[1], -imag[2], -real[3]],
        [imag[0], real[1], real[2], -imag[3]],
    )


def unfold4(ee, eo, oe, oo):
    a, b = ee + eo, ee - eo
    c, d = oe + oo, oe - oo
    return a + c, b + d, a - c, b - d


def field(ref, lead, row, q):
    return quad(ref, lead + (0,), row, q), quad(ref, lead + (1,), row, q)


def fold_pairs(pairs):
    return fold4(*[v[0] for v in pairs]), fold4(*[v[1] for v in pairs])


def window_of(place, mine, other):
    y0, x0, odd = place[0], place[1], place[2]
    scale = place[3].astype(F32)
    rows = lax.broadcasted_iota(jnp.int32, (N, N), 0)
    upper = jnp.where(rows >= y0, 1 - odd, odd) > 0
    result = []
    for p in range(2):
        value = jnp.where(upper, mine[p] * scale, other[p])
        value = pltpu.roll(pltpu.roll(value, lax.rem(N - y0, N), 0), lax.rem(N - x0, N), 1)
        result.append(mirror(value))
    return result


def wrapped(place, value):
    return pltpu.roll(pltpu.roll(mirror(value), place[0], 0), place[1], 1)


def add_pair(total, value):
    return total[0] + value[0], total[1] + value[1]


def zeros():
    return [(jnp.zeros((CH, H), F32), jnp.zeros((CH, H), F32))] * 4


def first_kernel(place, mine, other, probes, table, q1, obj, op, mid, out):
    modes = probes.shape[0]
    obj[0], obj[1] = window_of(place, mine, other)
    for m in range(modes):
        for k in range(CHUNKS):
            row = k * CH
            pairs = [mul(field(probes, (m,), row, q), field(obj, (), row, q)) for q in QUADS]
            store_right_prop(op, m, row, *fold_pairs(pairs))
    prop_products(op, mid, out, table, 0, modes)
    for m in range(modes):
        for k in range(CHUNKS):
            row = k * CH
            real, imag = load_prop(out, m, row)
            for q, v in zip(QUADS, zip(unfold4(*real), unfold4(*imag))):
                put(q1, (m, 0), row, q, v[0])
                put(q1, (m, 1), row, q, v[1])


def second_kernel(
    place, mine, other, q1, amplitude, table, phases, probes, first_obj,
    grads1, grads0, send, keep,
    obj, amp, op, mid, out,
):
    modes = q1.shape[0]
    obj[0], obj[1] = mul(window_of(place, mine, other), (phases[0], phases[1]))
    amp[...] = mirror(amplitude[0])
    for m in range(modes):
        for k in range(CHUNKS):
            row = k * CH
            pairs = [mul(field(q1, (m,), row, q), field(obj, (), row, q)) for q in QUADS]
            store_right_four(op, m, row, *fold_pairs(pairs))
    four_products(op, mid, out, table, modes)
    for k in range(CHUNKS):
        row = k * CH
        total = [jnp.zeros((CH, H), F32)] * 4
        for m in range(modes):
            real, imag = load_four(out, m, row, 1)
            for i, v in enumerate(zip(unfold4(*real), unfold4(*imag))):
                total[i] = total[i] + (v[0] * v[0] + v[1] * v[1])
        factor = [
            1.0 - quad(amp, (), row, q) * lax.rsqrt(total[i] + 1.0) for i, q in enumerate(QUADS)
        ]
        for m in range(modes):
            real, imag = load_four(out, m, row, 1)
            pairs = [
                (factor[i] * v[0], factor[i] * v[1])
                for i, v in enumerate(zip(unfold4(*real), unfold4(*imag)))
            ]
            store_right_four(op, m, row, *fold_pairs(pairs))
    four_products(op, mid, out, table, modes)
    for k in range(CHUNKS):
        row = k * CH
        total = zeros()
        for m in range(modes):
            real, imag = load_four(out, m, row, -1)
            pairs = []
            for i, v in enumerate(zip(unfold4(*real), unfold4(*imag))):
                q = QUADS[i]
                total[i] = add_pair(total[i], mulc(field(q1, (m,), row, q), v))
                pairs.append(mulc(field(obj, (), row, q), v))
            store_right_prop(op, m, row, *fold_pairs(pairs))
        for i, q in enumerate(QUADS):
            total[i] = mulc(field(phases, (), row, q), total[i])
        for i, q in enumerate(QUADS):
            put(grads1, (0,), row, q, total[i][0])
            put(grads1, (1,), row, q, total[i][1])
    prop_products(op, mid, out, table, 1, modes)
    half = modes // 2
    for k in range(CHUNKS):
        row = k * CH
        total = zeros()
        for m in range(modes):
            real, imag = load_prop(out, m, row)
            terms = send if m < half else keep
            for i, v in enumerate(zip(unfold4(*real), unfold4(*imag))):
                q = QUADS[i]
                total[i] = add_pair(total[i], mulc(field(probes, (m,), row, q), v))
                term = mulc(field(first_obj, (), row, q), v)
                put(terms, (m % half, 0), row, q, term[0])
                put(terms, (m % half, 1), row, q, term[1])
        for i, q in enumerate(QUADS):
            put(grads0, (0,), row, q, total[i][0])
            put(grads0, (1,), row, q, total[i][1])
    for terms in (send, keep):
        for m in range(half):
            for p in range(2):
                terms[m, p] = mirror(terms[m, p])
    for p in range(2):
        grads1[p] = wrapped(place, grads1[p])
        grads0[p] = wrapped(place, grads0[p])


def call(kernel, args, shapes, scratch, flops, mib):
    spec = pl.BlockSpec(memory_space=pltpu.VMEM)
    return pl.pallas_call(
        kernel,
        in_specs=[pl.BlockSpec(memory_space=pltpu.SMEM)] + [spec] * (len(args) - 1),
        out_specs=[spec] * len(shapes),
        out_shape=[jax.ShapeDtypeStruct(shape, dtype) for shape, dtype in shapes],
        scratch_shapes=[pltpu.VMEM(shape, dtype) for shape, dtype in scratch],
        compiler_params=pltpu.CompilerParams(vmem_limit_bytes=mib << 20),
        cost_estimate=pl.CostEstimate(flops=flops, bytes_accessed=4 << 20, transcendentals=0),
    )(*args)


def products_scratch(modes):
    return [((2, 2 * N, modes * N), BF16), ((2, N, modes * N), F32)]


def operand(modes):
    return ((2, modes * N, 2 * N), BF16)


def first(place, mine, other, probes, table):
    modes = probes.shape[0]
    return call(
        first_kernel,
        (place, mine, other, probes, table),
        [(probes.shape, F32), ((2, N, N), F32)],
        [operand(modes)] + products_scratch(modes),
        3 << 30,
        20,
    )


def second(place, mine, other, q1, amplitude, table, phases, probes, first_obj):
    modes = q1.shape[0]
    field_shape, terms_shape = ((2, N, N), F32), ((modes // 2, 2, N, N), F32)
    return call(
        second_kernel,
        (place, mine, other, q1, amplitude, table, phases, probes, first_obj),
        [field_shape, field_shape, terms_shape, terms_shape],
        [field_shape, ((N, N), F32), operand(modes)] + products_scratch(modes),
        9 << 30,
        26,
    )


def stage_kernel(core, source, table, phases, target, table_out, phases_out):
    target[0] = mirror(source[0])

    @pl.when(pl.program_id(0) == 0)
    def _():
        table_out[...] = table[...]
        phases_out[...] = phases[...]


def staged(core, probes):
    table, phases = (jnp.asarray(v) for v in constants())
    images = probes.reshape(-1, N, N)
    count = images.shape[0]
    half = count // 2
    whole = lambda value: pl.BlockSpec(value.shape, lambda i, core: (0,) * value.ndim)
    flip, table, phases = pl.pallas_call(
        stage_kernel,
        grid_spec=pltpu.PrefetchScalarGridSpec(
            num_scalar_prefetch=1,
            grid=(count,),
            in_specs=[
                pl.BlockSpec((1, N, N), lambda i, core: ((i + half * (1 - core[0])) % count, 0, 0)),
                whole(table),
                whole(phases),
            ],
            out_specs=[
                pl.BlockSpec((1, N, N), lambda i, core: (i, 0, 0)),
                whole(table),
                whole(phases),
            ],
        ),
        out_shape=[
            jax.ShapeDtypeStruct(images.shape, F32),
            jax.ShapeDtypeStruct(table.shape, table.dtype),
            jax.ShapeDtypeStruct(phases.shape, phases.dtype),
        ],
    )(core, images, table, phases)
    return flip.reshape(probes.shape), table, phases


POS = ("y", "zh", "core")
TILE = ("x", "zl")
ROWS = 32
COLUMNS = 8
MODES = 4


def shifted(value, axes, steps):
    count = math.prod(lax.axis_size(axis) for axis in axes)
    first, last = (max(0, -steps), min(count, count - steps))
    return lax.ppermute(value, axes, [(source, source + steps) for source in range(first, last)])


def piece(value, index):
    return lax.dynamic_index_in_dim(value, index, 0, keepdims=False)


def ring(value, axis, step):
    count = lax.axis_size(axis)
    return lax.ppermute(value, axis, [(i, (i + step) % count) for i in range(count)])


def pieces(value, axis):
    count, me = lax.axis_size(axis), lax.axis_index(axis)
    value = value.reshape(count, -1, N)
    return [piece(value, (me + step) % count) for step in range(1, count)] + [piece(value, me)]


def scatter_sum(parts, axis):
    arrived = [ring(part, axis, step + 1) for step, part in enumerate(parts[:-1])]
    total = parts[-1]
    for part in arrived:
        total = total + part
    return total


def after(value, *others):
    return lax.optimization_barrier((value,) + others)[0]


def collected(value, travelled, axis, *beside):
    count, me = lax.axis_size(axis), lax.axis_index(axis)
    whole = jnp.zeros((count,) + value.shape, value.dtype)
    whole = after(lax.dynamic_update_index_in_dim(whole, value, me, 0), *beside)
    for step, part in enumerate(travelled):
        whole = lax.dynamic_update_index_in_dim(whole, part, (me + step + 1) % count, 0)
    return whole.reshape(-1, N)


def gather(value, axis, *beside):
    steps = range(1, lax.axis_size(axis))
    return collected(value, [ring(value, axis, -step) for step in steps], axis, *beside)


def circular_gather(value, axis):
    travelled = [ring(value, axis, -1)]
    for _ in range(2, lax.axis_size(axis)):
        travelled.append(ring(travelled[-1], axis, -1))
    return collected(value, travelled, axis)


def exchange(value, bits):
    axes = ("zh", "zl")
    count = math.prod(lax.axis_size(axis) for axis in axes)
    return lax.ppermute(value, axes, [(i, i ^ bits) for i in range(count)])


def summed_over_z(value):
    value = (value + exchange(value, 1)) + (exchange(value, 2) + exchange(value, 3))
    return value + exchange(value, 4)


def moved(value, even, odd):
    pairs = []
    for row in range(ROWS):
        for column in range(COLUMNS):
            target = row + (odd if column % 2 else even)
            if column % 2:
                target %= ROWS
            if 0 <= target < ROWS:
                pairs.append((row * COLUMNS + column, target * COLUMNS + column))
    return lax.ppermute(value, POS + TILE, pairs)


def per_device(object_field, probe_modes, amplitudes, corners):
    row = lax.broadcasted_iota(jnp.int32, (N, N), 0)
    col = lax.broadcasted_iota(jnp.int32, (N, N), 1)
    odd = lax.axis_index("zl")
    is_odd = odd == 1
    first_row = (lax.axis_index(POS) == 0) & is_odd
    above = lax.ppermute(corners, POS, [(i, (i + 1) % ROWS) for i in range(ROWS)])
    yp, xp = [jnp.where(is_odd, above[0, i], corners[0, i]) for i in (0, 1)]
    yq, xq = [jnp.where(is_odd, corners[0, i], above[0, i]) for i in (0, 1)]
    live = jnp.where(first_row, 0, 1)
    place = jnp.stack([yp, xp, odd, live]).astype(jnp.int32)
    flip, table, phases = staged(lax.axis_index("core").astype(jnp.int32).reshape(1), probe_modes)
    right = after(shifted(after(object_field, above), TILE, -1), flip)
    mine, mixed = [
        [jnp.where(col < x, right[s], object_field[s]) for s in range(2)] for x in (xp, xq)
    ]
    other = [moved(mixed[s], -1, 1) for s in range(2)]

    def split(grads, arrived):
        kept = jnp.where(((row >= yp) != is_odd) & ~first_row, grads, 0.0)
        taken = jnp.where((row < yq) != is_odd, arrived, 0.0)
        leaving = jnp.where(col < xp, kept, 0.0) + jnp.where(col < xq, taken, 0.0)
        staying = jnp.where(col >= xp, kept, 0.0) + jnp.where(col >= xq, taken, 0.0)
        return staying, leaving

    amplitude = moved(after(amplitudes, *mixed), 0, 1)
    q1, obj = first(place, mine[0], other[0], flip, table)
    grads1, grads0, send, keep = second(
        place, mine[1], other[1], q1, amplitude, table, phases, flip, obj
    )
    swap = [(0, 1), (1, 0)]
    arrived1 = moved(grads1, 1, -1)
    across = pieces(keep + lax.ppermute(send, "core", swap), "y")
    staying1, leaving1 = split(grads1, after(arrived1, *across))
    received1 = shifted(leaving1, TILE, 1)
    across[-1] = after(across[-1], leaving1)
    across = pieces(after(scatter_sum(across, "y"), received1), "x")
    arrived0 = moved(after(grads0, received1), 1, -1)
    partial = scatter_sum(across, "x")
    staying0, leaving0 = split(grads0, arrived0)
    total = summed_over_z(after(partial, leaving0))
    received0 = shifted(after(leaving0, total), TILE, 1)
    total = circular_gather(total, "x")
    object_grad = jnp.stack([staying0 + received0, staying1 + received1])
    total = gather(total, "y", object_grad)
    opposite = lax.ppermute(total, "core", swap)
    half = lax.broadcasted_iota(jnp.int32, (2, 1, 1), 0)
    probe_grad = jnp.where(half == lax.axis_index("core"), total, opposite)
    probe_grad = probe_grad.reshape(probe_modes.shape)
    return (object_grad, probe_grad)


def solution(mesh):
    split = jax.sharding.Mesh(mesh.devices.reshape(4, 4, 2, 4, 2), POS + TILE)
    in_specs = (
        P(None, None, POS, TILE),
        P(),
        P(POS + TILE, None, None),
        P(POS + TILE, None),
    )
    out_specs = (P(None, None, POS, TILE), P())
    return jax.shard_map(
        per_device, mesh=split, in_specs=in_specs, out_specs=out_specs, check_vma=False
    )
```

```python
import functools
import math

import jax
import jax.numpy as jnp
import numpy as np
from jax import lax
from jax.experimental import pallas as pl
from jax.experimental.pallas import tpu as pltpu
from jax.sharding import PartitionSpec as P

N = 256
H = 128
F32 = jnp.float32
BF16 = jnp.bfloat16


def split_np(matrix):
    high = matrix.astype(np.float32).astype(jnp.bfloat16)
    low = (matrix - high.astype(np.float64)).astype(np.float32).astype(jnp.bfloat16)
    return high, low


def constants():
    count = np.arange(N)
    fourier = np.exp(-2j * np.pi * (np.outer(count, count) % N) / N) / math.sqrt(N)
    freq = np.where(count < H, count, count - N).astype(np.float64)
    fresnel = np.exp(-1j * np.pi * freq * freq / (2.0 * N))
    prop = (np.conj(fourier) * fresnel[None, :]) @ fourier
    straight, turned = prop[:H, :H], prop[:H, ::-1][:, :H]
    mats = []
    for part in ((straight + turned) / 2, (straight - turned) / 2):
        for side in (part, np.conj(part)):
            real, imag = side.real, side.imag
            mats.append(np.stack(split_np(np.block([[real, imag], [-imag, real]]))))
    half = np.arange(H) - 127.5
    angle = 2 * np.pi * np.outer(half, half) / N
    zero = np.zeros((H, H))
    both = np.block([[np.cos(angle) / 16, zero], [zero, np.sin(angle) / 16]])
    mats.append(np.stack(split_np(both)))
    table = np.stack(mats)
    order = np.concatenate([np.arange(H), N - 1 - np.arange(H)])
    tilt = np.exp(-2j * np.pi * 127.5 * order / N)
    phase = np.outer(tilt, tilt)
    phases = np.stack([phase.real, phase.imag]).astype(np.float32)
    return table, phases


def mirror(value):
    lanes = H - 1 - lax.broadcasted_iota(jnp.int32, (N, H), 1)
    right = jnp.take_along_axis(value[:, H:], lanes, axis=1)
    value = jnp.concatenate([value[:, :H], right], axis=1)
    rows = 7 - lax.broadcasted_iota(jnp.int32, (8, N), 0)
    tiles = [
        jnp.take_along_axis(value[N - 8 - 8 * i : N - 8 * i], rows, axis=0) for i in range(H // 8)
    ]
    return jnp.concatenate([value[:H]] + tiles, axis=0)


def parts(value):
    high = value.astype(BF16)
    return high, (value - high.astype(F32)).astype(BF16)


def dot(left, right):
    return jnp.dot(left, right, preferred_element_type=F32)


CH = 16
CHUNKS = H // CH


def fold4(tl, tr, bl, br):
    a, b = tl + bl, tr + br
    c, d = tl - bl, tr - br
    return a + b, a - b, c + d, c - d


def mul(a, b):
    return a[0] * b[0] - a[1] * b[1], a[0] * b[1] + a[1] * b[0]


def mulc(a, b):
    return a[0] * b[0] + a[1] * b[1], a[0] * b[1] - a[1] * b[0]


QUADS = ((0, 0), (0, 1), (1, 0), (1, 1))


def quad(ref, lead, row, q):
    r, c = q
    return ref[lead + (slice(r * H + row, r * H + row + CH), slice(c * H, c * H + H))]


def put(ref, lead, row, q, value):
    r, c = q
    ref[lead + (slice(r * H + row, r * H + row + CH), slice(c * H, c * H + H))] = value


def store_right_prop(op, mode, row, real, imag):
    for index, (r, c) in enumerate(QUADS):
        for part, value in ((0, real[index]), (1, imag[index])):
            high, low = parts(value)
            rows = slice(mode * N + r * H + row, mode * N + r * H + row + CH)
            op[c, rows, part * H : part * H + H] = high
            op[c, rows, N + part * H : N + part * H + H] = low


def store_right_four(op, mode, row, real, imag):
    for index, (r, c) in enumerate(QUADS):
        for part, value in ((0, real[index]), (1, imag[index])):
            high, low = parts(value)
            rows = slice(mode * N + r * H + row, mode * N + r * H + row + CH)
            op[part, rows, c * H : c * H + H] = high
            op[part, rows, N + c * H : N + c * H + H] = low


def stack_rows(table, which):
    return jnp.concatenate([table[which, 0], table[which, 0], table[which, 1]], axis=0)


def stack_cols(table, which):
    return jnp.concatenate([table[which, 0], table[which, 0], table[which, 1]], axis=1)


def three(ref_value):
    return jnp.concatenate([ref_value, ref_value[:, :N]], axis=1)


def prop_products(op, mid, out, table, conjugate, modes):
    for c in (0, 1):
        matrix = stack_rows(table, 2 * c + conjugate)
        for m in range(modes):
            rows = slice(m * N, m * N + N)
            res = dot(three(op[c, rows, :]), matrix)
            high, low = parts(res)
            for level, value in ((0, high), (1, low)):
                for r in (0, 1):
                    for p in (0, 1):
                        mid[
                            r,
                            level * N + p * H : level * N + p * H + H,
                            m * N + c * H : m * N + c * H + H,
                        ] = value[r * H : r * H + H, p * H : p * H + H]
    for r in (0, 1):
        matrix = stack_cols(table, 2 * r + 1 - conjugate)
        for m in range(modes):
            cols = slice(m * N, m * N + N)
            x = mid[r, :, cols]
            x = jnp.concatenate([x, x[:N]], axis=0)
            out[r, :, cols] = dot(matrix, x)


def four_products(op, mid, out, table, modes):
    matrix = stack_rows(table, 4)
    for p in (0, 1):
        for m in range(modes):
            rows = slice(m * N, m * N + N)
            res = dot(three(op[p, rows, :]), matrix)
            high, low = parts(res)
            mid[p, :N, m * N : m * N + N] = high
            mid[p, N:, m * N : m * N + N] = low
    matrix = stack_cols(table, 4)
    for p in (0, 1):
        for m in range(modes):
            cols = slice(m * N, m * N + N)
            x = mid[p, :, cols]
            x = jnp.concatenate([x, x[:N]], axis=0)
            out[p, :, cols] = dot(matrix, x)


def load_prop(out, mode, row):
    result = []
    for p in (0, 1):
        result.append(
            [
                out[r, p * H + row : p * H + row + CH, mode * N + c * H : mode * N + c * H + H]
                for r, c in QUADS
            ]
        )
    return result


def load_four(out, mode, row, sign):
    real, imag = [
        [
            out[p, r * H + row : r * H + row + CH, mode * N + c * H : mode * N + c * H + H]
            for r, c in QUADS
        ]
        for p in (0, 1)
    ]
    if sign > 0:
        return (
            [real[0], imag[1], imag[2], -real[3]],
            [imag[0], -real[1], -real[2], -imag[3]],
        )
    return (
        [real[0], -imag[1], -imag[2], -real[3]],
        [imag[0], real[1], real[2], -imag[3]],
    )


def unfold4(ee, eo, oe, oo):
    a, b = ee + eo, ee - eo
    c, d = oe + oo, oe - oo
    return a + c, b + d, a - c, b - d


def field(ref, lead, row, q):
    return quad(ref, lead + (0,), row, q), quad(ref, lead + (1,), row, q)


def fold_pairs(pairs):
    return fold4(*[v[0] for v in pairs]), fold4(*[v[1] for v in pairs])


def window_of(place, mine, other):
    y0, x0, odd = place[0], place[1], place[2]
    scale = place[3].astype(F32)
    rows = lax.broadcasted_iota(jnp.int32, (N, N), 0)
    upper = jnp.where(rows >= y0, 1 - odd, odd) > 0
    result = []
    for p in range(2):
        value = jnp.where(upper, mine[p] * scale, other[p])
        value = pltpu.roll(pltpu.roll(value, lax.rem(N - y0, N), 0), lax.rem(N - x0, N), 1)
        result.append(mirror(value))
    return result


def wrapped(place, value):
    return pltpu.roll(pltpu.roll(mirror(value), place[0], 0), place[1], 1)


def add_pair(total, value):
    return total[0] + value[0], total[1] + value[1]


def zeros():
    return [(jnp.zeros((CH, H), F32), jnp.zeros((CH, H), F32))] * 4


def first_kernel(place, mine, other, probes, table, q1, obj, op, mid, out):
    modes = probes.shape[0]
    obj[0], obj[1] = window_of(place, mine, other)
    for m in range(modes):
        for k in range(CHUNKS):
            row = k * CH
            pairs = [mul(field(probes, (m,), row, q), field(obj, (), row, q)) for q in QUADS]
            store_right_prop(op, m, row, *fold_pairs(pairs))
    prop_products(op, mid, out, table, 0, modes)
    for m in range(modes):
        for k in range(CHUNKS):
            row = k * CH
            real, imag = load_prop(out, m, row)
            for q, v in zip(QUADS, zip(unfold4(*real), unfold4(*imag))):
                put(q1, (m, 0), row, q, v[0])
                put(q1, (m, 1), row, q, v[1])


def second_kernel(
    place, mine, other, q1, amplitude, table, phases, probes, first_obj,
    grads1, grads0, send, keep,
    obj, amp, op, mid, out,
):
    modes = q1.shape[0]
    obj[0], obj[1] = mul(window_of(place, mine, other), (phases[0], phases[1]))
    amp[...] = mirror(amplitude[0])
    for m in range(modes):
        for k in range(CHUNKS):
            row = k * CH
            pairs = [mul(field(q1, (m,), row, q), field(obj, (), row, q)) for q in QUADS]
            store_right_four(op, m, row, *fold_pairs(pairs))
    four_products(op, mid, out, table, modes)
    for k in range(CHUNKS):
        row = k * CH
        total = [jnp.zeros((CH, H), F32)] * 4
        for m in range(modes):
            real, imag = load_four(out, m, row, 1)
            for i, v in enumerate(zip(unfold4(*real), unfold4(*imag))):
                total[i] = total[i] + (v[0] * v[0] + v[1] * v[1])
        factor = [
            1.0 - quad(amp, (), row, q) * lax.rsqrt(total[i] + 1.0) for i, q in enumerate(QUADS)
        ]
        for m in range(modes):
            real, imag = load_four(out, m, row, 1)
            pairs = [
                (factor[i] * v[0], factor[i] * v[1])
                for i, v in enumerate(zip(unfold4(*real), unfold4(*imag)))
            ]
            store_right_four(op, m, row, *fold_pairs(pairs))
    four_products(op, mid, out, table, modes)
    for k in range(CHUNKS):
        row = k * CH
        total = zeros()
        for m in range(modes):
            real, imag = load_four(out, m, row, -1)
            pairs = []
            for i, v in enumerate(zip(unfold4(*real), unfold4(*imag))):
                q = QUADS[i]
                total[i] = add_pair(total[i], mulc(field(q1, (m,), row, q), v))
                pairs.append(mulc(field(obj, (), row, q), v))
            store_right_prop(op, m, row, *fold_pairs(pairs))
        for i, q in enumerate(QUADS):
            total[i] = mulc(field(phases, (), row, q), total[i])
        for i, q in enumerate(QUADS):
            put(grads1, (0,), row, q, total[i][0])
            put(grads1, (1,), row, q, total[i][1])
    prop_products(op, mid, out, table, 1, modes)
    half = modes // 2
    for k in range(CHUNKS):
        row = k * CH
        total = zeros()
        for m in range(modes):
            real, imag = load_prop(out, m, row)
            terms = send if m < half else keep
            for i, v in enumerate(zip(unfold4(*real), unfold4(*imag))):
                q = QUADS[i]
                total[i] = add_pair(total[i], mulc(field(probes, (m,), row, q), v))
                term = mulc(field(first_obj, (), row, q), v)
                put(terms, (m % half, 0), row, q, term[0])
                put(terms, (m % half, 1), row, q, term[1])
        for i, q in enumerate(QUADS):
            put(grads0, (0,), row, q, total[i][0])
            put(grads0, (1,), row, q, total[i][1])
    for terms in (send, keep):
        for m in range(half):
            for p in range(2):
                terms[m, p] = mirror(terms[m, p])
    for p in range(2):
        grads1[p] = wrapped(place, grads1[p])
        grads0[p] = wrapped(place, grads0[p])


def call(kernel, args, shapes, scratch, flops, mib):
    spec = pl.BlockSpec(memory_space=pltpu.VMEM)
    return pl.pallas_call(
        kernel,
        in_specs=[pl.BlockSpec(memory_space=pltpu.SMEM)] + [spec] * (len(args) - 1),
        out_specs=[spec] * len(shapes),
        out_shape=[jax.ShapeDtypeStruct(shape, dtype) for shape, dtype in shapes],
        scratch_shapes=[pltpu.VMEM(shape, dtype) for shape, dtype in scratch],
        compiler_params=pltpu.CompilerParams(vmem_limit_bytes=mib << 20),
        cost_estimate=pl.CostEstimate(flops=flops, bytes_accessed=4 << 20, transcendentals=0),
    )(*args)


def products_scratch(modes):
    return [((2, 2 * N, modes * N), BF16), ((2, N, modes * N), F32)]


def operand(modes):
    return ((2, modes * N, 2 * N), BF16)


def first(place, mine, other, probes, table):
    modes = probes.shape[0]
    return call(
        first_kernel,
        (place, mine, other, probes, table),
        [(probes.shape, F32), ((2, N, N), F32)],
        [operand(modes)] + products_scratch(modes),
        3 << 30,
        20,
    )


def second(place, mine, other, q1, amplitude, table, phases, probes, first_obj):
    modes = q1.shape[0]
    field_shape, terms_shape = ((2, N, N), F32), ((modes // 2, 2, N, N), F32)
    return call(
        second_kernel,
        (place, mine, other, q1, amplitude, table, phases, probes, first_obj),
        [field_shape, field_shape, terms_shape, terms_shape],
        [field_shape, ((N, N), F32), operand(modes)] + products_scratch(modes),
        9 << 30,
        26,
    )


def stage_kernel(core, source, table, phases, target, table_out, phases_out):
    target[0] = mirror(source[0])

    @pl.when(pl.program_id(0) == 0)
    def _():
        table_out[...] = table[...]
        phases_out[...] = phases[...]


def staged(core, probes):
    table, phases = (jnp.asarray(v) for v in constants())
    images = probes.reshape(-1, N, N)
    count = images.shape[0]
    half = count // 2
    whole = lambda value: pl.BlockSpec(value.shape, lambda i, core: (0,) * value.ndim)
    flip, table, phases = pl.pallas_call(
        stage_kernel,
        grid_spec=pltpu.PrefetchScalarGridSpec(
            num_scalar_prefetch=1,
            grid=(count,),
            in_specs=[
                pl.BlockSpec((1, N, N), lambda i, core: ((i + half * (1 - core[0])) % count, 0, 0)),
                whole(table),
                whole(phases),
            ],
            out_specs=[
                pl.BlockSpec((1, N, N), lambda i, core: (i, 0, 0)),
                whole(table),
                whole(phases),
            ],
        ),
        out_shape=[
            jax.ShapeDtypeStruct(images.shape, F32),
            jax.ShapeDtypeStruct(table.shape, table.dtype),
            jax.ShapeDtypeStruct(phases.shape, phases.dtype),
        ],
    )(core, images, table, phases)
    return flip.reshape(probes.shape), table, phases


POS = ("y", "zh", "core")
TILE = ("x", "zl")
ROWS = 32
COLUMNS = 8
MODES = 4


def shifted(value, axes, steps):
    count = math.prod(lax.axis_size(axis) for axis in axes)
    first, last = (max(0, -steps), min(count, count - steps))
    return lax.ppermute(value, axes, [(source, source + steps) for source in range(first, last)])


def piece(value, index):
    return lax.dynamic_index_in_dim(value, index, 0, keepdims=False)


def ring(value, axis, step):
    count = lax.axis_size(axis)
    return lax.ppermute(value, axis, [(i, (i + step) % count) for i in range(count)])


def pieces(value, axis):
    count, me = lax.axis_size(axis), lax.axis_index(axis)
    value = value.reshape(count, -1, N)
    return [piece(value, (me + step) & (count - 1)) for step in range(1, count)] + [piece(value, me)]


def scatter_sum(parts, axis):
    arrived = [ring(part, axis, step + 1) for step, part in enumerate(parts[:-1])]
    total = parts[-1]
    for part in arrived:
        total = total + part
    return total


def after(value, *others):
    return lax.optimization_barrier((value,) + others)[0]


def circular_sum(parts, axis, *beside):
    total = ring(parts[0], axis, -1)
    for step, part in enumerate(parts[1:-1]):
        total = ring(total + (after(part, *beside) if step else part), axis, -1)
    return total + parts[-1]


def collected(value, travelled, axis, *beside):
    count, me = lax.axis_size(axis), lax.axis_index(axis)
    whole = jnp.zeros((count,) + value.shape, value.dtype)
    whole = after(lax.dynamic_update_index_in_dim(whole, value, me, 0), *beside)
    for step, part in enumerate(travelled):
        whole = lax.dynamic_update_index_in_dim(whole, part, (me + step + 1) & (count - 1), 0)
    return whole.reshape(-1, N)


def gather(value, axis, *beside):
    steps = range(1, lax.axis_size(axis))
    return collected(value, [ring(value, axis, -step) for step in steps], axis, *beside)


def circular_gather(value, axis):
    travelled = [ring(value, axis, -1)]
    for _ in range(2, lax.axis_size(axis)):
        travelled.append(ring(travelled[-1], axis, -1))
    return collected(value, travelled, axis)


def exchange(value, bits):
    axes = ("zh", "zl")
    count = math.prod(lax.axis_size(axis) for axis in axes)
    return lax.ppermute(value, axes, [(i, i ^ bits) for i in range(count)])


def summed_over_z(value):
    value = (value + exchange(value, 1)) + (exchange(value, 2) + exchange(value, 3))
    return value + exchange(value, 4)


def moved(value, even, odd):
    pairs = []
    for row in range(ROWS):
        for column in range(COLUMNS):
            target = row + (odd if column % 2 else even)
            if column % 2:
                target %= ROWS
            if 0 <= target < ROWS:
                pairs.append((row * COLUMNS + column, target * COLUMNS + column))
    return lax.ppermute(value, POS + TILE, pairs)


def per_device(object_field, probe_modes, amplitudes, corners):
    row = lax.broadcasted_iota(jnp.int32, (N, N), 0)
    col = lax.broadcasted_iota(jnp.int32, (N, N), 1)
    odd = lax.axis_index("zl")
    is_odd = odd == 1
    first_row = (lax.axis_index(POS) == 0) & is_odd
    above = lax.ppermute(corners, POS, [(i, (i + 1) % ROWS) for i in range(ROWS)])
    yp, xp = [jnp.where(is_odd, above[0, i], corners[0, i]) for i in (0, 1)]
    yq, xq = [jnp.where(is_odd, corners[0, i], above[0, i]) for i in (0, 1)]
    live = jnp.where(first_row, 0, 1)
    place = jnp.stack([yp, xp, odd, live]).astype(jnp.int32)
    flip, table, phases = staged(lax.axis_index("core").astype(jnp.int32).reshape(1), probe_modes)
    right = after(shifted(after(object_field, above), TILE, -1), flip)
    mine, mixed = [
        [jnp.where(col < x, right[s], object_field[s]) for s in range(2)] for x in (xp, xq)
    ]
    other = [moved(mixed[s], -1, 1) for s in range(2)]

    def split(grads, arrived):
        kept = jnp.where(((row >= yp) != is_odd) & ~first_row, grads, 0.0)
        taken = jnp.where((row < yq) != is_odd, arrived, 0.0)
        leaving = jnp.where(col < xp, kept, 0.0) + jnp.where(col < xq, taken, 0.0)
        staying = jnp.where(col >= xp, kept, 0.0) + jnp.where(col >= xq, taken, 0.0)
        return staying, leaving

    amplitude = moved(after(amplitudes, *mixed), 0, 1)
    q1, obj = first(place, mine[0], other[0], flip, table)
    grads1, grads0, send, keep = second(
        place, mine[1], other[1], q1, amplitude, table, phases, flip, obj
    )
    swap = [(0, 1), (1, 0)]
    arrived1 = moved(grads1, 1, -1)
    across = pieces(keep + lax.ppermute(send, "core", swap), "y")
    staying1, leaving1 = split(grads1, after(arrived1, *across))
    received1 = shifted(leaving1, TILE, 1)
    across[-1] = after(across[-1], leaving1)
    across = pieces(scatter_sum(across, "y"), "x")
    arrived0 = moved(after(grads0, leaving1), 1, -1)
    partial = circular_sum(across, "x", received1)
    staying0, leaving0 = split(grads0, arrived0)
    total = summed_over_z(after(partial, leaving0))
    received0 = shifted(after(leaving0, total), TILE, 1)
    total = circular_gather(total, "x")
    object_grad = jnp.stack([staying0 + received0, staying1 + received1])
    total = gather(total, "y", object_grad)
    opposite = lax.ppermute(total, "core", swap)
    half = lax.broadcasted_iota(jnp.int32, (2, 1, 1), 0)
    probe_grad = jnp.where(half == lax.axis_index("core"), total, opposite)
    probe_grad = probe_grad.reshape(probe_modes.shape)
    return (object_grad, probe_grad)


def solution(mesh):
    split = jax.sharding.Mesh(mesh.devices.reshape(4, 4, 2, 4, 2), POS + TILE)
    in_specs = (
        P(None, None, POS, TILE),
        P(),
        P(POS + TILE, None, None),
        P(POS + TILE, None),
    )
    out_specs = (P(None, None, POS, TILE), P())
    return jax.shard_map(
        per_device, mesh=split, in_specs=in_specs, out_specs=out_specs, check_vma=False
    )
```

```python
import functools
import math

import jax
import jax.numpy as jnp
import numpy as np
from jax import lax
from jax.experimental import pallas as pl
from jax.experimental.pallas import tpu as pltpu
from jax.sharding import PartitionSpec as P

N = 256
H = 128
F32 = jnp.float32
BF16 = jnp.bfloat16


def split_np(matrix):
    high = matrix.astype(np.float32).astype(jnp.bfloat16)
    low = (matrix - high.astype(np.float64)).astype(np.float32).astype(jnp.bfloat16)
    return high, low


def constants():
    count = np.arange(N)
    fourier = np.exp(-2j * np.pi * (np.outer(count, count) % N) / N) / math.sqrt(N)
    freq = np.where(count < H, count, count - N).astype(np.float64)
    fresnel = np.exp(-1j * np.pi * freq * freq / (2.0 * N))
    prop = (np.conj(fourier) * fresnel[None, :]) @ fourier
    straight, turned = prop[:H, :H], prop[:H, ::-1][:, :H]
    mats = []
    for part in ((straight + turned) / 2, (straight - turned) / 2):
        for side in (part, np.conj(part)):
            real, imag = side.real, side.imag
            mats.append(np.stack(split_np(np.block([[real, imag], [-imag, real]]))))
    half = np.arange(H) - 127.5
    angle = 2 * np.pi * np.outer(half, half) / N
    zero = np.zeros((H, H))
    both = np.block([[np.cos(angle) / 16, zero], [zero, np.sin(angle) / 16]])
    mats.append(np.stack(split_np(both)))
    table = np.stack(mats)
    order = np.concatenate([np.arange(H), N - 1 - np.arange(H)])
    tilt = np.exp(-2j * np.pi * 127.5 * order / N)
    phase = np.outer(tilt, tilt)
    phases = np.stack([phase.real, phase.imag]).astype(np.float32)
    return table, phases


def mirror(value):
    lanes = H - 1 - lax.broadcasted_iota(jnp.int32, (N, H), 1)
    right = jnp.take_along_axis(value[:, H:], lanes, axis=1)
    value = jnp.concatenate([value[:, :H], right], axis=1)
    rows = 7 - lax.broadcasted_iota(jnp.int32, (8, N), 0)
    tiles = [
        jnp.take_along_axis(value[N - 8 - 8 * i : N - 8 * i], rows, axis=0) for i in range(H // 8)
    ]
    return jnp.concatenate([value[:H]] + tiles, axis=0)


def parts(value):
    high = value.astype(BF16)
    return high, (value - high.astype(F32)).astype(BF16)


def dot(left, right):
    return jnp.dot(left, right, preferred_element_type=F32)


CH = 16
CHUNKS = H // CH


def fold4(tl, tr, bl, br):
    a, b = tl + bl, tr + br
    c, d = tl - bl, tr - br
    return a + b, a - b, c + d, c - d


def mul(a, b):
    return a[0] * b[0] - a[1] * b[1], a[0] * b[1] + a[1] * b[0]


def mulc(a, b):
    return a[0] * b[0] + a[1] * b[1], a[0] * b[1] - a[1] * b[0]


QUADS = ((0, 0), (0, 1), (1, 0), (1, 1))


def quad(ref, lead, row, q):
    r, c = q
    return ref[lead + (slice(r * H + row, r * H + row + CH), slice(c * H, c * H + H))]


def put(ref, lead, row, q, value):
    r, c = q
    ref[lead + (slice(r * H + row, r * H + row + CH), slice(c * H, c * H + H))] = value


def store_right_prop(op, mode, row, real, imag):
    for index, (r, c) in enumerate(QUADS):
        for part, value in ((0, real[index]), (1, imag[index])):
            high, low = parts(value)
            rows = slice(mode * N + r * H + row, mode * N + r * H + row + CH)
            op[c, rows, part * H : part * H + H] = high
            op[c, rows, N + part * H : N + part * H + H] = low


def store_right_four(op, mode, row, real, imag):
    for index, (r, c) in enumerate(QUADS):
        for part, value in ((0, real[index]), (1, imag[index])):
            high, low = parts(value)
            rows = slice(mode * N + r * H + row, mode * N + r * H + row + CH)
            op[part, rows, c * H : c * H + H] = high
            op[part, rows, N + c * H : N + c * H + H] = low


def stack_rows(table, which):
    return jnp.concatenate([table[which, 0], table[which, 0], table[which, 1]], axis=0)


def stack_cols(table, which):
    return jnp.concatenate([table[which, 0], table[which, 0], table[which, 1]], axis=1)


def three(ref_value):
    return jnp.concatenate([ref_value, ref_value[:, :N]], axis=1)


def prop_products(op, mid, out, table, conjugate, modes):
    for c in (0, 1):
        matrix = stack_rows(table, 2 * c + conjugate)
        for m in range(modes):
            rows = slice(m * N, m * N + N)
            res = dot(three(op[c, rows, :]), matrix)
            high, low = parts(res)
            for level, value in ((0, high), (1, low)):
                for r in (0, 1):
                    for p in (0, 1):
                        mid[
                            r,
                            level * N + p * H : level * N + p * H + H,
                            m * N + c * H : m * N + c * H + H,
                        ] = value[r * H : r * H + H, p * H : p * H + H]
    for r in (0, 1):
        matrix = stack_cols(table, 2 * r + 1 - conjugate)
        for m in range(modes):
            cols = slice(m * N, m * N + N)
            x = mid[r, :, cols]
            x = jnp.concatenate([x, x[:N]], axis=0)
            out[r, :, cols] = dot(matrix, x)


def four_products(op, mid, out, table, modes):
    matrix = stack_rows(table, 4)
    for p in (0, 1):
        for m in range(modes):
            rows = slice(m * N, m * N + N)
            res = dot(three(op[p, rows, :]), matrix)
            high, low = parts(res)
            mid[p, :N, m * N : m * N + N] = high
            mid[p, N:, m * N : m * N + N] = low
    matrix = stack_cols(table, 4)
    for p in (0, 1):
        for m in range(modes):
            cols = slice(m * N, m * N + N)
            x = mid[p, :, cols]
            x = jnp.concatenate([x, x[:N]], axis=0)
            out[p, :, cols] = dot(matrix, x)


def load_prop(out, mode, row):
    result = []
    for p in (0, 1):
        result.append(
            [
                out[r, p * H + row : p * H + row + CH, mode * N + c * H : mode * N + c * H + H]
                for r, c in QUADS
            ]
        )
    return result


def load_four(out, mode, row, sign):
    real, imag = [
        [
            out[p, r * H + row : r * H + row + CH, mode * N + c * H : mode * N + c * H + H]
            for r, c in QUADS
        ]
        for p in (0, 1)
    ]
    if sign > 0:
        return (
            [real[0], imag[1], imag[2], -real[3]],
            [imag[0], -real[1], -real[2], -imag[3]],
        )
    return (
        [real[0], -imag[1], -imag[2], -real[3]],
        [imag[0], real[1], real[2], -imag[3]],
    )


def unfold4(ee, eo, oe, oo):
    a, b = ee + eo, ee - eo
    c, d = oe + oo, oe - oo
    return a + c, b + d, a - c, b - d


def field(ref, lead, row, q):
    return quad(ref, lead + (0,), row, q), quad(ref, lead + (1,), row, q)


def fold_pairs(pairs):
    return fold4(*[v[0] for v in pairs]), fold4(*[v[1] for v in pairs])


def window_of(place, mine, other):
    y0, x0, odd = place[0], place[1], place[2]
    scale = place[3].astype(F32)
    rows = lax.broadcasted_iota(jnp.int32, (N, N), 0)
    upper = jnp.where(rows >= y0, 1 - odd, odd) > 0
    result = []
    for p in range(2):
        value = jnp.where(upper, mine[p] * scale, other[p])
        value = pltpu.roll(pltpu.roll(value, lax.rem(N - y0, N), 0), lax.rem(N - x0, N), 1)
        result.append(mirror(value))
    return result


def wrapped(place, value):
    return pltpu.roll(pltpu.roll(mirror(value), place[0], 0), place[1], 1)


def add_pair(total, value):
    return total[0] + value[0], total[1] + value[1]


def zeros():
    return [(jnp.zeros((CH, H), F32), jnp.zeros((CH, H), F32))] * 4


def first_kernel(place, mine, other, probes, table, q1, obj, op, mid, out):
    modes = probes.shape[0]
    obj[0], obj[1] = window_of(place, mine, other)
    for m in range(modes):
        for k in range(CHUNKS):
            row = k * CH
            pairs = [mul(field(probes, (m,), row, q), field(obj, (), row, q)) for q in QUADS]
            store_right_prop(op, m, row, *fold_pairs(pairs))
    prop_products(op, mid, out, table, 0, modes)
    for m in range(modes):
        for k in range(CHUNKS):
            row = k * CH
            real, imag = load_prop(out, m, row)
            for q, v in zip(QUADS, zip(unfold4(*real), unfold4(*imag))):
                put(q1, (m, 0), row, q, v[0])
                put(q1, (m, 1), row, q, v[1])


def second_kernel(
    place, mine, other, q1, amplitude, table, phases, probes, first_obj,
    grads1, grads0, send, keep,
    obj, amp, op, mid, out,
):
    modes = q1.shape[0]
    obj[0], obj[1] = mul(window_of(place, mine, other), (phases[0], phases[1]))
    amp[...] = mirror(amplitude[0])
    for m in range(modes):
        for k in range(CHUNKS):
            row = k * CH
            pairs = [mul(field(q1, (m,), row, q), field(obj, (), row, q)) for q in QUADS]
            store_right_four(op, m, row, *fold_pairs(pairs))
    four_products(op, mid, out, table, modes)
    for k in range(CHUNKS):
        row = k * CH
        total = [jnp.zeros((CH, H), F32)] * 4
        for m in range(modes):
            real, imag = load_four(out, m, row, 1)
            for i, v in enumerate(zip(unfold4(*real), unfold4(*imag))):
                total[i] = total[i] + (v[0] * v[0] + v[1] * v[1])
        factor = [
            1.0 - quad(amp, (), row, q) * lax.rsqrt(total[i] + 1.0) for i, q in enumerate(QUADS)
        ]
        for m in range(modes):
            real, imag = load_four(out, m, row, 1)
            pairs = [
                (factor[i] * v[0], factor[i] * v[1])
                for i, v in enumerate(zip(unfold4(*real), unfold4(*imag)))
            ]
            store_right_four(op, m, row, *fold_pairs(pairs))
    four_products(op, mid, out, table, modes)
    for k in range(CHUNKS):
        row = k * CH
        total = zeros()
        for m in range(modes):
            real, imag = load_four(out, m, row, -1)
            pairs = []
            for i, v in enumerate(zip(unfold4(*real), unfold4(*imag))):
                q = QUADS[i]
                total[i] = add_pair(total[i], mulc(field(q1, (m,), row, q), v))
                pairs.append(mulc(field(obj, (), row, q), v))
            store_right_prop(op, m, row, *fold_pairs(pairs))
        for i, q in enumerate(QUADS):
            total[i] = mulc(field(phases, (), row, q), total[i])
        for i, q in enumerate(QUADS):
            put(grads1, (0,), row, q, total[i][0])
            put(grads1, (1,), row, q, total[i][1])
    prop_products(op, mid, out, table, 1, modes)
    half = modes // 2
    for k in range(CHUNKS):
        row = k * CH
        total = zeros()
        for m in range(modes):
            real, imag = load_prop(out, m, row)
            terms = send if m < half else keep
            for i, v in enumerate(zip(unfold4(*real), unfold4(*imag))):
                q = QUADS[i]
                total[i] = add_pair(total[i], mulc(field(probes, (m,), row, q), v))
                term = mulc(field(first_obj, (), row, q), v)
                put(terms, (m % half, 0), row, q, term[0])
                put(terms, (m % half, 1), row, q, term[1])
        for i, q in enumerate(QUADS):
            put(grads0, (0,), row, q, total[i][0])
            put(grads0, (1,), row, q, total[i][1])
    for terms in (send, keep):
        for m in range(half):
            for p in range(2):
                terms[m, p] = mirror(terms[m, p])
    for p in range(2):
        grads1[p] = wrapped(place, grads1[p])
        grads0[p] = wrapped(place, grads0[p])


def call(kernel, args, shapes, scratch, flops, mib):
    spec = pl.BlockSpec(memory_space=pltpu.VMEM)
    return pl.pallas_call(
        kernel,
        in_specs=[pl.BlockSpec(memory_space=pltpu.SMEM)] + [spec] * (len(args) - 1),
        out_specs=[spec] * len(shapes),
        out_shape=[jax.ShapeDtypeStruct(shape, dtype) for shape, dtype in shapes],
        scratch_shapes=[pltpu.VMEM(shape, dtype) for shape, dtype in scratch],
        compiler_params=pltpu.CompilerParams(vmem_limit_bytes=mib << 20),
        cost_estimate=pl.CostEstimate(flops=flops, bytes_accessed=4 << 20, transcendentals=0),
    )(*args)


def products_scratch(modes):
    return [((2, 2 * N, modes * N), BF16), ((2, N, modes * N), F32)]


def operand(modes):
    return ((2, modes * N, 2 * N), BF16)


def first(place, mine, other, probes, table):
    modes = probes.shape[0]
    return call(
        first_kernel,
        (place, mine, other, probes, table),
        [(probes.shape, F32), ((2, N, N), F32)],
        [operand(modes)] + products_scratch(modes),
        3 << 30,
        14,
    )


def second(place, mine, other, q1, amplitude, table, phases, probes, first_obj):
    modes = q1.shape[0]
    field_shape, terms_shape = ((2, N, N), F32), ((modes // 2, 2, N, N), F32)
    return call(
        second_kernel,
        (place, mine, other, q1, amplitude, table, phases, probes, first_obj),
        [field_shape, field_shape, terms_shape, terms_shape],
        [field_shape, ((N, N), F32), operand(modes)] + products_scratch(modes),
        9 << 30,
        22,
    )


def stage_kernel(core, source, table, phases, target, table_out, phases_out):
    target[0] = mirror(source[0])

    @pl.when(pl.program_id(0) == 0)
    def _():
        table_out[...] = table[...]
        phases_out[...] = phases[...]


def staged(core, probes):
    table, phases = (jnp.asarray(v) for v in constants())
    images = probes.reshape(-1, N, N)
    count = images.shape[0]
    half = count // 2
    whole = lambda value: pl.BlockSpec(value.shape, lambda i, core: (0,) * value.ndim)
    flip, table, phases = pl.pallas_call(
        stage_kernel,
        grid_spec=pltpu.PrefetchScalarGridSpec(
            num_scalar_prefetch=1,
            grid=(count,),
            in_specs=[
                pl.BlockSpec((1, N, N), lambda i, core: ((i + half * (1 - core[0])) % count, 0, 0)),
                whole(table),
                whole(phases),
            ],
            out_specs=[
                pl.BlockSpec((1, N, N), lambda i, core: (i, 0, 0)),
                whole(table),
                whole(phases),
            ],
        ),
        out_shape=[
            jax.ShapeDtypeStruct(images.shape, F32),
            jax.ShapeDtypeStruct(table.shape, table.dtype),
            jax.ShapeDtypeStruct(phases.shape, phases.dtype),
        ],
    )(core, images, table, phases)
    return flip.reshape(probes.shape), table, phases


POS = ("y", "zh", "core")
TILE = ("x", "zl")
ROWS = 32
COLUMNS = 8
MODES = 4


def shifted(value, axes, steps):
    count = math.prod(lax.axis_size(axis) for axis in axes)
    first, last = (max(0, -steps), min(count, count - steps))
    return lax.ppermute(value, axes, [(source, source + steps) for source in range(first, last)])


def piece(value, index):
    return lax.dynamic_index_in_dim(value, index, 0, keepdims=False)


def ring(value, axis, step):
    count = lax.axis_size(axis)
    return lax.ppermute(value, axis, [(i, (i + step) % count) for i in range(count)])


def pieces(value, axis):
    count, me = lax.axis_size(axis), lax.axis_index(axis)
    value = value.reshape(count, -1, N)
    return [piece(value, (me + step) & (count - 1)) for step in range(1, count)] + [piece(value, me)]


def scatter_sum(parts, axis):
    arrived = [ring(part, axis, step + 1) for step, part in enumerate(parts[:-1])]
    total = parts[-1]
    for part in arrived:
        total = total + part
    return total


def after(value, *others):
    return lax.optimization_barrier((value,) + others)[0]


def circular_sum(parts, axis, *beside):
    total = ring(parts[0], axis, -1)
    for step, part in enumerate(parts[1:-1]):
        total = ring(total + (after(part, *beside) if step else part), axis, -1)
    return total + parts[-1]


def collected(value, travelled, axis, *beside):
    count, me = lax.axis_size(axis), lax.axis_index(axis)
    whole = jnp.zeros((count,) + value.shape, value.dtype)
    whole = after(lax.dynamic_update_index_in_dim(whole, value, me, 0), *beside)
    for step, part in enumerate(travelled):
        whole = lax.dynamic_update_index_in_dim(whole, part, (me + step + 1) & (count - 1), 0)
    return whole.reshape(-1, N)


def gather(value, axis, *beside):
    steps = range(1, lax.axis_size(axis))
    return collected(value, [ring(value, axis, -step) for step in steps], axis, *beside)


def exchange(value, bits):
    axes = ("zh", "zl")
    count = math.prod(lax.axis_size(axis) for axis in axes)
    return lax.ppermute(value, axes, [(i, i ^ bits) for i in range(count)])


def summed_over_z(value):
    value = (value + exchange(value, 1)) + (exchange(value, 2) + exchange(value, 3))
    return value + exchange(value, 4)


def moved(value, even, odd):
    pairs = []
    for row in range(ROWS):
        for column in range(COLUMNS):
            target = row + (odd if column % 2 else even)
            if column % 2:
                target %= ROWS
            if 0 <= target < ROWS:
                pairs.append((row * COLUMNS + column, target * COLUMNS + column))
    return lax.ppermute(value, POS + TILE, pairs)


def per_device(object_field, probe_modes, amplitudes, corners):
    row = lax.broadcasted_iota(jnp.int32, (N, N), 0)
    col = lax.broadcasted_iota(jnp.int32, (N, N), 1)
    odd = lax.axis_index("zl")
    is_odd = odd == 1
    first_row = (lax.axis_index(POS) == 0) & is_odd
    above = lax.ppermute(corners, POS, [(i, (i + 1) % ROWS) for i in range(ROWS)])
    yp, xp = [jnp.where(is_odd, above[0, i], corners[0, i]) for i in (0, 1)]
    yq, xq = [jnp.where(is_odd, corners[0, i], above[0, i]) for i in (0, 1)]
    live = jnp.where(first_row, 0, 1)
    place = jnp.stack([yp, xp, odd, live]).astype(jnp.int32)
    flip, table, phases = staged(lax.axis_index("core").astype(jnp.int32).reshape(1), probe_modes)
    right = after(shifted(after(object_field, above), TILE, -1), flip)
    mine, mixed = [
        [jnp.where(col < x, right[s], object_field[s]) for s in range(2)] for x in (xp, xq)
    ]
    other = [moved(mixed[s], -1, 1) for s in range(2)]

    def split(grads, arrived):
        kept = jnp.where(((row >= yp) != is_odd) & ~first_row, grads, 0.0)
        taken = jnp.where((row < yq) != is_odd, arrived, 0.0)
        leaving = jnp.where(col < xp, kept, 0.0) + jnp.where(col < xq, taken, 0.0)
        staying = jnp.where(col >= xp, kept, 0.0) + jnp.where(col >= xq, taken, 0.0)
        return staying, leaving

    amplitude = moved(after(amplitudes, *mixed), 0, 1)
    q1, obj = first(place, mine[0], other[0], flip, table)
    grads1, grads0, send, keep = second(
        place, mine[1], other[1], q1, amplitude, table, phases, flip, obj
    )
    swap = [(0, 1), (1, 0)]
    arrived1 = moved(grads1, 1, -1)
    across = pieces(keep + lax.ppermute(send, "core", swap), "y")
    staying1, leaving1 = split(grads1, after(arrived1, *across))
    received1 = shifted(leaving1, TILE, 1)
    across[-1] = after(across[-1], leaving1)
    across = pieces(scatter_sum(across, "y"), "x")
    arrived0 = moved(after(grads0, leaving1), 1, -1)
    partial = circular_sum(across, "x", received1)
    staying0, leaving0 = split(grads0, arrived0)
    total = summed_over_z(after(partial, leaving0))
    total = gather(total, "x")
    received0 = shifted(after(leaving0, total), TILE, 1)
    total = after(gather(total, "y"), received0)
    object_grad = jnp.stack([staying0 + received0, staying1 + received1])
    opposite = lax.ppermute(total, "core", swap)
    half = lax.broadcasted_iota(jnp.int32, (2, 1, 1), 0)
    probe_grad = jnp.where(half == lax.axis_index("core"), total, opposite)
    probe_grad = probe_grad.reshape(probe_modes.shape)
    return (object_grad, probe_grad)


def solution(mesh):
    split = jax.sharding.Mesh(mesh.devices.reshape(4, 4, 2, 4, 2), POS + TILE)
    in_specs = (
        P(None, None, POS, TILE),
        P(),
        P(POS + TILE, None, None),
        P(POS + TILE, None),
    )
    out_specs = (P(None, None, POS, TILE), P())
    return jax.shard_map(
        per_device, mesh=split, in_specs=in_specs, out_specs=out_specs, check_vma=False
    )
```

```python
import functools
import math

import jax
import jax.numpy as jnp
import numpy as np
from jax import lax
from jax.experimental import pallas as pl
from jax.experimental.pallas import tpu as pltpu
from jax.sharding import PartitionSpec as P

N = 256
H = 128
F32 = jnp.float32
BF16 = jnp.bfloat16


def split_np(matrix):
    high = matrix.astype(np.float32).astype(jnp.bfloat16)
    low = (matrix - high.astype(np.float64)).astype(np.float32).astype(jnp.bfloat16)
    return high, low


def constants():
    count = np.arange(N)
    fourier = np.exp(-2j * np.pi * (np.outer(count, count) % N) / N) / math.sqrt(N)
    freq = np.where(count < H, count, count - N).astype(np.float64)
    fresnel = np.exp(-1j * np.pi * freq * freq / (2.0 * N))
    prop = (np.conj(fourier) * fresnel[None, :]) @ fourier
    straight, turned = prop[:H, :H], prop[:H, ::-1][:, :H]
    mats = []
    for part in ((straight + turned) / 2, (straight - turned) / 2):
        for side in (part, np.conj(part)):
            real, imag = side.real, side.imag
            mats.append(np.stack(split_np(np.block([[real, imag], [-imag, real]]))))
    half = np.arange(H) - 127.5
    angle = 2 * np.pi * np.outer(half, half) / N
    zero = np.zeros((H, H))
    both = np.block([[np.cos(angle) / 16, zero], [zero, np.sin(angle) / 16]])
    mats.append(np.stack(split_np(both)))
    table = np.stack(mats)
    order = np.concatenate([np.arange(H), N - 1 - np.arange(H)])
    tilt = np.exp(-2j * np.pi * 127.5 * order / N)
    phase = np.outer(tilt, tilt)
    phases = np.stack([phase.real, phase.imag]).astype(np.float32)
    return table, phases


def mirror(value):
    lanes = H - 1 - lax.broadcasted_iota(jnp.int32, (N, H), 1)
    right = jnp.take_along_axis(value[:, H:], lanes, axis=1)
    value = jnp.concatenate([value[:, :H], right], axis=1)
    rows = 7 - lax.broadcasted_iota(jnp.int32, (8, N), 0)
    tiles = [
        jnp.take_along_axis(value[N - 8 - 8 * i : N - 8 * i], rows, axis=0) for i in range(H // 8)
    ]
    return jnp.concatenate([value[:H]] + tiles, axis=0)


def parts(value):
    high = value.astype(BF16)
    return high, (value - high.astype(F32)).astype(BF16)


def dot(left, right):
    return jnp.dot(left, right, preferred_element_type=F32)


CH = 16
CHUNKS = H // CH


def fold4(tl, tr, bl, br):
    a, b = tl + bl, tr + br
    c, d = tl - bl, tr - br
    return a + b, a - b, c + d, c - d


def mul(a, b):
    return a[0] * b[0] - a[1] * b[1], a[0] * b[1] + a[1] * b[0]


def mulc(a, b):
    return a[0] * b[0] + a[1] * b[1], a[0] * b[1] - a[1] * b[0]


QUADS = ((0, 0), (0, 1), (1, 0), (1, 1))


def quad(ref, lead, row, q):
    r, c = q
    return ref[lead + (slice(r * H + row, r * H + row + CH), slice(c * H, c * H + H))]


def put(ref, lead, row, q, value):
    r, c = q
    ref[lead + (slice(r * H + row, r * H + row + CH), slice(c * H, c * H + H))] = value


def store_right_prop(op, mode, row, real, imag):
    for index, (r, c) in enumerate(QUADS):
        for part, value in ((0, real[index]), (1, imag[index])):
            high, low = parts(value)
            rows = slice(mode * N + r * H + row, mode * N + r * H + row + CH)
            op[c, rows, part * H : part * H + H] = high
            op[c, rows, N + part * H : N + part * H + H] = low


def store_right_four(op, mode, row, real, imag):
    for index, (r, c) in enumerate(QUADS):
        for part, value in ((0, real[index]), (1, imag[index])):
            high, low = parts(value)
            rows = slice(mode * N + r * H + row, mode * N + r * H + row + CH)
            op[part, rows, c * H : c * H + H] = high
            op[part, rows, N + c * H : N + c * H + H] = low


def stack_rows(table, which):
    return jnp.concatenate([table[which, 0], table[which, 0], table[which, 1]], axis=0)


def stack_cols(table, which):
    return jnp.concatenate([table[which, 0], table[which, 0], table[which, 1]], axis=1)


def three(ref_value):
    return jnp.concatenate([ref_value, ref_value[:, :N]], axis=1)


def prop_products(op, mid, out, table, conjugate, modes):
    for c in (0, 1):
        matrix = stack_rows(table, 2 * c + conjugate)
        for m in range(modes):
            rows = slice(m * N, m * N + N)
            res = dot(three(op[c, rows, :]), matrix)
            high, low = parts(res)
            for level, value in ((0, high), (1, low)):
                for r in (0, 1):
                    for p in (0, 1):
                        mid[
                            r,
                            level * N + p * H : level * N + p * H + H,
                            m * N + c * H : m * N + c * H + H,
                        ] = value[r * H : r * H + H, p * H : p * H + H]
    for r in (0, 1):
        matrix = stack_cols(table, 2 * r + 1 - conjugate)
        for m in range(modes):
            cols = slice(m * N, m * N + N)
            x = mid[r, :, cols]
            x = jnp.concatenate([x, x[:N]], axis=0)
            out[r, :, cols] = dot(matrix, x)


def four_products(op, mid, out, table, modes):
    matrix = stack_rows(table, 4)
    for p in (0, 1):
        for m in range(modes):
            rows = slice(m * N, m * N + N)
            res = dot(three(op[p, rows, :]), matrix)
            high, low = parts(res)
            mid[p, :N, m * N : m * N + N] = high
            mid[p, N:, m * N : m * N + N] = low
    matrix = stack_cols(table, 4)
    for p in (0, 1):
        for m in range(modes):
            cols = slice(m * N, m * N + N)
            x = mid[p, :, cols]
            x = jnp.concatenate([x, x[:N]], axis=0)
            out[p, :, cols] = dot(matrix, x)


def load_prop(out, mode, row):
    result = []
    for p in (0, 1):
        result.append(
            [
                out[r, p * H + row : p * H + row + CH, mode * N + c * H : mode * N + c * H + H]
                for r, c in QUADS
            ]
        )
    return result


def load_four(out, mode, row, sign):
    real, imag = [
        [
            out[p, r * H + row : r * H + row + CH, mode * N + c * H : mode * N + c * H + H]
            for r, c in QUADS
        ]
        for p in (0, 1)
    ]
    if sign > 0:
        return (
            [real[0], imag[1], imag[2], -real[3]],
            [imag[0], -real[1], -real[2], -imag[3]],
        )
    return (
        [real[0], -imag[1], -imag[2], -real[3]],
        [imag[0], real[1], real[2], -imag[3]],
    )


def unfold4(ee, eo, oe, oo):
    a, b = ee + eo, ee - eo
    c, d = oe + oo, oe - oo
    return a + c, b + d, a - c, b - d


def field(ref, lead, row, q):
    return quad(ref, lead + (0,), row, q), quad(ref, lead + (1,), row, q)


def fold_pairs(pairs):
    return fold4(*[v[0] for v in pairs]), fold4(*[v[1] for v in pairs])


def window_of(place, mine, other):
    y0, x0, odd = place[0], place[1], place[2]
    scale = place[3].astype(F32)
    rows = lax.broadcasted_iota(jnp.int32, (N, N), 0)
    upper = jnp.where(rows >= y0, 1 - odd, odd) > 0
    result = []
    for p in range(2):
        value = jnp.where(upper, mine[p] * scale, other[p])
        value = pltpu.roll(pltpu.roll(value, lax.rem(N - y0, N), 0), lax.rem(N - x0, N), 1)
        result.append(mirror(value))
    return result


def wrapped(place, value):
    return pltpu.roll(pltpu.roll(mirror(value), place[0], 0), place[1], 1)


def add_pair(total, value):
    return total[0] + value[0], total[1] + value[1]


def zeros():
    return [(jnp.zeros((CH, H), F32), jnp.zeros((CH, H), F32))] * 4


def first_kernel(place, mine, other, source, table, q1, obj, op, mid, out, probes, arrived):
    modes = probes.shape[0]
    copy = pltpu.make_async_copy(source, probes, arrived)
    copy.start()
    obj[0], obj[1] = window_of(place, mine, other)
    copy.wait()
    for m in range(modes):
        for k in range(CHUNKS):
            row = k * CH
            pairs = [mul(field(probes, (m,), row, q), field(obj, (), row, q)) for q in QUADS]
            store_right_prop(op, m, row, *fold_pairs(pairs))
    prop_products(op, mid, out, table, 0, modes)
    for m in range(modes):
        for k in range(CHUNKS):
            row = k * CH
            real, imag = load_prop(out, m, row)
            for q, v in zip(QUADS, zip(unfold4(*real), unfold4(*imag))):
                put(q1, (m, 0), row, q, v[0])
                put(q1, (m, 1), row, q, v[1])


def second_kernel(
    place, mine, other, q1, amplitude, table, phases, probes, first_obj,
    grads1, grads0, send, keep,
    obj, amp, op, mid, out,
):
    modes = q1.shape[0]
    obj[0], obj[1] = mul(window_of(place, mine, other), (phases[0], phases[1]))
    amp[...] = mirror(amplitude[0])
    for m in range(modes):
        for k in range(CHUNKS):
            row = k * CH
            pairs = [mul(field(q1, (m,), row, q), field(obj, (), row, q)) for q in QUADS]
            store_right_four(op, m, row, *fold_pairs(pairs))
    four_products(op, mid, out, table, modes)
    for k in range(CHUNKS):
        row = k * CH
        total = [jnp.zeros((CH, H), F32)] * 4
        for m in range(modes):
            real, imag = load_four(out, m, row, 1)
            for i, v in enumerate(zip(unfold4(*real), unfold4(*imag))):
                total[i] = total[i] + (v[0] * v[0] + v[1] * v[1])
        factor = [
            1.0 - quad(amp, (), row, q) * lax.rsqrt(total[i] + 1.0) for i, q in enumerate(QUADS)
        ]
        for m in range(modes):
            real, imag = load_four(out, m, row, 1)
            pairs = [
                (factor[i] * v[0], factor[i] * v[1])
                for i, v in enumerate(zip(unfold4(*real), unfold4(*imag)))
            ]
            store_right_four(op, m, row, *fold_pairs(pairs))
    four_products(op, mid, out, table, modes)
    for k in range(CHUNKS):
        row = k * CH
        total = zeros()
        for m in range(modes):
            real, imag = load_four(out, m, row, -1)
            pairs = []
            for i, v in enumerate(zip(unfold4(*real), unfold4(*imag))):
                q = QUADS[i]
                total[i] = add_pair(total[i], mulc(field(q1, (m,), row, q), v))
                pairs.append(mulc(field(obj, (), row, q), v))
            store_right_prop(op, m, row, *fold_pairs(pairs))
        for i, q in enumerate(QUADS):
            total[i] = mulc(field(phases, (), row, q), total[i])
        for i, q in enumerate(QUADS):
            put(grads1, (0,), row, q, total[i][0])
            put(grads1, (1,), row, q, total[i][1])
    prop_products(op, mid, out, table, 1, modes)
    half = modes // 2
    for k in range(CHUNKS):
        row = k * CH
        total = zeros()
        for m in range(modes):
            real, imag = load_prop(out, m, row)
            terms = send if m < half else keep
            for i, v in enumerate(zip(unfold4(*real), unfold4(*imag))):
                q = QUADS[i]
                total[i] = add_pair(total[i], mulc(field(probes, (m,), row, q), v))
                term = mulc(field(first_obj, (), row, q), v)
                put(terms, (m % half, 0), row, q, term[0])
                put(terms, (m % half, 1), row, q, term[1])
        for i, q in enumerate(QUADS):
            put(grads0, (0,), row, q, total[i][0])
            put(grads0, (1,), row, q, total[i][1])
    for terms in (send, keep):
        for m in range(half):
            for p in range(2):
                terms[m, p] = mirror(terms[m, p])
    for p in range(2):
        grads1[p] = wrapped(place, grads1[p])
        grads0[p] = wrapped(place, grads0[p])


def call(kernel, args, shapes, scratch, flops, mib):
    spec = pl.BlockSpec(memory_space=pltpu.VMEM)
    return pl.pallas_call(
        kernel,
        in_specs=[pl.BlockSpec(memory_space=pltpu.SMEM)] + [spec] * (len(args) - 1),
        out_specs=[spec] * len(shapes),
        out_shape=[jax.ShapeDtypeStruct(shape, dtype) for shape, dtype in shapes],
        scratch_shapes=[pltpu.VMEM(shape, dtype) for shape, dtype in scratch],
        compiler_params=pltpu.CompilerParams(vmem_limit_bytes=mib << 20),
        cost_estimate=pl.CostEstimate(flops=flops, bytes_accessed=4 << 20, transcendentals=0),
    )(*args)


def products_scratch(modes):
    return [((2, 2 * N, modes * N), BF16), ((2, N, modes * N), F32)]


def operand(modes):
    return ((2, modes * N, 2 * N), BF16)


def first(place, mine, other, probes, table):
    modes = probes.shape[0]
    spec = pl.BlockSpec(memory_space=pltpu.VMEM)
    scratch = [operand(modes)] + products_scratch(modes) + [(probes.shape, F32)]
    return pl.pallas_call(
        first_kernel,
        in_specs=[pl.BlockSpec(memory_space=pltpu.SMEM), spec, spec]
        + [pl.BlockSpec(memory_space=pl.ANY), spec],
        out_specs=[spec, spec],
        out_shape=[
            jax.ShapeDtypeStruct(probes.shape, F32),
            jax.ShapeDtypeStruct((2, N, N), F32),
        ],
        scratch_shapes=[pltpu.VMEM(shape, dtype) for shape, dtype in scratch]
        + [pltpu.SemaphoreType.DMA],
        compiler_params=pltpu.CompilerParams(vmem_limit_bytes=18 << 20),
        cost_estimate=pl.CostEstimate(flops=3 << 30, bytes_accessed=4 << 20, transcendentals=0),
    )(place, mine, other, probes, table)


def second(place, mine, other, q1, amplitude, table, phases, probes, first_obj):
    modes = q1.shape[0]
    field_shape, terms_shape = ((2, N, N), F32), ((modes // 2, 2, N, N), F32)
    return call(
        second_kernel,
        (place, mine, other, q1, amplitude, table, phases, probes, first_obj),
        [field_shape, field_shape, terms_shape, terms_shape],
        [field_shape, ((N, N), F32), operand(modes)] + products_scratch(modes),
        9 << 30,
        22,
    )


def stage_kernel(core, source, table, phases, target, table_out, phases_out):
    target[0] = mirror(source[0])

    @pl.when(pl.program_id(0) == 0)
    def _():
        table_out[...] = table[...]
        phases_out[...] = phases[...]


def staged(core, probes):
    table, phases = (jnp.asarray(v) for v in constants())
    images = probes.reshape(-1, N, N)
    count = images.shape[0]
    half = count // 2
    whole = lambda value: pl.BlockSpec(value.shape, lambda i, core: (0,) * value.ndim)
    flip, table, phases = pl.pallas_call(
        stage_kernel,
        grid_spec=pltpu.PrefetchScalarGridSpec(
            num_scalar_prefetch=1,
            grid=(count,),
            in_specs=[
                pl.BlockSpec((1, N, N), lambda i, core: ((i + half * (1 - core[0])) % count, 0, 0)),
                whole(table),
                whole(phases),
            ],
            out_specs=[
                pl.BlockSpec((1, N, N), lambda i, core: (i, 0, 0)),
                whole(table),
                whole(phases),
            ],
        ),
        out_shape=[
            jax.ShapeDtypeStruct(images.shape, F32),
            jax.ShapeDtypeStruct(table.shape, table.dtype),
            jax.ShapeDtypeStruct(phases.shape, phases.dtype),
        ],
    )(core, images, table, phases)
    return flip.reshape(probes.shape), table, phases


POS = ("y", "zh", "core")
TILE = ("x", "zl")
ROWS = 32
COLUMNS = 8
MODES = 4


def shifted(value, axes, steps):
    count = math.prod(lax.axis_size(axis) for axis in axes)
    first, last = (max(0, -steps), min(count, count - steps))
    return lax.ppermute(value, axes, [(source, source + steps) for source in range(first, last)])


def piece(value, index):
    return lax.dynamic_index_in_dim(value, index, 0, keepdims=False)


def ring(value, axis, step):
    count = lax.axis_size(axis)
    return lax.ppermute(value, axis, [(i, (i + step) % count) for i in range(count)])


def pieces(value, axis):
    count, me = lax.axis_size(axis), lax.axis_index(axis)
    value = value.reshape(count, -1, N)
    return [piece(value, (me + step) & (count - 1)) for step in range(1, count)] + [piece(value, me)]


def scatter_sum(parts, axis):
    arrived = [ring(part, axis, step + 1) for step, part in enumerate(parts[:-1])]
    total = parts[-1]
    for part in arrived:
        total = total + part
    return total


def after(value, *others):
    return lax.optimization_barrier((value,) + others)[0]


def circular_sum(parts, axis, *beside):
    total = ring(parts[0], axis, -1)
    for step, part in enumerate(parts[1:-1]):
        total = ring(total + (after(part, *beside) if step else part), axis, -1)
    return total + parts[-1]


def collected(value, travelled, axis, *beside):
    count, me = lax.axis_size(axis), lax.axis_index(axis)
    whole = jnp.zeros((count,) + value.shape, value.dtype)
    whole = after(lax.dynamic_update_index_in_dim(whole, value, me, 0), *beside)
    for step, part in enumerate(travelled):
        whole = lax.dynamic_update_index_in_dim(whole, part, (me + step + 1) & (count - 1), 0)
    return whole.reshape(-1, N)


def gather(value, axis, *beside):
    steps = range(1, lax.axis_size(axis))
    return collected(value, [ring(value, axis, -step) for step in steps], axis, *beside)


def exchange(value, bits):
    axes = ("zh", "zl")
    count = math.prod(lax.axis_size(axis) for axis in axes)
    return lax.ppermute(value, axes, [(i, i ^ bits) for i in range(count)])


def summed_over_z(value):
    value = (value + exchange(value, 1)) + (exchange(value, 2) + exchange(value, 3))
    return value + exchange(value, 4)


def moved(value, even, odd):
    pairs = []
    for row in range(ROWS):
        for column in range(COLUMNS):
            target = row + (odd if column % 2 else even)
            if column % 2:
                target %= ROWS
            if 0 <= target < ROWS:
                pairs.append((row * COLUMNS + column, target * COLUMNS + column))
    return lax.ppermute(value, POS + TILE, pairs)


def per_device(object_field, probe_modes, amplitudes, corners):
    row = lax.broadcasted_iota(jnp.int32, (N, N), 0)
    col = lax.broadcasted_iota(jnp.int32, (N, N), 1)
    odd = lax.axis_index("zl")
    is_odd = odd == 1
    first_row = (lax.axis_index(POS) == 0) & is_odd
    above = lax.ppermute(corners, POS, [(i, (i + 1) % ROWS) for i in range(ROWS)])
    yp, xp = [jnp.where(is_odd, above[0, i], corners[0, i]) for i in (0, 1)]
    yq, xq = [jnp.where(is_odd, corners[0, i], above[0, i]) for i in (0, 1)]
    live = jnp.where(first_row, 0, 1)
    place = jnp.stack([yp, xp, odd, live]).astype(jnp.int32)
    flip, table, phases = staged(lax.axis_index("core").astype(jnp.int32).reshape(1), probe_modes)
    right = after(shifted(after(object_field, above), TILE, -1), flip)
    mine, mixed = [
        [jnp.where(col < x, right[s], object_field[s]) for s in range(2)] for x in (xp, xq)
    ]
    other = [moved(mixed[s], -1, 1) for s in range(2)]

    def split(grads, arrived):
        kept = jnp.where(((row >= yp) != is_odd) & ~first_row, grads, 0.0)
        taken = jnp.where((row < yq) != is_odd, arrived, 0.0)
        leaving = jnp.where(col < xp, kept, 0.0) + jnp.where(col < xq, taken, 0.0)
        staying = jnp.where(col >= xp, kept, 0.0) + jnp.where(col >= xq, taken, 0.0)
        return staying, leaving

    amplitude = moved(after(amplitudes, *mixed), 0, 1)
    q1, obj = first(place, mine[0], other[0], flip, table)
    grads1, grads0, send, keep = second(
        place, mine[1], other[1], q1, amplitude, table, phases, flip, obj
    )
    swap = [(0, 1), (1, 0)]
    arrived1 = moved(grads1, 1, -1)
    across = pieces(keep + lax.ppermute(send, "core", swap), "y")
    staying1, leaving1 = split(grads1, after(arrived1, *across))
    received1 = shifted(leaving1, TILE, 1)
    across[-1] = after(across[-1], leaving1)
    across = pieces(scatter_sum(across, "y"), "x")
    arrived0 = moved(after(grads0, leaving1), 1, -1)
    partial = circular_sum(across, "x", received1)
    staying0, leaving0 = split(grads0, arrived0)
    total = summed_over_z(after(partial, leaving0))
    total = gather(total, "x")
    received0 = shifted(after(leaving0, total), TILE, 1)
    total = after(gather(total, "y"), received0)
    object_grad = jnp.stack([staying0 + received0, staying1 + received1])
    opposite = lax.ppermute(total, "core", swap)
    half = lax.broadcasted_iota(jnp.int32, (2, 1, 1), 0)
    probe_grad = jnp.where(half == lax.axis_index("core"), total, opposite)
    probe_grad = probe_grad.reshape(probe_modes.shape)
    return (object_grad, probe_grad)


def solution(mesh):
    split = jax.sharding.Mesh(mesh.devices.reshape(4, 4, 2, 4, 2), POS + TILE)
    in_specs = (
        P(None, None, POS, TILE),
        P(),
        P(POS + TILE, None, None),
        P(POS + TILE, None),
    )
    out_specs = (P(None, None, POS, TILE), P())
    return jax.shard_map(
        per_device, mesh=split, in_specs=in_specs, out_specs=out_specs, check_vma=False
    )
```
